256 devices in a mesh: tm: 32 (over x, z), chan: 4 (over y), clip: 2 (over core).
Axes of the slice: x: 4, y: 4, z: 8, core: 2. Of those that a mesh axis runs over, the one named last changes fastest.
Arguments:
- frames: bfloat16 [2048, 16, 16, 256], P(('clip', 'tm')), parts along dimension 0, may hold values from -6 to 6
- intervals: float32 [2048], P(('clip', 'tm')), parts along dimension 0, may hold values from 0.35 to 924.6
- decay_rates: float32 [256], P('chan'), may hold values from 0.00016276042 to 0.03448276
- in_kernel: bfloat16 [3, 3, 256, 256], P(None, None, None, 'chan'), may hold values from -0.125 to 0.125
- out_kernel: bfloat16 [3, 3, 256, 256], P(None, None, 'chan'), may hold values from -0.125 to 0.125
- skip_gain: float32 [256], replicated, may hold values from 0.5 to 1.5
Outputs:
- readout: bfloat16 [2048, 16, 16, 256], P(('clip', 'tm'), 'chan'), parts along dimension 0
The draws below stay inside these ranges and needn't reach their ends.
There are 2 independent parts, one for each index of `clip`. The reference program is written for one: setup_inputs(seed, part) draws one part's arguments, and reference() takes and returns one part's arrays. A program takes and returns all parts, laid end to end along the dimension named above; an argument that names none is the same for every part. Nothing has to cross between parts.
All inputs are finite; a program needn't handle non-finite values.
Results may differ from the reference program's by a relative error of at most 0.019.
Values may be sent and summed in bfloat16 or wider, within the bound.
No kernel may reach another device: no remote copies, remote signals or barrier semaphores. Data moves between devices by JAX's collectives and lax.ppermute only.
A program may use at most 128 MiB of HBM per device.

```python
import math
import jax
import jax.numpy as jnp
from jax import lax

CH = 256
STATES = 256
FRAME_H = 16
FRAME_W = 16
FRAMES_DEV = 32
TIME = 1024


def draw_intervals(key, part):
    key = jax.random.fold_in(key, 11)
    key_level, key_jitter, key_places = jax.random.split(key, 3)
    blocks = TIME // FRAMES_DEV
    levels = jnp.exp(jax.random.uniform(key_level, (blocks,), jnp.float32, math.log(0.5), math.log(2.0)))
    jitter = jax.random.uniform(key_jitter, (TIME,), jnp.float32, 0.7, 1.3)
    places = jax.random.randint(key_places, (3,), 0, TIME)
    jumped = jnp.sum((jnp.arange(TIME)[:, None] == places[None, :]).astype(jnp.float32), axis=1)
    return (jnp.repeat(levels, FRAMES_DEV) * jitter + jumped * (0.3 * TIME)).astype(jnp.float32)


def draw_decay_rates(key, part):
    key = jax.random.fold_in(key, 23)
    lowest = math.log(0.2 / TIME)
    highest = math.log(1.0 / 30.0)
    return jnp.exp(jax.random.uniform(key, (STATES,), jnp.float32, lowest, highest)).astype(jnp.float32)


def level_of(stream_key, extent, pieces, smallest, top_value):
    level = 1.0
    for position, blocks in pieces:
        draws = jax.random.uniform(jax.random.fold_in(jax.random.fold_in(stream_key, 6), position), (blocks,), jnp.float32, smallest / len(pieces), top_value / len(pieces))
        level = level * jnp.repeat(jnp.exp(draws), extent[position] // blocks).reshape((-1,) + (1,) * (len(extent) - 1 - position))
    return level


def noise(own_key, dims, scale, limit, shards=(), kind=jnp.bfloat16):
    array = jax.random.normal(own_key, dims, jnp.float32) * scale
    if len(shards) > 0:
        array = level_of(own_key, dims, shards, -0.22, 0.18) * array
    return jnp.clip(array, min=-limit, max=limit).astype(kind)


def setup_inputs(seed: int = 0, part: int = 0) -> dict:
    key_of = jax.random.split(jax.random.key(seed), 7)
    own_keys = jax.random.split(jax.random.fold_in(key_of[6], part), 7)
    return {
        "frames": noise(own_keys[0], (TIME, FRAME_H, FRAME_W, CH), 1.0, 6.0, ((0, 32),)),
        "intervals": draw_intervals(jax.random.fold_in(jax.random.fold_in(key_of[6], part), 71), part),
        "decay_rates": draw_decay_rates(jax.random.fold_in(key_of[6], 71), part),
        "in_kernel": noise(key_of[3], (3, 3, CH, STATES), (9 * CH) ** -0.5, 0.125, ((3, 4),)),
        "out_kernel": noise(key_of[4], (3, 3, STATES, CH), (9 * STATES) ** -0.5, 0.125, ((2, 4),)),
        "skip_gain": jnp.clip(jax.random.uniform(key_of[5], (CH,), jnp.float32, 0.5, 1.5), 0.5, 1.5),
    }


def convolve(volume, kernel):
    return lax.conv_general_dilated(volume, kernel, (1, 1), 'SAME', dimension_numbers=('NHWC', 'HWIO', 'NHWC'), preferred_element_type=jnp.float32)

def reference(frames, intervals, decay_rates, in_kernel, out_kernel, skip_gain):
    drives = convolve(frames, in_kernel)
    scaled = intervals[:, None] * decay_rates[None, :]
    decays = jnp.exp(-scaled)
    gain_rows = jnp.sqrt(-jnp.expm1(-2.0 * scaled))

    def advance(carried, inputs):
        decay_now, gain_now, drive_now = inputs
        carried = decay_now * carried + gain_now * drive_now
        return (carried, carried.astype(jnp.bfloat16))
    initial = jnp.zeros(drives.shape[1:], jnp.float32)
    unused, states = lax.scan(advance, initial, (decays, gain_rows, drives))
    readout = convolve(states, out_kernel) + skip_gain * frames.astype(jnp.float32)
    return readout.astype(jnp.bfloat16)
```

```python
import functools

import jax
import jax.numpy as jnp
from jax import lax
from jax.experimental import pallas as pl
from jax.experimental.pallas import tpu as pltpu
from jax.sharding import PartitionSpec as P

F32 = jnp.float32
BF16 = jnp.bfloat16
FRAMES = 32
HALF = 16
ROWS = 16
WIDE = 16
CH = 256
OWN = 64
LANES = 128
CHANS = 4
ZS = 8
XS = 4
WINDOW = 6
STEP = 2
CHUNKS = HALF // STEP


def split3(value):
    high = value.astype(BF16)
    rest = value - high.astype(F32)
    middle = rest.astype(BF16)
    low = (rest - middle.astype(F32)).astype(BF16)
    return high, middle, low


def join3(block, start):
    parts = block.astype(F32)
    return parts[start : start + 1] + parts[start + 1 : start + 2] + parts[start + 2 : start + 3]


def low_half(shape):
    return lax.broadcasted_iota(jnp.int32, shape, len(shape) - 1) < OWN


def swap_halves(value):
    return pltpu.roll(value, OWN, value.ndim - 1)


def doubled(rates):
    row = jnp.concatenate([rates, rates], axis=1)
    return row


def table(low_values, high_values):
    row = lax.broadcasted_iota(jnp.int32, (HALF, LANES), 0)
    low = low_half((HALF, LANES))
    result = jnp.zeros((HALF, LANES), F32)
    for t in range(HALF):
        result = jnp.where(row == t, jnp.where(low, low_values[t], high_values[t]), result)
    return result


def spread(target, index, lanes, rows):
    for t in range(HALF):
        target[index, t, :, lanes] = jnp.broadcast_to(rows[t : t + 1], (WIDE, LANES))


def one_minus_exp(value):
    series = value * (
        1.0 - value * (0.5 - value * (1.0 / 6 - value * (1.0 / 24 - value * (1.0 / 120))))
    )
    return jnp.where(value < 0.125, series, 1.0 - jnp.exp(-value))


def running(values):
    sums = [values[0]]
    for value in values[1:]:
        sums.append(sums[-1] + value)
    return sums


def drive_kernel(
    place, intervals, rates, kernel_t, frames,
    own, one, two, three, message,
    padded, weights, factors, state, kept, load_sem, store_sem,
):
    windows = (own, one, two, three)

    def load(chunk, half):
        start = half * HALF + chunk * STEP
        return pltpu.make_async_copy(
            frames.at[pl.ds(start, STEP)],
            padded.at[pl.ds(start, STEP), pl.ds(1, ROWS)],
            load_sem.at[chunk, half],
        )

    def store(chunk, step):
        first = CHANS * lax.rem(place[0] + step, CHANS)
        return pltpu.make_async_copy(
            kept.at[pl.ds(chunk * STEP, STEP), pl.ds(first, WINDOW)],
            windows[step].at[pl.ds(chunk * STEP, STEP)],
            store_sem.at[chunk, step],
        )

    for chunk in range(CHUNKS):
        load(chunk, 0).start()
        load(chunk, 1).start()

    empty = jnp.zeros((FRAMES, 1, WIDE, CH), BF16)
    padded[:, 0:1] = empty
    padded[:, ROWS + 1 : ROWS + 2] = empty
    empty = jnp.zeros((HALF, 1, WIDE, LANES), BF16)
    kept[:, 0:1] = empty
    kept[:, ROWS + 1 : ROWS + 2] = empty
    nothing = jnp.zeros((CH, OWN), BF16)
    for i in range(3):
        tap = [kernel_t[3 * i + j].astype(F32).T.astype(BF16) for j in range(3)]
        weights[0, CH * i : CH * (i + 1), :] = jnp.concatenate([tap[0], tap[1], tap[2], nothing], 1)
        weights[1, CH * i : CH * (i + 1), :] = jnp.concatenate([tap[1], tap[0], nothing, tap[2]], 1)

    values = [intervals[t] for t in range(FRAMES)]
    rate = doubled(rates[...])
    scaled = table(values[:HALF], values[HALF:]) * rate
    spread(factors, 0, slice(None), jnp.exp(-scaled))
    spread(factors, 1, slice(None), jnp.sqrt(one_minus_exp(2.0 * scaled)))
    state[...] = jnp.zeros_like(state)

    def advance(chunk, carry):
        start = pl.multiple_of(chunk * STEP, STEP)

        def product(half):
            block = padded[pl.ds(half * HALF + start, STEP)]
            taps = [block[:, i : i + ROWS].reshape(STEP * ROWS * WIDE, CH) for i in range(3)]
            return jnp.dot(
                jnp.concatenate(taps, axis=1), weights[half], preferred_element_type=F32
            )

        load(chunk, 0).wait()
        load(chunk, 1).wait()
        first, second = product(0), product(1)
        low = low_half((STEP * ROWS * WIDE, LANES))
        left = jnp.where(low, first[:, :LANES], second[:, :LANES])
        centre = swap_halves(jnp.where(low, second[:, :LANES], first[:, :LANES]))
        right = first[:, LANES:] + second[:, LANES:]
        shape = (STEP * ROWS, WIDE, LANES)
        column = lax.broadcasted_iota(jnp.int32, shape, 1)
        left = jnp.where(column == 0, 0.0, pltpu.roll(left.reshape(shape), 1, 1))
        right = jnp.where(column == WIDE - 1, 0.0, pltpu.roll(right.reshape(shape), WIDE - 1, 1))
        drives = (left + centre.reshape(shape) + right).reshape(STEP, ROWS, WIDE, LANES)
        carried = state[...]
        for step in range(STEP):
            decay, gain = factors[0, start + step], factors[1, start + step]
            carried = decay * carried + gain * drives[step]
            kept[start + step, 1 : ROWS + 1] = carried.astype(BF16)
        state[...] = carried
        for step in range(CHANS):
            store(chunk, step).start()
        return carry

    lax.fori_loop(0, CHUNKS, advance, 0)

    late = functools.reduce(lambda a, b: a + b, values[HALF:])
    total = functools.reduce(lambda a, b: a + b, values[:HALF]) + late
    carried = state[...]
    end = carried + jnp.exp(-late * rate).reshape(1, 1, LANES) * swap_halves(carried)
    other = swap_halves(end)
    low = low_half((ROWS // 2, WIDE, LANES))
    packed = jnp.where(low, other[: ROWS // 2], end[ROWS // 2 :]).astype(BF16)
    row = lax.broadcasted_iota(jnp.int32, (WIDE, LANES), 0)
    pieces = split3(jnp.full((WIDE, LANES), total, F32))
    extra = jnp.where(row == 0, pieces[0].astype(F32), jnp.where(row == 1, pieces[1].astype(F32), pieces[2].astype(F32))).astype(BF16)
    for z in range(ZS):
        message[z, : ROWS // 2] = packed
        message[z, ROWS // 2] = extra
    for chunk in range(CHUNKS):
        for step in range(CHANS):
            store(chunk, step).wait()


def relay_kernel(place, rates, received, message):
    x, z = place[1], place[2]
    rate = doubled(rates[...])
    total = jnp.zeros((ROWS // 2, WIDE, LANES), F32)
    before = total
    elapsed = jnp.zeros((1, LANES), F32)
    elapsed_before = elapsed
    for other in range(ZS):
        mine = z == other
        before = jnp.where(mine, total, before)
        elapsed_before = jnp.where(mine, elapsed, elapsed_before)
        spent = join3(received[other, ROWS // 2], 0)
        decay = jnp.exp(-spent * rate).reshape(1, 1, LANES)
        total = decay * total + received[other, : ROWS // 2].astype(F32)
        elapsed = elapsed + spent

    low = low_half((WIDE, LANES))
    blank = jnp.zeros((WIDE, LANES), F32)

    def rows_of(value):
        swapped = swap_halves(value)
        top = [jnp.where(low, value[r], swapped[r]) for r in range(ROWS // 2)]
        bottom = [jnp.where(low, swapped[r], value[r]) for r in range(ROWS // 2)]
        return [blank] + top + bottom + [blank]

    totals, befores = rows_of(total), rows_of(before)
    row = lax.broadcasted_iota(jnp.int32, (WIDE, LANES), 0)
    extra = blank
    pieces = split3(elapsed) + split3(elapsed_before) + split3(rate)
    for index, piece in enumerate(pieces):
        extra = jnp.where(row == index, piece.astype(F32), extra)
    extra = extra.astype(BF16)
    for chan in range(CHANS):
        for q in range(WINDOW // 2):
            here = CHANS * chan + q
            there = here + WINDOW // 2
            later = jnp.where(low, totals[here], totals[there]).astype(BF16)
            level = jnp.where(low, befores[here], befores[there]).astype(BF16)
            for to in range(XS):
                message[to * CHANS + chan, q] = jnp.where(x == to, level, later)
        for to in range(XS):
            message[to * CHANS + chan, WINDOW // 2] = extra


OUT_STEP = 8
OUT_CHUNKS = FRAMES // OUT_STEP


def readout_kernel(
    place, intervals, skip_gain, received, own, one, two, three, out_kernel, frames,
    result,
    weights, direct, states, written, flows, base, load_sem, store_sem,
):
    chan, x = place[0], place[1]
    blocks = (own, one, two, three)

    def fetch(step):
        return pltpu.make_async_copy(
            out_kernel.at[lax.rem(chan + CHANS - step, CHANS)],
            weights.at[:, pl.ds(OWN * step, OWN)],
            load_sem.at[step],
        )

    def fetch_direct():
        return pltpu.make_async_copy(
            frames.at[:, pl.ds(CHANS * chan, CHANS)], direct, load_sem.at[CHANS]
        )

    def store(chunk):
        part = pl.ds(chunk * OUT_STEP, OUT_STEP)
        return pltpu.make_async_copy(written.at[part], result.at[part], store_sem.at[chunk])

    for step in range(CHANS):
        fetch(step).start()
    fetch_direct().start()

    low = low_half((WIDE, LANES))
    rates, entering = [], []
    for step in range(CHANS):
        source = lax.rem(chan + CHANS - step, CHANS)
        level = received[x * CHANS + source]
        rate = join3(level[WINDOW // 2], 6)
        spent = join3(level[WINDOW // 2], 3)
        total = jnp.zeros((WINDOW // 2, WIDE, LANES), F32)
        for other in range(XS - 1):
            earlier = received[other * CHANS + source]
            decay = jnp.exp(-join3(earlier[WINDOW // 2], 0) * rate).reshape(1, 1, LANES)
            added = decay * total + earlier[: WINDOW // 2].astype(F32)
            total = jnp.where(other < x, added, total)
        decay = jnp.exp(-spent * rate).reshape(1, 1, LANES)
        total = level[: WINDOW // 2].astype(F32) + decay * total
        swapped = swap_halves(total)
        rates.append(rate)
        entering.append(
            [jnp.where(low, total[r], swapped[r]) for r in range(WINDOW // 2)]
            + [jnp.where(low, swapped[r], total[r]) for r in range(WINDOW // 2)]
        )

    values = [intervals[t] for t in range(FRAMES)]
    first, second = running(values[:HALF]), running(values[HALF:])
    first_table, second_table = table(first, first), table(second, second)
    low_row = low_half((1, LANES))

    def halves(t, pair):
        a = blocks[2 * pair][t].astype(F32)
        b = blocks[2 * pair + 1][t].astype(F32)
        low = low_half(a.shape)
        return jnp.where(low, a, swap_halves(b)), jnp.where(low, swap_halves(a), b)

    for pair in range(2):
        rate = jnp.where(low_row, rates[2 * pair], rates[2 * pair + 1])
        part = slice(LANES * pair, LANES * (pair + 1))
        inflow = jnp.exp(-first_table * rate)
        spread(flows, 0, part, inflow)
        spread(flows, 1, part, jnp.exp(-second_table * rate))
        last = halves(HALF - 1, pair)[0]
        for r in range(WINDOW):
            arriving = jnp.where(low, entering[2 * pair][r], entering[2 * pair + 1][r])
            base[0, r, :, part] = arriving
            base[1, r, :, part] = inflow[HALF - 1 :] * arriving + last[r]

    def fill(t, carry):
        for pair in range(2):
            part = slice(LANES * pair, LANES * (pair + 1))
            for half, local in enumerate(halves(t, pair)):
                flow = flows[half, t, :, part]
                full = local + flow * base[half, :, :, part]
                states[half * HALF + t, :, :, part] = full.astype(BF16)
        return carry

    lax.fori_loop(0, HALF, fill, 0)
    for step in range(CHANS):
        fetch(step).wait()
    fetch_direct().wait()

    def convolve(chunk, carry):
        start = pl.multiple_of(chunk * OUT_STEP, OUT_STEP)
        size = OUT_STEP * CHANS * WIDE
        block = states[pl.ds(start, OUT_STEP)]
        taps = [block[:, i : i + CHANS].reshape(size, CH) for i in range(3)]
        operand = jnp.concatenate(taps, axis=1)
        shape = (OUT_STEP * CHANS, WIDE, CH)
        column = lax.broadcasted_iota(jnp.int32, shape, 1)
        parts = []
        for j in range(3):
            weight = jnp.concatenate([weights[3 * i + j] for i in range(3)], axis=0)
            parts.append(jnp.dot(operand, weight, preferred_element_type=F32).reshape(shape))
        total = parts[1]
        total += jnp.where(column == 0, 0.0, pltpu.roll(parts[0], 1, 1))
        total += jnp.where(column == WIDE - 1, 0.0, pltpu.roll(parts[2], WIDE - 1, 1))
        passed = direct[pl.ds(start, OUT_STEP)].astype(F32).reshape(shape)
        total += skip_gain[...].reshape(1, 1, CH) * passed
        written[pl.ds(start, OUT_STEP)] = total.astype(BF16).reshape(OUT_STEP, CHANS, WIDE, CH)
        store(chunk).start()
        return carry

    lax.fori_loop(0, OUT_CHUNKS, convolve, 0)
    for chunk in range(OUT_CHUNKS):
        store(chunk).wait()


def in_vmem():
    return pl.BlockSpec(memory_space=pltpu.VMEM)


def in_smem():
    return pl.BlockSpec(memory_space=pltpu.SMEM)


def anywhere():
    return pl.BlockSpec(memory_space=pl.ANY)


def drive(place, intervals, rates, kernel_t, frames):
    window = jax.ShapeDtypeStruct((HALF, WINDOW, WIDE, LANES), BF16)
    return pl.pallas_call(
        drive_kernel,
        out_shape=[window] * CHANS
        + [jax.ShapeDtypeStruct((ZS, ROWS // 2 + 1, WIDE, LANES), BF16)],
        in_specs=[in_smem(), in_smem(), in_vmem(), in_vmem(), anywhere()],
        out_specs=[anywhere()] * CHANS + [in_vmem()],
        scratch_shapes=[
            pltpu.VMEM((FRAMES, ROWS + 2, WIDE, CH), BF16),
            pltpu.VMEM((2, 3 * CH, CH), BF16),
            pltpu.VMEM((2, HALF, WIDE, LANES), F32),
            pltpu.VMEM((ROWS, WIDE, LANES), F32),
            pltpu.VMEM((HALF, ROWS + 2, WIDE, LANES), BF16),
            pltpu.SemaphoreType.DMA((CHUNKS, 2)),
            pltpu.SemaphoreType.DMA((CHUNKS, CHANS)),
        ],
        compiler_params=pltpu.CompilerParams(vmem_limit_bytes=32 << 20),
        name="drive",
    )(place, intervals, rates, kernel_t, frames)


def relay(place, rates, received):
    return pl.pallas_call(
        relay_kernel,
        out_shape=jax.ShapeDtypeStruct((XS * CHANS, WINDOW // 2 + 1, WIDE, LANES), BF16),
        in_specs=[in_smem(), in_vmem(), in_vmem()],
        out_specs=in_vmem(),
        compiler_params=pltpu.CompilerParams(vmem_limit_bytes=16 << 20),
        name="relay",
    )(place, rates, received)


def read_out(place, intervals, skip_gain, received, blocks, out_kernel, frames):
    return pl.pallas_call(
        readout_kernel,
        out_shape=jax.ShapeDtypeStruct((FRAMES, CHANS, WIDE, CH), BF16),
        in_specs=[in_smem(), in_smem(), in_vmem(), in_vmem()]
        + [in_vmem()] * CHANS
        + [anywhere(), anywhere()],
        out_specs=anywhere(),
        scratch_shapes=[
            pltpu.VMEM((9, CHANS * OWN, CH), BF16),
            pltpu.VMEM((FRAMES, CHANS, WIDE, CH), BF16),
            pltpu.VMEM((FRAMES, WINDOW, WIDE, CH), BF16),
            pltpu.VMEM((FRAMES, CHANS, WIDE, CH), BF16),
            pltpu.VMEM((2, HALF, WIDE, CH), F32),
            pltpu.VMEM((2, WINDOW, WIDE, CH), F32),
            pltpu.SemaphoreType.DMA((CHANS + 1,)),
            pltpu.SemaphoreType.DMA((OUT_CHUNKS,)),
        ],
        compiler_params=pltpu.CompilerParams(vmem_limit_bytes=32 << 20),
        name="read_out",
    )(place, intervals, skip_gain, received, *blocks, out_kernel, frames)


def local(frames, intervals, decay_rates, in_kernel, out_kernel, skip_gain):
    place = jnp.stack([lax.axis_index(name) for name in ("chan", "x", "z")]).astype(jnp.int32)
    rates = decay_rates.reshape(1, OWN)
    kernel_t = jnp.transpose(in_kernel.reshape(9, CH, OWN), (0, 2, 1))
    gathered = lax.all_gather(out_kernel.reshape(9, OWN, CH), "chan")
    *windows, message = drive(place, intervals, rates, kernel_t, frames)
    arrived = lax.all_to_all(message, "z", 0, 0)
    blocks = [windows[0]]
    for step in range(1, CHANS):
        route = [(c, (c + step) % CHANS) for c in range(CHANS)]
        blocks.append(lax.ppermute(windows[step], "chan", route))
    onward = relay(place, rates, arrived)
    onward = lax.all_to_all(onward, ("x", "chan"), 0, 0)
    return read_out(place, intervals, skip_gain.reshape(1, CH), onward, blocks, gathered, frames)


def solution(mesh):
    whole = jax.sharding.Mesh(
        mesh.devices.reshape(XS, ZS, CHANS, 2), ("x", "z", "chan", "clip")
    )
    time = ("clip", "x", "z")
    placed = (
        P(time, None, None, None),
        P(time),
        P("chan"),
        P(None, None, None, "chan"),
        P(None, None, "chan", None),
        P(),
    )
    return jax.shard_map(
        local,
        mesh=whole,
        in_specs=placed,
        out_specs=P(time, "chan", None, None),
        check_vma=False,
    )
```

```python
import functools

import jax
import jax.numpy as jnp
from jax import lax
from jax.experimental import pallas as pl
from jax.experimental.pallas import tpu as pltpu
from jax.sharding import PartitionSpec as P

F32 = jnp.float32
BF16 = jnp.bfloat16
FRAMES = 32
HALF = 16
ROWS = 16
WIDE = 16
CH = 256
OWN = 64
LANES = 128
CHANS = 4
ZS = 8
XS = 4
WINDOW = 6
STEP = 2
CHUNKS = HALF // STEP


def split3(value):
    high = value.astype(BF16)
    rest = value - high.astype(F32)
    middle = rest.astype(BF16)
    low = (rest - middle.astype(F32)).astype(BF16)
    return high, middle, low


def join3(block, start):
    parts = block.astype(F32)
    return parts[start : start + 1] + parts[start + 1 : start + 2] + parts[start + 2 : start + 3]


def low_half(shape):
    return lax.broadcasted_iota(jnp.int32, shape, len(shape) - 1) < OWN


def swap_halves(value):
    return pltpu.roll(value, OWN, value.ndim - 1)


def doubled(rates):
    row = jnp.concatenate([rates, rates], axis=1)
    return row


def table(low_values, high_values):
    row = lax.broadcasted_iota(jnp.int32, (HALF, LANES), 0)
    low = low_half((HALF, LANES))
    result = jnp.zeros((HALF, LANES), F32)
    for t in range(HALF):
        result = jnp.where(row == t, jnp.where(low, low_values[t], high_values[t]), result)
    return result


def spread(target, index, lanes, rows):
    for t in range(HALF):
        target[index, t, :, lanes] = jnp.broadcast_to(rows[t : t + 1], (WIDE, LANES))


def one_minus_exp(value):
    series = value * (
        1.0 - value * (0.5 - value * (1.0 / 6 - value * (1.0 / 24 - value * (1.0 / 120))))
    )
    return jnp.where(value < 0.125, series, 1.0 - jnp.exp(-value))


def running(values):
    sums = [values[0]]
    for value in values[1:]:
        sums.append(sums[-1] + value)
    return sums


def drive_kernel(
    place, intervals_far, rates_far, kernel_far, frames,
    own, one, two, three, message,
    intervals, rates, kernel_t, padded, weights, factors, state, kept,
    load_sem, store_sem, small_sem,
):
    windows = (own, one, two, three)
    small = [
        pltpu.make_async_copy(source, target, small_sem.at[index])
        for index, (source, target) in enumerate(
            ((kernel_far, kernel_t), (intervals_far, intervals), (rates_far, rates))
        )
    ]
    for copy in small:
        copy.start()

    def load(chunk, half):
        start = half * HALF + chunk * STEP
        return pltpu.make_async_copy(
            frames.at[pl.ds(start, STEP)],
            padded.at[pl.ds(start, STEP), pl.ds(1, ROWS)],
            load_sem.at[chunk, half],
        )

    def store(chunk, step):
        first = CHANS * lax.rem(place[0] + step, CHANS)
        return pltpu.make_async_copy(
            kept.at[pl.ds(chunk * STEP, STEP), pl.ds(first, WINDOW)],
            windows[step].at[pl.ds(chunk * STEP, STEP)],
            store_sem.at[chunk, step],
        )

    for chunk in range(CHUNKS):
        load(chunk, 0).start()
        load(chunk, 1).start()

    empty = jnp.zeros((FRAMES, 1, WIDE, CH), BF16)
    padded[:, 0:1] = empty
    padded[:, ROWS + 1 : ROWS + 2] = empty
    empty = jnp.zeros((HALF, 1, WIDE, LANES), BF16)
    kept[:, 0:1] = empty
    kept[:, ROWS + 1 : ROWS + 2] = empty
    nothing = jnp.zeros((CH, OWN), BF16)
    for copy in small:
        copy.wait()
    for i in range(3):
        tap = [kernel_t[3 * i + j].astype(F32).T.astype(BF16) for j in range(3)]
        weights[0, CH * i : CH * (i + 1), :] = jnp.concatenate([tap[0], tap[1], tap[2], nothing], 1)
        weights[1, CH * i : CH * (i + 1), :] = jnp.concatenate([tap[1], tap[0], nothing, tap[2]], 1)

    values = [intervals[t] for t in range(FRAMES)]
    rate = doubled(rates[...])
    scaled = table(values[:HALF], values[HALF:]) * rate
    spread(factors, 0, slice(None), jnp.exp(-scaled))
    spread(factors, 1, slice(None), jnp.sqrt(one_minus_exp(2.0 * scaled)))
    state[...] = jnp.zeros_like(state)

    def advance(chunk, carry):
        start = pl.multiple_of(chunk * STEP, STEP)

        def product(half):
            block = padded[pl.ds(half * HALF + start, STEP)]
            taps = [block[:, i : i + ROWS].reshape(STEP * ROWS * WIDE, CH) for i in range(3)]
            return jnp.dot(
                jnp.concatenate(taps, axis=1), weights[half], preferred_element_type=F32
            )

        load(chunk, 0).wait()
        load(chunk, 1).wait()
        first, second = product(0), product(1)
        low = low_half((STEP * ROWS * WIDE, LANES))
        left = jnp.where(low, first[:, :LANES], second[:, :LANES])
        centre = swap_halves(jnp.where(low, second[:, :LANES], first[:, :LANES]))
        right = first[:, LANES:] + second[:, LANES:]
        shape = (STEP * ROWS, WIDE, LANES)
        column = lax.broadcasted_iota(jnp.int32, shape, 1)
        left = jnp.where(column == 0, 0.0, pltpu.roll(left.reshape(shape), 1, 1))
        right = jnp.where(column == WIDE - 1, 0.0, pltpu.roll(right.reshape(shape), WIDE - 1, 1))
        drives = (left + centre.reshape(shape) + right).reshape(STEP, ROWS, WIDE, LANES)
        carried = state[...]
        for step in range(STEP):
            decay, gain = factors[0, start + step], factors[1, start + step]
            carried = decay * carried + gain * drives[step]
            kept[start + step, 1 : ROWS + 1] = carried.astype(BF16)
        state[...] = carried
        for step in range(CHANS):
            store(chunk, step).start()
        return carry

    lax.fori_loop(0, CHUNKS, advance, 0)

    late = functools.reduce(lambda a, b: a + b, values[HALF:])
    total = functools.reduce(lambda a, b: a + b, values[:HALF]) + late
    carried = state[...]
    end = carried + jnp.exp(-late * rate).reshape(1, 1, LANES) * swap_halves(carried)
    other = swap_halves(end)
    low = low_half((ROWS // 2, WIDE, LANES))
    packed = jnp.where(low, other[: ROWS // 2], end[ROWS // 2 :]).astype(BF16)
    row = lax.broadcasted_iota(jnp.int32, (WIDE, LANES), 0)
    pieces = split3(jnp.full((WIDE, LANES), total, F32))
    extra = jnp.where(row == 0, pieces[0].astype(F32), jnp.where(row == 1, pieces[1].astype(F32), pieces[2].astype(F32))).astype(BF16)
    for z in range(ZS):
        message[z, : ROWS // 2] = packed
        message[z, ROWS // 2] = extra
    for chunk in range(CHUNKS):
        for step in range(CHANS):
            store(chunk, step).wait()


def relay_kernel(place, rates_far, received, message, rates, small_sem):
    x, z = place[1], place[2]
    copy = pltpu.make_async_copy(rates_far, rates, small_sem)
    copy.start()
    copy.wait()
    rate = doubled(rates[...])
    total = jnp.zeros((ROWS // 2, WIDE, LANES), F32)
    before = total
    elapsed = jnp.zeros((1, LANES), F32)
    elapsed_before = elapsed
    for other in range(ZS):
        mine = z == other
        before = jnp.where(mine, total, before)
        elapsed_before = jnp.where(mine, elapsed, elapsed_before)
        spent = join3(received[other, ROWS // 2], 0)
        decay = jnp.exp(-spent * rate).reshape(1, 1, LANES)
        total = decay * total + received[other, : ROWS // 2].astype(F32)
        elapsed = elapsed + spent

    low = low_half((WIDE, LANES))
    blank = jnp.zeros((WIDE, LANES), F32)

    def rows_of(value):
        swapped = swap_halves(value)
        top = [jnp.where(low, value[r], swapped[r]) for r in range(ROWS // 2)]
        bottom = [jnp.where(low, swapped[r], value[r]) for r in range(ROWS // 2)]
        return [blank] + top + bottom + [blank]

    totals, befores = rows_of(total), rows_of(before)
    row = lax.broadcasted_iota(jnp.int32, (WIDE, LANES), 0)
    extra = blank
    pieces = split3(elapsed) + split3(elapsed_before) + split3(rate)
    for index, piece in enumerate(pieces):
        extra = jnp.where(row == index, piece.astype(F32), extra)
    extra = extra.astype(BF16)
    for chan in range(CHANS):
        for q in range(WINDOW // 2):
            here = CHANS * chan + q
            there = here + WINDOW // 2
            later = jnp.where(low, totals[here], totals[there]).astype(BF16)
            level = jnp.where(low, befores[here], befores[there]).astype(BF16)
            for to in range(XS):
                message[to * CHANS + chan, q] = jnp.where(x == to, level, later)
        for to in range(XS):
            message[to * CHANS + chan, WINDOW // 2] = extra


OUT_STEP = 8
OUT_CHUNKS = FRAMES // OUT_STEP


def readout_kernel(
    place, intervals_far, gain_far, received, own, one, two, three,
    kernel_own, kernel_one, kernel_two, kernel_three, frames,
    result,
    intervals, skip_gain, weights, direct, states, written, flows, base,
    load_sem, store_sem, small_sem,
):
    small = [
        pltpu.make_async_copy(intervals_far, intervals, small_sem.at[0]),
        pltpu.make_async_copy(gain_far, skip_gain, small_sem.at[1]),
    ]
    for copy in small:
        copy.start()
    kernels = (kernel_own, kernel_one, kernel_two, kernel_three)
    chan, x = place[0], place[1]
    blocks = (own, one, two, three)

    def fetch(step):
        return pltpu.make_async_copy(
            kernels[step],
            weights.at[:, pl.ds(OWN * step, OWN)],
            load_sem.at[step],
        )

    def fetch_direct():
        return pltpu.make_async_copy(
            frames.at[:, pl.ds(CHANS * chan, CHANS)], direct, load_sem.at[CHANS]
        )

    def store(chunk):
        part = pl.ds(chunk * OUT_STEP, OUT_STEP)
        return pltpu.make_async_copy(written.at[part], result.at[part], store_sem.at[chunk])

    for step in range(CHANS):
        fetch(step).start()
    fetch_direct().start()

    low = low_half((WIDE, LANES))
    rates, entering = [], []
    for step in range(CHANS):
        source = lax.rem(chan + CHANS - step, CHANS)
        level = received[x * CHANS + source]
        rate = join3(level[WINDOW // 2], 6)
        spent = join3(level[WINDOW // 2], 3)
        total = jnp.zeros((WINDOW // 2, WIDE, LANES), F32)
        for other in range(XS - 1):
            earlier = received[other * CHANS + source]
            decay = jnp.exp(-join3(earlier[WINDOW // 2], 0) * rate).reshape(1, 1, LANES)
            added = decay * total + earlier[: WINDOW // 2].astype(F32)
            total = jnp.where(other < x, added, total)
        decay = jnp.exp(-spent * rate).reshape(1, 1, LANES)
        total = level[: WINDOW // 2].astype(F32) + decay * total
        swapped = swap_halves(total)
        rates.append(rate)
        entering.append(
            [jnp.where(low, total[r], swapped[r]) for r in range(WINDOW // 2)]
            + [jnp.where(low, swapped[r], total[r]) for r in range(WINDOW // 2)]
        )

    for copy in small:
        copy.wait()
    values = [intervals[t] for t in range(FRAMES)]
    first, second = running(values[:HALF]), running(values[HALF:])
    first_table, second_table = table(first, first), table(second, second)
    low_row = low_half((1, LANES))

    def halves(t, pair):
        a = blocks[2 * pair][t].astype(F32)
        b = blocks[2 * pair + 1][t].astype(F32)
        low = low_half(a.shape)
        return jnp.where(low, a, swap_halves(b)), jnp.where(low, swap_halves(a), b)

    for pair in range(2):
        rate = jnp.where(low_row, rates[2 * pair], rates[2 * pair + 1])
        part = slice(LANES * pair, LANES * (pair + 1))
        inflow = jnp.exp(-first_table * rate)
        spread(flows, 0, part, inflow)
        spread(flows, 1, part, jnp.exp(-second_table * rate))
        last = halves(HALF - 1, pair)[0]
        for r in range(WINDOW):
            arriving = jnp.where(low, entering[2 * pair][r], entering[2 * pair + 1][r])
            base[0, r, :, part] = arriving
            base[1, r, :, part] = inflow[HALF - 1 :] * arriving + last[r]

    def fill(t, carry):
        for pair in range(2):
            part = slice(LANES * pair, LANES * (pair + 1))
            for half, local in enumerate(halves(t, pair)):
                flow = flows[half, t, :, part]
                full = local + flow * base[half, :, :, part]
                states[half * HALF + t, :, :, part] = full.astype(BF16)
        return carry

    lax.fori_loop(0, HALF, fill, 0)
    for step in range(CHANS):
        fetch(step).wait()
    fetch_direct().wait()

    def convolve(chunk, carry):
        start = pl.multiple_of(chunk * OUT_STEP, OUT_STEP)
        size = OUT_STEP * CHANS * WIDE
        block = states[pl.ds(start, OUT_STEP)]
        taps = [block[:, i : i + CHANS].reshape(size, CH) for i in range(3)]
        operand = jnp.concatenate(taps, axis=1)
        shape = (OUT_STEP * CHANS, WIDE, CH)
        column = lax.broadcasted_iota(jnp.int32, shape, 1)
        parts = []
        for j in range(3):
            weight = jnp.concatenate([weights[3 * i + j] for i in range(3)], axis=0)
            parts.append(jnp.dot(operand, weight, preferred_element_type=F32).reshape(shape))
        total = parts[1]
        total += jnp.where(column == 0, 0.0, pltpu.roll(parts[0], 1, 1))
        total += jnp.where(column == WIDE - 1, 0.0, pltpu.roll(parts[2], WIDE - 1, 1))
        passed = direct[pl.ds(start, OUT_STEP)].astype(F32).reshape(shape)
        total += skip_gain[...].reshape(1, 1, CH) * passed
        written[pl.ds(start, OUT_STEP)] = total.astype(BF16).reshape(OUT_STEP, CHANS, WIDE, CH)
        store(chunk).start()
        return carry

    lax.fori_loop(0, OUT_CHUNKS, convolve, 0)
    for chunk in range(OUT_CHUNKS):
        store(chunk).wait()


def in_vmem():
    return pl.BlockSpec(memory_space=pltpu.VMEM)


def in_smem():
    return pl.BlockSpec(memory_space=pltpu.SMEM)


def anywhere():
    return pl.BlockSpec(memory_space=pl.ANY)


def far():
    return pl.BlockSpec(memory_space=pltpu.HBM)


def drive(place, intervals, rates, kernel_t, frames):
    window = jax.ShapeDtypeStruct((HALF, WINDOW, WIDE, LANES), BF16)
    return pl.pallas_call(
        drive_kernel,
        out_shape=[window] * CHANS
        + [jax.ShapeDtypeStruct((ZS, ROWS // 2 + 1, WIDE, LANES), BF16)],
        in_specs=[in_smem(), far(), far(), far(), far()],
        out_specs=[anywhere()] * CHANS + [in_vmem()],
        scratch_shapes=[
            pltpu.SMEM((FRAMES,), F32),
            pltpu.VMEM((1, OWN), F32),
            pltpu.VMEM((9, OWN, CH), BF16),
            pltpu.VMEM((FRAMES, ROWS + 2, WIDE, CH), BF16),
            pltpu.VMEM((2, 3 * CH, CH), BF16),
            pltpu.VMEM((2, HALF, WIDE, LANES), F32),
            pltpu.VMEM((ROWS, WIDE, LANES), F32),
            pltpu.VMEM((HALF, ROWS + 2, WIDE, LANES), BF16),
            pltpu.SemaphoreType.DMA((CHUNKS, 2)),
            pltpu.SemaphoreType.DMA((CHUNKS, CHANS)),
            pltpu.SemaphoreType.DMA((3,)),
        ],
        compiler_params=pltpu.CompilerParams(vmem_limit_bytes=62 << 20),
        name="drive",
    )(place, intervals, rates, kernel_t, frames)


def relay(place, rates, received):
    return pl.pallas_call(
        relay_kernel,
        out_shape=jax.ShapeDtypeStruct((XS * CHANS, WINDOW // 2 + 1, WIDE, LANES), BF16),
        in_specs=[in_smem(), far(), in_vmem()],
        out_specs=in_vmem(),
        scratch_shapes=[pltpu.VMEM((1, OWN), F32), pltpu.SemaphoreType.DMA],
        compiler_params=pltpu.CompilerParams(vmem_limit_bytes=16 << 20),
        name="relay",
    )(place, rates, received)


def read_out(place, intervals, skip_gain, received, blocks, kernels, frames):
    return pl.pallas_call(
        readout_kernel,
        out_shape=jax.ShapeDtypeStruct((FRAMES, CHANS, WIDE, CH), BF16),
        in_specs=[in_smem(), far(), far(), in_vmem()]
        + [in_vmem()] * CHANS
        + [far()]
        + [anywhere()] * (CHANS - 1)
        + [far()],
        out_specs=anywhere(),
        scratch_shapes=[
            pltpu.SMEM((FRAMES,), F32),
            pltpu.VMEM((1, CH), F32),
            pltpu.VMEM((9, CHANS * OWN, CH), BF16),
            pltpu.VMEM((FRAMES, CHANS, WIDE, CH), BF16),
            pltpu.VMEM((FRAMES, WINDOW, WIDE, CH), BF16),
            pltpu.VMEM((FRAMES, CHANS, WIDE, CH), BF16),
            pltpu.VMEM((2, HALF, WIDE, CH), F32),
            pltpu.VMEM((2, WINDOW, WIDE, CH), F32),
            pltpu.SemaphoreType.DMA((CHANS + 1,)),
            pltpu.SemaphoreType.DMA((OUT_CHUNKS,)),
            pltpu.SemaphoreType.DMA((2,)),
        ],
        compiler_params=pltpu.CompilerParams(vmem_limit_bytes=62 << 20),
        name="read_out",
    )(place, intervals, skip_gain, received, *blocks, *kernels, frames)


def local(frames, intervals, decay_rates, in_kernel, out_kernel, skip_gain):
    place = jnp.stack([lax.axis_index(name) for name in ("chan", "x", "z")]).astype(jnp.int32)
    rates = decay_rates.reshape(1, OWN)
    kernel_t = jnp.transpose(in_kernel.reshape(9, CH, OWN), (0, 2, 1))
    kernels = [out_kernel.reshape(9, OWN, CH)]
    kernels += [around(kernels[0], step) for step in range(1, CHANS)]
    *windows, message = drive(place, intervals, rates, kernel_t, frames)
    arrived = lax.all_to_all(message, "z", 0, 0)
    blocks = [windows[0]] + [around(windows[step], step) for step in range(1, CHANS)]
    onward = relay(place, rates, arrived)
    onward = lax.all_to_all(onward, ("x", "chan"), 0, 0)
    return read_out(place, intervals, skip_gain.reshape(1, CH), onward, blocks, kernels, frames)


def around(value, step):
    return lax.ppermute(value, "chan", [(c, (c + step) % CHANS) for c in range(CHANS)])


def solution(mesh):
    whole = jax.sharding.Mesh(
        mesh.devices.reshape(XS, ZS, CHANS, 2), ("x", "z", "chan", "clip")
    )
    time = ("clip", "x", "z")
    placed = (
        P(time, None, None, None),
        P(time),
        P("chan"),
        P(None, None, None, "chan"),
        P(None, None, "chan", None),
        P(),
    )
    return jax.shard_map(
        local,
        mesh=whole,
        in_specs=placed,
        out_specs=P(time, "chan", None, None),
        check_vma=False,
    )
```

```python
import functools

import jax
import jax.numpy as jnp
from jax import lax
from jax.experimental import pallas as pl
from jax.experimental.pallas import tpu as pltpu
from jax.sharding import PartitionSpec as P

F32 = jnp.float32
BF16 = jnp.bfloat16
FRAMES = 32
HALF = 16
ROWS = 16
WIDE = 16
CH = 256
OWN = 64
LANES = 128
CHANS = 4
ZS = 8
XS = 4
WINDOW = 6
STEP = 2
CHUNKS = HALF // STEP


def split3(value):
    high = value.astype(BF16)
    rest = value - high.astype(F32)
    middle = rest.astype(BF16)
    low = (rest - middle.astype(F32)).astype(BF16)
    return high, middle, low


def join3(block, start):
    parts = block.astype(F32)
    return parts[start : start + 1] + parts[start + 1 : start + 2] + parts[start + 2 : start + 3]


def low_half(shape):
    return lax.broadcasted_iota(jnp.int32, shape, len(shape) - 1) < OWN


def swap_halves(value):
    return pltpu.roll(value, OWN, value.ndim - 1)


def doubled(rates):
    row = jnp.concatenate([rates, rates], axis=1)
    return row


def table(low_values, high_values):
    row = lax.broadcasted_iota(jnp.int32, (HALF, LANES), 0)
    low = low_half((HALF, LANES))
    result = jnp.zeros((HALF, LANES), F32)
    for t in range(HALF):
        result = jnp.where(row == t, jnp.where(low, low_values[t], high_values[t]), result)
    return result


def spread(target, index, lanes, rows):
    for t in range(HALF):
        target[index, t, :, lanes] = jnp.broadcast_to(rows[t : t + 1], (WIDE, LANES))


def one_minus_exp(value):
    series = value * (
        1.0 - value * (0.5 - value * (1.0 / 6 - value * (1.0 / 24 - value * (1.0 / 120))))
    )
    return jnp.where(value < 0.125, series, 1.0 - jnp.exp(-value))


def beside(left, centre, right):
    column = lax.broadcasted_iota(jnp.int32, centre.shape, 1)
    total = centre + jnp.where(column == 0, 0.0, pltpu.roll(left, 1, 1))
    return total + jnp.where(column == WIDE - 1, 0.0, pltpu.roll(right, WIDE - 1, 1))


def running(values):
    sums = [values[0]]
    for value in values[1:]:
        sums.append(sums[-1] + value)
    return sums


def drive_kernel(
    intervals_far, rates_far, kernel_far, frames,
    message,
    intervals, rates, kernel_t, padded, weights, factors, state, load_sem, small_sem,
):
    small = [
        pltpu.make_async_copy(source, target, small_sem.at[index])
        for index, (source, target) in enumerate(
            ((kernel_far, kernel_t), (intervals_far, intervals), (rates_far, rates))
        )
    ]
    for copy in small:
        copy.start()

    def load(chunk, half):
        start = half * HALF + chunk * STEP
        return pltpu.make_async_copy(
            frames.at[pl.ds(start, STEP)],
            padded.at[pl.ds(start, STEP), pl.ds(1, ROWS)],
            load_sem.at[chunk, half],
        )

    for chunk in range(CHUNKS):
        load(chunk, 0).start()
        load(chunk, 1).start()

    empty = jnp.zeros((FRAMES, 1, WIDE, CH), BF16)
    padded[:, 0:1] = empty
    padded[:, ROWS + 1 : ROWS + 2] = empty
    nothing = jnp.zeros((CH, OWN), BF16)
    for copy in small:
        copy.wait()
    for i in range(3):
        tap = [kernel_t[3 * i + j].astype(F32).T.astype(BF16) for j in range(3)]
        weights[0, CH * i : CH * (i + 1), :] = jnp.concatenate([tap[0], tap[1], tap[2], nothing], 1)
        weights[1, CH * i : CH * (i + 1), :] = jnp.concatenate([tap[1], tap[0], nothing, tap[2]], 1)

    values = [intervals[t] for t in range(FRAMES)]
    rate = doubled(rates[...])
    scaled = table(values[:HALF], values[HALF:]) * rate
    spread(factors, 0, slice(None), jnp.exp(-scaled))
    spread(factors, 1, slice(None), jnp.sqrt(one_minus_exp(2.0 * scaled)))
    state[...] = jnp.zeros_like(state)

    def advance(chunk, carry):
        start = pl.multiple_of(chunk * STEP, STEP)

        def product(half):
            block = padded[pl.ds(half * HALF + start, STEP)]
            taps = [block[:, i : i + ROWS].reshape(STEP * ROWS * WIDE, CH) for i in range(3)]
            return jnp.dot(
                jnp.concatenate(taps, axis=1), weights[half], preferred_element_type=F32
            )

        load(chunk, 0).wait()
        load(chunk, 1).wait()
        first, second = product(0), product(1)
        low = low_half((STEP * ROWS * WIDE, LANES))
        left = jnp.where(low, first[:, :LANES], second[:, :LANES])
        centre = swap_halves(jnp.where(low, second[:, :LANES], first[:, :LANES]))
        right = first[:, LANES:] + second[:, LANES:]
        shape = (STEP * ROWS, WIDE, LANES)
        drives = beside(left.reshape(shape), centre.reshape(shape), right.reshape(shape))
        drives = drives.reshape(STEP, ROWS, WIDE, LANES)
        carried = state[...]
        for step in range(STEP):
            decay, gain = factors[0, start + step], factors[1, start + step]
            carried = decay * carried + gain * drives[step]
        state[...] = carried
        return carry

    lax.fori_loop(0, CHUNKS, advance, 0)

    late = functools.reduce(lambda a, b: a + b, values[HALF:])
    total = functools.reduce(lambda a, b: a + b, values[:HALF]) + late
    carried = state[...]
    end = carried + jnp.exp(-late * rate).reshape(1, 1, LANES) * swap_halves(carried)
    other = swap_halves(end)
    low = low_half((ROWS // 2, WIDE, LANES))
    packed = jnp.where(low, other[: ROWS // 2], end[ROWS // 2 :]).astype(BF16)
    row = lax.broadcasted_iota(jnp.int32, (WIDE, LANES), 0)
    pieces = split3(jnp.full((WIDE, LANES), total, F32))
    extra = jnp.zeros((WIDE, LANES), F32)
    for index, piece in enumerate(pieces):
        extra = jnp.where(row == index, piece.astype(F32), extra)
    extra = extra.astype(BF16)
    for z in range(ZS):
        message[z, : ROWS // 2] = packed
        message[z, ROWS // 2] = extra


WINDOW_STEP = 4
WINDOW_CHUNKS = FRAMES // WINDOW_STEP
TALL = 12


def window_kernel(
    place, kernel_own, kernel_one, kernel_two, kernel_three, frames,
    drives, token,
    rows, weights, written, load_sem, kernel_sem, store_sem,
):
    chan = place[0]
    kernels = (kernel_own, kernel_one, kernel_two, kernel_three)
    source = jnp.clip(CHANS * chan - 2, 0, 8)
    target = source - CHANS * chan + 4

    def load(chunk):
        part = pl.ds(chunk * WINDOW_STEP, WINDOW_STEP)
        return pltpu.make_async_copy(
            frames.at[part, pl.ds(source, 8)], rows.at[part, pl.ds(target, 8)], load_sem.at[chunk]
        )

    def fetch(step):
        return pltpu.make_async_copy(
            kernels[step], weights.at[:, pl.ds(OWN * step, OWN)], kernel_sem.at[step]
        )

    def store(chunk):
        part = pl.ds(chunk * WINDOW_STEP, WINDOW_STEP)
        return pltpu.make_async_copy(written.at[part], drives.at[part], store_sem.at[chunk])

    token[...] = jnp.zeros_like(token)
    for step in range(CHANS):
        fetch(step).start()
    for chunk in range(WINDOW_CHUNKS):
        load(chunk).start()
    empty = jnp.zeros((FRAMES, 2, WIDE, CH), BF16)

    @pl.when(chan == 0)
    def _():
        rows[:, 2:4] = empty

    @pl.when(chan == CHANS - 1)
    def _():
        rows[:, 8:10] = empty

    for step in range(CHANS):
        fetch(step).wait()

    def convolve(chunk, carry):
        load(chunk).wait()
        start = pl.multiple_of(chunk * WINDOW_STEP, WINDOW_STEP)
        block = rows[pl.ds(start, WINDOW_STEP)]
        size = WINDOW_STEP * WINDOW * WIDE
        taps = [block[:, 2 + i : 2 + i + WINDOW].reshape(size, CH) for i in range(3)]
        operand = jnp.concatenate(taps, axis=1)
        shape = (WINDOW_STEP * WINDOW, WIDE, CH)
        parts = []
        for j in range(3):
            weight = jnp.concatenate([weights[3 * i + j] for i in range(3)], axis=1)
            parts.append(
                lax.dot_general(
                    operand, weight, (((1,), (1,)), ((), ())), preferred_element_type=F32
                ).reshape(shape)
            )
        total = beside(*parts).reshape(WINDOW_STEP, WINDOW, WIDE, CH)
        for r in range(WINDOW):
            kept = total[:, r]
            if r == 0:
                kept = jnp.where(chan == 0, 0.0, kept)
            if r == WINDOW - 1:
                kept = jnp.where(chan == CHANS - 1, 0.0, kept)
            written[pl.ds(start, WINDOW_STEP), r] = kept.astype(BF16)
        store(chunk).start()
        return carry

    lax.fori_loop(0, WINDOW_CHUNKS, convolve, 0)
    for chunk in range(WINDOW_CHUNKS):
        store(chunk).wait()


def relay_kernel(place, rates_far, received, token, message, rates, small_sem):
    x, z = place[1], place[2]
    copy = pltpu.make_async_copy(rates_far, rates, small_sem)
    copy.start()
    copy.wait()
    rate = doubled(rates[...])
    total = jnp.zeros((ROWS // 2, WIDE, LANES), F32)
    before = total
    elapsed = jnp.zeros((1, LANES), F32)
    elapsed_before = elapsed
    for other in range(ZS):
        mine = z == other
        before = jnp.where(mine, total, before)
        elapsed_before = jnp.where(mine, elapsed, elapsed_before)
        spent = join3(received[other, ROWS // 2], 0)
        decay = jnp.exp(-spent * rate).reshape(1, 1, LANES)
        total = decay * total + received[other, : ROWS // 2].astype(F32)
        elapsed = elapsed + spent

    low = low_half((WIDE, LANES))
    blank = jnp.zeros((WIDE, LANES), F32)

    def rows_of(value):
        swapped = swap_halves(value)
        top = [jnp.where(low, value[r], swapped[r]) for r in range(ROWS // 2)]
        bottom = [jnp.where(low, swapped[r], value[r]) for r in range(ROWS // 2)]
        return [blank] + top + bottom + [blank]

    totals, befores = rows_of(total), rows_of(before)
    row = lax.broadcasted_iota(jnp.int32, (WIDE, LANES), 0)
    extra = blank
    pieces = split3(elapsed) + split3(elapsed_before) + split3(rate)
    for index, piece in enumerate(pieces):
        extra = jnp.where(row == index, piece.astype(F32), extra)
    extra = extra.astype(BF16)
    for chan in range(CHANS):
        for q in range(WINDOW // 2):
            here = CHANS * chan + q
            there = here + WINDOW // 2
            later = jnp.where(low, totals[here], totals[there]).astype(BF16)
            level = jnp.where(low, befores[here], befores[there]).astype(BF16)
            for to in range(XS):
                message[to * CHANS + chan, q] = jnp.where(x == to, level, later)
        for to in range(XS):
            message[to * CHANS + chan, WINDOW // 2] = extra


OUT_STEP = 8
OUT_CHUNKS = FRAMES // OUT_STEP


def readout_kernel(
    place, intervals_far, gain_far, received, drives_far,
    kernel_own, kernel_one, kernel_two, kernel_three, frames,
    result,
    intervals, skip_gain, weights, direct, drives, states, written, factors, state,
    load_sem, drive_sem, store_sem, small_sem,
):
    small = [
        pltpu.make_async_copy(intervals_far, intervals, small_sem.at[0]),
        pltpu.make_async_copy(gain_far, skip_gain, small_sem.at[1]),
    ]
    for copy in small:
        copy.start()
    kernels = (kernel_own, kernel_one, kernel_two, kernel_three)
    chan, x = place[0], place[1]

    def fetch(step):
        return pltpu.make_async_copy(
            kernels[step], weights.at[:, pl.ds(OWN * step, OWN)], load_sem.at[step]
        )

    def fetch_direct():
        return pltpu.make_async_copy(
            frames.at[:, pl.ds(CHANS * chan, CHANS)], direct, load_sem.at[CHANS]
        )

    def load(chunk):
        part = pl.ds(chunk * OUT_STEP, OUT_STEP)
        return pltpu.make_async_copy(drives_far.at[part], drives.at[part], drive_sem.at[chunk])

    def store(chunk):
        part = pl.ds(chunk * OUT_STEP, OUT_STEP)
        return pltpu.make_async_copy(written.at[part], result.at[part], store_sem.at[chunk])

    for chunk in range(OUT_CHUNKS):
        load(chunk).start()
    for step in range(CHANS):
        fetch(step).start()
    fetch_direct().start()

    low = low_half((WIDE, LANES))
    rates, entering = [], []
    for step in range(CHANS):
        source = lax.rem(chan + CHANS - step, CHANS)
        level = received[x * CHANS + source]
        rate = join3(level[WINDOW // 2], 6)
        spent = join3(level[WINDOW // 2], 3)
        total = jnp.zeros((WINDOW // 2, WIDE, LANES), F32)
        for other in range(XS - 1):
            earlier = received[other * CHANS + source]
            decay = jnp.exp(-join3(earlier[WINDOW // 2], 0) * rate).reshape(1, 1, LANES)
            added = decay * total + earlier[: WINDOW // 2].astype(F32)
            total = jnp.where(other < x, added, total)
        decay = jnp.exp(-spent * rate).reshape(1, 1, LANES)
        total = level[: WINDOW // 2].astype(F32) + decay * total
        swapped = swap_halves(total)
        rates.append(rate)
        entering.append(
            [jnp.where(low, total[r], swapped[r]) for r in range(WINDOW // 2)]
            + [jnp.where(low, swapped[r], total[r]) for r in range(WINDOW // 2)]
        )

    for copy in small:
        copy.wait()
    values = [intervals[t] for t in range(FRAMES)]
    low_row = low_half((1, LANES))
    for pair in range(2):
        rate = jnp.where(low_row, rates[2 * pair], rates[2 * pair + 1])
        part = slice(LANES * pair, LANES * (pair + 1))
        for half in range(2):
            some = values[HALF * half : HALF * (half + 1)]
            scaled = table(some, some) * rate
            rest = pl.ds(HALF * half, HALF)
            spread(factors.at[:, rest], 0, part, jnp.exp(-scaled))
            spread(factors.at[:, rest], 1, part, jnp.sqrt(one_minus_exp(2.0 * scaled)))
        for r in range(WINDOW):
            state[r, :, part] = jnp.where(low, entering[2 * pair][r], entering[2 * pair + 1][r])

    for step in range(CHANS):
        fetch(step).wait()
    fetch_direct().wait()

    def convolve(chunk, carry):
        start = pl.multiple_of(chunk * OUT_STEP, OUT_STEP)
        load(chunk).wait()
        carried = state[...]
        for step in range(OUT_STEP):
            decay, gain = factors[0, start + step], factors[1, start + step]
            carried = decay * carried + gain * drives[start + step].astype(F32)
            states[start + step] = carried.astype(BF16)
        state[...] = carried
        size = OUT_STEP * CHANS * WIDE
        block = states[pl.ds(start, OUT_STEP)]
        taps = [block[:, i : i + CHANS].reshape(size, CH) for i in range(3)]
        operand = jnp.concatenate(taps, axis=1)
        shape = (OUT_STEP * CHANS, WIDE, CH)
        parts = []
        for j in range(3):
            weight = jnp.concatenate([weights[3 * i + j] for i in range(3)], axis=0)
            parts.append(jnp.dot(operand, weight, preferred_element_type=F32).reshape(shape))
        passed = direct[pl.ds(start, OUT_STEP)].astype(F32).reshape(shape)
        total = beside(*parts) + skip_gain[...].reshape(1, 1, CH) * passed
        written[pl.ds(start, OUT_STEP)] = total.astype(BF16).reshape(OUT_STEP, CHANS, WIDE, CH)
        store(chunk).start()
        return carry

    lax.fori_loop(0, OUT_CHUNKS, convolve, 0)
    for chunk in range(OUT_CHUNKS):
        store(chunk).wait()


def in_vmem():
    return pl.BlockSpec(memory_space=pltpu.VMEM)


def in_smem():
    return pl.BlockSpec(memory_space=pltpu.SMEM)


def anywhere():
    return pl.BlockSpec(memory_space=pl.ANY)


def cost(microseconds):
    return pl.CostEstimate(
        flops=int(microseconds * 1.1e9), bytes_accessed=1 << 20, transcendentals=0
    )


def drive(intervals, rates, kernel_t, frames):
    return pl.pallas_call(
        drive_kernel,
        out_shape=jax.ShapeDtypeStruct((ZS, ROWS // 2 + 1, WIDE, LANES), BF16),
        in_specs=[anywhere()] * 4,
        out_specs=in_vmem(),
        scratch_shapes=[
            pltpu.SMEM((FRAMES,), F32),
            pltpu.VMEM((1, OWN), F32),
            pltpu.VMEM((9, OWN, CH), BF16),
            pltpu.VMEM((FRAMES, ROWS + 2, WIDE, CH), BF16),
            pltpu.VMEM((2, 3 * CH, CH), BF16),
            pltpu.VMEM((2, HALF, WIDE, LANES), F32),
            pltpu.VMEM((ROWS, WIDE, LANES), F32),
            pltpu.SemaphoreType.DMA((CHUNKS, 2)),
            pltpu.SemaphoreType.DMA((3,)),
        ],
        compiler_params=pltpu.CompilerParams(vmem_limit_bytes=62 << 20),
        cost_estimate=cost(8),
        name="drive",
    )(intervals, rates, kernel_t, frames)


def window(place, kernels, frames):
    return pl.pallas_call(
        window_kernel,
        out_shape=[
            jax.ShapeDtypeStruct((FRAMES, WINDOW, WIDE, CH), BF16),
            jax.ShapeDtypeStruct((8, LANES), F32),
        ],
        in_specs=[in_smem()] + [anywhere()] * (CHANS + 1),
        out_specs=[anywhere(), in_vmem()],
        scratch_shapes=[
            pltpu.VMEM((FRAMES, TALL, WIDE, CH), BF16),
            pltpu.VMEM((9, CHANS * OWN, CH), BF16),
            pltpu.VMEM((FRAMES, WINDOW, WIDE, CH), BF16),
            pltpu.SemaphoreType.DMA((WINDOW_CHUNKS,)),
            pltpu.SemaphoreType.DMA((CHANS,)),
            pltpu.SemaphoreType.DMA((WINDOW_CHUNKS,)),
        ],
        compiler_params=pltpu.CompilerParams(vmem_limit_bytes=61 << 20),
        cost_estimate=cost(6),
        name="window",
    )(place, *kernels, frames)


def relay(place, rates, received, token):
    return pl.pallas_call(
        relay_kernel,
        out_shape=jax.ShapeDtypeStruct((XS * CHANS, WINDOW // 2 + 1, WIDE, LANES), BF16),
        in_specs=[in_smem(), anywhere(), in_vmem(), anywhere()],
        out_specs=in_vmem(),
        scratch_shapes=[pltpu.VMEM((1, OWN), F32), pltpu.SemaphoreType.DMA],
        compiler_params=pltpu.CompilerParams(vmem_limit_bytes=16 << 20),
        cost_estimate=cost(1),
        name="relay",
    )(place, rates, received, token)


def read_out(place, intervals, skip_gain, received, drives, kernels, frames):
    return pl.pallas_call(
        readout_kernel,
        out_shape=jax.ShapeDtypeStruct((FRAMES, CHANS, WIDE, CH), BF16),
        in_specs=[in_smem(), anywhere(), anywhere(), in_vmem()] + [anywhere()] * (CHANS + 2),
        out_specs=anywhere(),
        scratch_shapes=[
            pltpu.SMEM((FRAMES,), F32),
            pltpu.VMEM((1, CH), F32),
            pltpu.VMEM((9, CHANS * OWN, CH), BF16),
            pltpu.VMEM((FRAMES, CHANS, WIDE, CH), BF16),
            pltpu.VMEM((FRAMES, WINDOW, WIDE, CH), BF16),
            pltpu.VMEM((FRAMES, WINDOW, WIDE, CH), BF16),
            pltpu.VMEM((FRAMES, CHANS, WIDE, CH), BF16),
            pltpu.VMEM((2, FRAMES, WIDE, CH), F32),
            pltpu.VMEM((WINDOW, WIDE, CH), F32),
            pltpu.SemaphoreType.DMA((CHANS + 1,)),
            pltpu.SemaphoreType.DMA((OUT_CHUNKS,)),
            pltpu.SemaphoreType.DMA((OUT_CHUNKS,)),
            pltpu.SemaphoreType.DMA((2,)),
        ],
        compiler_params=pltpu.CompilerParams(vmem_limit_bytes=61 << 20),
        cost_estimate=cost(6),
        name="read_out",
    )(place, intervals, skip_gain, received, drives, *kernels, frames)


def around(value):
    routes = [[(c, (c + step) % CHANS) for c in range(CHANS)] for step in range(1, CHANS)]
    return [value] + [lax.ppermute(value, "chan", route) for route in routes]


def local(frames, intervals, decay_rates, in_kernel, out_kernel, skip_gain):
    place = jnp.stack([lax.axis_index(name) for name in ("chan", "x", "z")]).astype(jnp.int32)
    rates = decay_rates.reshape(1, OWN)
    kernel_t = jnp.transpose(in_kernel.reshape(9, CH, OWN), (0, 2, 1))
    in_kernels = around(kernel_t)
    out_kernels = around(out_kernel.reshape(9, OWN, CH))
    message = drive(intervals, rates, kernel_t, frames)
    arrived = lax.all_to_all(message, "z", 0, 0)
    drives, token = window(place, in_kernels, frames)
    onward = relay(place, rates, arrived, token)
    onward = lax.all_to_all(onward, ("x", "chan"), 0, 0)
    return read_out(
        place, intervals, skip_gain.reshape(1, CH), onward, drives, out_kernels, frames
    )


def solution(mesh):
    whole = jax.sharding.Mesh(
        mesh.devices.reshape(XS, ZS, CHANS, 2), ("x", "z", "chan", "clip")
    )
    time = ("clip", "x", "z")
    placed = (
        P(time, None, None, None),
        P(time),
        P("chan"),
        P(None, None, None, "chan"),
        P(None, None, "chan", None),
        P(),
    )
    return jax.shard_map(
        local,
        mesh=whole,
        in_specs=placed,
        out_specs=P(time, "chan", None, None),
        check_vma=False,
    )
```

```python
import functools

import jax
import jax.numpy as jnp
from jax import lax
from jax.experimental import pallas as pl
from jax.experimental.pallas import tpu as pltpu
from jax.sharding import PartitionSpec as P

F32 = jnp.float32
BF16 = jnp.bfloat16
FRAMES = 32
HALF = 16
ROWS = 16
WIDE = 16
CH = 256
OWN = 64
LANES = 128
CHANS = 4
ZS = 8
XS = 4
WINDOW = 6
STEP = 4
CHUNKS = HALF // STEP


def split3(value):
    high = value.astype(BF16)
    rest = value - high.astype(F32)
    middle = rest.astype(BF16)
    low = (rest - middle.astype(F32)).astype(BF16)
    return high, middle, low


def join3(block, start):
    parts = block.astype(F32)
    return parts[start : start + 1] + parts[start + 1 : start + 2] + parts[start + 2 : start + 3]


def low_half(shape):
    return lax.broadcasted_iota(jnp.int32, shape, len(shape) - 1) < OWN


def swap_halves(value):
    return pltpu.roll(value, OWN, value.ndim - 1)


def doubled(rates):
    row = jnp.concatenate([rates, rates], axis=1)
    return row


def table(low_values, high_values):
    row = lax.broadcasted_iota(jnp.int32, (HALF, LANES), 0)
    low = low_half((HALF, LANES))
    result = jnp.zeros((HALF, LANES), F32)
    for t in range(HALF):
        result = jnp.where(row == t, jnp.where(low, low_values[t], high_values[t]), result)
    return result


def spread(target, index, lanes, rows):
    for t in range(HALF):
        target[index, t, :, lanes] = jnp.broadcast_to(rows[t : t + 1], (WIDE, LANES))


def one_minus_exp(value):
    series = value * (
        1.0 - value * (0.5 - value * (1.0 / 6 - value * (1.0 / 24 - value * (1.0 / 120))))
    )
    return jnp.where(value < 0.125, series, 1.0 - jnp.exp(-value))


def beside(left, centre, right):
    column = lax.broadcasted_iota(jnp.int32, centre.shape, 1)
    total = centre + jnp.where(column == 0, 0.0, pltpu.roll(left, 1, 1))
    return total + jnp.where(column == WIDE - 1, 0.0, pltpu.roll(right, WIDE - 1, 1))


def running(values):
    sums = [values[0]]
    for value in values[1:]:
        sums.append(sums[-1] + value)
    return sums


def drive_kernel(
    intervals_far, rates_far, kernel_far, frames,
    message,
    intervals, rates, kernel_t, padded, weights, factors, state, load_sem, small_sem,
):
    small = [
        pltpu.make_async_copy(source, target, small_sem.at[index])
        for index, (source, target) in enumerate(
            ((kernel_far, kernel_t), (intervals_far, intervals), (rates_far, rates))
        )
    ]
    for copy in small:
        copy.start()

    def load(chunk, half):
        start = half * HALF + chunk * STEP
        return pltpu.make_async_copy(
            frames.at[pl.ds(start, STEP)],
            padded.at[pl.ds(start, STEP), pl.ds(1, ROWS)],
            load_sem.at[chunk, half],
        )

    for chunk in range(CHUNKS):
        load(chunk, 0).start()
        load(chunk, 1).start()

    empty = jnp.zeros((FRAMES, 1, WIDE, CH), BF16)
    padded[:, 0:1] = empty
    padded[:, ROWS + 1 : ROWS + 2] = empty
    nothing = jnp.zeros((CH, OWN), BF16)
    for copy in small:
        copy.wait()
    for i in range(3):
        tap = [kernel_t[3 * i + j].astype(F32).T.astype(BF16) for j in range(3)]
        weights[0, CH * i : CH * (i + 1), :] = jnp.concatenate([tap[0], tap[1], tap[2], nothing], 1)
        weights[1, CH * i : CH * (i + 1), :] = jnp.concatenate([tap[1], tap[0], nothing, tap[2]], 1)

    values = [intervals[t] for t in range(FRAMES)]
    rate = doubled(rates[...])
    scaled = table(values[:HALF], values[HALF:]) * rate
    spread(factors, 0, slice(None), jnp.exp(-scaled))
    spread(factors, 1, slice(None), jnp.sqrt(one_minus_exp(2.0 * scaled)))
    state[...] = jnp.zeros_like(state)

    def advance(chunk, carry):
        start = pl.multiple_of(chunk * STEP, STEP)

        def product(half):
            block = padded[pl.ds(half * HALF + start, STEP)]
            taps = [block[:, i : i + ROWS].reshape(STEP * ROWS * WIDE, CH) for i in range(3)]
            return jnp.dot(
                jnp.concatenate(taps, axis=1), weights[half], preferred_element_type=F32
            )

        load(chunk, 0).wait()
        load(chunk, 1).wait()
        first, second = product(0), product(1)
        low = low_half((STEP * ROWS * WIDE, LANES))
        left = jnp.where(low, first[:, :LANES], second[:, :LANES])
        centre = swap_halves(jnp.where(low, second[:, :LANES], first[:, :LANES]))
        right = first[:, LANES:] + second[:, LANES:]
        shape = (STEP * ROWS, WIDE, LANES)
        drives = beside(left.reshape(shape), centre.reshape(shape), right.reshape(shape))
        drives = drives.reshape(STEP, ROWS, WIDE, LANES)
        carried = state[...]
        for step in range(STEP):
            decay, gain = factors[0, start + step], factors[1, start + step]
            carried = decay * carried + gain * drives[step]
        state[...] = carried
        return carry

    lax.fori_loop(0, CHUNKS, advance, 0)

    late = functools.reduce(lambda a, b: a + b, values[HALF:])
    total = functools.reduce(lambda a, b: a + b, values[:HALF]) + late
    carried = state[...]
    end = carried + jnp.exp(-late * rate).reshape(1, 1, LANES) * swap_halves(carried)
    other = swap_halves(end)
    low = low_half((ROWS // 2, WIDE, LANES))
    packed = jnp.where(low, other[: ROWS // 2], end[ROWS // 2 :]).astype(BF16)
    row = lax.broadcasted_iota(jnp.int32, (WIDE, LANES), 0)
    pieces = split3(jnp.full((WIDE, LANES), total, F32))
    extra = jnp.zeros((WIDE, LANES), F32)
    for index, piece in enumerate(pieces):
        extra = jnp.where(row == index, piece.astype(F32), extra)
    extra = extra.astype(BF16)
    for z in range(ZS):
        message[z, : ROWS // 2] = packed
        message[z, ROWS // 2] = extra


def whole(kernels, tap):
    return jnp.concatenate([kernel[tap] for kernel in kernels], axis=0)


WINDOW_STEP = 8
WINDOW_CHUNKS = FRAMES // WINDOW_STEP
TALL = 12


def window_kernel(
    place, kernel_own, kernel_one, kernel_two, kernel_three, frames,
    drives, token,
    rows, written, load_sem, store_sem,
):
    chan = place[0]
    kernels = (kernel_own, kernel_one, kernel_two, kernel_three)
    source = jnp.clip(CHANS * chan - 2, 0, 8)
    target = source - CHANS * chan + 4

    def load(chunk):
        part = pl.ds(chunk * WINDOW_STEP, WINDOW_STEP)
        return pltpu.make_async_copy(
            frames.at[part, pl.ds(source, 8)], rows.at[part, pl.ds(target, 8)], load_sem.at[chunk]
        )

    def store(chunk):
        part = pl.ds(chunk * WINDOW_STEP, WINDOW_STEP)
        return pltpu.make_async_copy(written.at[part], drives.at[part], store_sem.at[chunk])

    token[...] = jnp.zeros_like(token)
    for chunk in range(WINDOW_CHUNKS):
        load(chunk).start()
    empty = jnp.zeros((FRAMES, 2, WIDE, CH), BF16)

    @pl.when(chan == 0)
    def _():
        rows[:, 2:4] = empty

    @pl.when(chan == CHANS - 1)
    def _():
        rows[:, 8:10] = empty

    def convolve(chunk, carry):
        load(chunk).wait()
        start = pl.multiple_of(chunk * WINDOW_STEP, WINDOW_STEP)
        block = rows[pl.ds(start, WINDOW_STEP)]
        size = WINDOW_STEP * WINDOW * WIDE
        taps = [block[:, 2 + i : 2 + i + WINDOW].reshape(size, CH) for i in range(3)]
        operand = jnp.concatenate(taps, axis=1)
        shape = (WINDOW_STEP * WINDOW, WIDE, CH)
        parts = []
        for j in range(3):
            weight = jnp.concatenate([whole(kernels, 3 * i + j) for i in range(3)], axis=1)
            parts.append(
                lax.dot_general(
                    operand, weight, (((1,), (1,)), ((), ())), preferred_element_type=F32
                ).reshape(shape)
            )
        total = beside(*parts).reshape(WINDOW_STEP, WINDOW, WIDE, CH)
        for r in range(WINDOW):
            kept = total[:, r]
            if r == 0:
                kept = jnp.where(chan == 0, 0.0, kept)
            if r == WINDOW - 1:
                kept = jnp.where(chan == CHANS - 1, 0.0, kept)
            written[pl.ds(start, WINDOW_STEP), r] = kept.astype(BF16)
        store(chunk).start()
        return carry

    lax.fori_loop(0, WINDOW_CHUNKS, convolve, 0)
    for chunk in range(WINDOW_CHUNKS):
        store(chunk).wait()


def relay_kernel(place, rates_far, received, token, message, rates, small_sem):
    x, z = place[1], place[2]
    copy = pltpu.make_async_copy(rates_far, rates, small_sem)
    copy.start()
    copy.wait()
    rate = doubled(rates[...])
    total = jnp.zeros((ROWS // 2, WIDE, LANES), F32)
    before = total
    elapsed = jnp.zeros((1, LANES), F32)
    elapsed_before = elapsed
    for other in range(ZS):
        mine = z == other
        before = jnp.where(mine, total, before)
        elapsed_before = jnp.where(mine, elapsed, elapsed_before)
        spent = join3(received[other, ROWS // 2], 0)
        decay = jnp.exp(-spent * rate).reshape(1, 1, LANES)
        total = decay * total + received[other, : ROWS // 2].astype(F32)
        elapsed = elapsed + spent

    low = low_half((WIDE, LANES))
    blank = jnp.zeros((WIDE, LANES), F32)

    def rows_of(value):
        swapped = swap_halves(value)
        top = [jnp.where(low, value[r], swapped[r]) for r in range(ROWS // 2)]
        bottom = [jnp.where(low, swapped[r], value[r]) for r in range(ROWS // 2)]
        return [blank] + top + bottom + [blank]

    totals, befores = rows_of(total), rows_of(before)
    row = lax.broadcasted_iota(jnp.int32, (WIDE, LANES), 0)
    extra = blank
    pieces = split3(elapsed) + split3(elapsed_before) + split3(rate)
    for index, piece in enumerate(pieces):
        extra = jnp.where(row == index, piece.astype(F32), extra)
    extra = extra.astype(BF16)
    for chan in range(CHANS):
        for q in range(WINDOW // 2):
            here = CHANS * chan + q
            there = here + WINDOW // 2
            later = jnp.where(low, totals[here], totals[there]).astype(BF16)
            level = jnp.where(low, befores[here], befores[there]).astype(BF16)
            for to in range(XS):
                message[to * CHANS + chan, q] = jnp.where(x == to, level, later)
        for to in range(XS):
            message[to * CHANS + chan, WINDOW // 2] = extra


OUT_STEP = 8
OUT_CHUNKS = FRAMES // OUT_STEP


def readout_kernel(
    place, intervals_far, gain_far, received, drives_far,
    kernel_own, kernel_one, kernel_two, kernel_three, frames,
    result,
    intervals, skip_gain, direct, drives, states, written, factors, state,
    load_sem, drive_sem, store_sem, small_sem,
):
    small = [
        pltpu.make_async_copy(intervals_far, intervals, small_sem.at[0]),
        pltpu.make_async_copy(gain_far, skip_gain, small_sem.at[1]),
    ]
    for copy in small:
        copy.start()
    kernels = (kernel_own, kernel_one, kernel_two, kernel_three)
    chan, x = place[0], place[1]

    def load(chunk):
        part = pl.ds(chunk * OUT_STEP, OUT_STEP)
        return pltpu.make_async_copy(
            frames.at[part, pl.ds(CHANS * chan, CHANS)], direct.at[part], load_sem.at[chunk]
        )

    def arrive(chunk):
        part = pl.ds(chunk * OUT_STEP, OUT_STEP)
        return pltpu.make_async_copy(drives_far.at[part], drives.at[part], drive_sem.at[chunk])

    def store(chunk):
        part = pl.ds(chunk * OUT_STEP, OUT_STEP)
        return pltpu.make_async_copy(written.at[part], result.at[part], store_sem.at[chunk])

    for chunk in range(OUT_CHUNKS):
        arrive(chunk).start()
        load(chunk).start()

    low = low_half((WIDE, LANES))
    rates, entering = [], []
    for step in range(CHANS):
        source = lax.rem(chan + CHANS - step, CHANS)
        level = received[x * CHANS + source]
        rate = join3(level[WINDOW // 2], 6)
        spent = join3(level[WINDOW // 2], 3)
        total = jnp.zeros((WINDOW // 2, WIDE, LANES), F32)
        for other in range(XS - 1):
            earlier = received[other * CHANS + source]
            decay = jnp.exp(-join3(earlier[WINDOW // 2], 0) * rate).reshape(1, 1, LANES)
            added = decay * total + earlier[: WINDOW // 2].astype(F32)
            total = jnp.where(other < x, added, total)
        decay = jnp.exp(-spent * rate).reshape(1, 1, LANES)
        total = level[: WINDOW // 2].astype(F32) + decay * total
        swapped = swap_halves(total)
        rates.append(rate)
        entering.append(
            [jnp.where(low, total[r], swapped[r]) for r in range(WINDOW // 2)]
            + [jnp.where(low, swapped[r], total[r]) for r in range(WINDOW // 2)]
        )

    for copy in small:
        copy.wait()
    values = [intervals[t] for t in range(FRAMES)]
    low_row = low_half((1, LANES))
    for pair in range(2):
        rate = jnp.where(low_row, rates[2 * pair], rates[2 * pair + 1])
        part = slice(LANES * pair, LANES * (pair + 1))
        for half in range(2):
            some = values[HALF * half : HALF * (half + 1)]
            scaled = table(some, some) * rate
            rest = pl.ds(HALF * half, HALF)
            spread(factors.at[:, rest], 0, part, jnp.exp(-scaled))
            spread(factors.at[:, rest], 1, part, jnp.sqrt(one_minus_exp(2.0 * scaled)))
        for r in range(WINDOW):
            state[r, :, part] = jnp.where(low, entering[2 * pair][r], entering[2 * pair + 1][r])

    def convolve(chunk, carry):
        start = pl.multiple_of(chunk * OUT_STEP, OUT_STEP)
        arrive(chunk).wait()
        carried = state[...]
        for step in range(OUT_STEP):
            decay, gain = factors[0, start + step], factors[1, start + step]
            carried = decay * carried + gain * drives[start + step].astype(F32)
            states[start + step] = carried.astype(BF16)
        state[...] = carried
        size = OUT_STEP * CHANS * WIDE
        block = states[pl.ds(start, OUT_STEP)]
        taps = [block[:, i : i + CHANS].reshape(size, CH) for i in range(3)]
        operand = jnp.concatenate(taps, axis=1)
        shape = (OUT_STEP * CHANS, WIDE, CH)
        parts = []
        for j in range(3):
            weight = jnp.concatenate([whole(kernels, 3 * i + j) for i in range(3)], axis=0)
            parts.append(jnp.dot(operand, weight, preferred_element_type=F32).reshape(shape))
        load(chunk).wait()
        passed = direct[pl.ds(start, OUT_STEP)].astype(F32).reshape(shape)
        total = beside(*parts) + skip_gain[...].reshape(1, 1, CH) * passed
        written[pl.ds(start, OUT_STEP)] = total.astype(BF16).reshape(OUT_STEP, CHANS, WIDE, CH)
        store(chunk).start()
        return carry

    lax.fori_loop(0, OUT_CHUNKS, convolve, 0)
    for chunk in range(OUT_CHUNKS):
        store(chunk).wait()


def in_vmem():
    return pl.BlockSpec(memory_space=pltpu.VMEM)


def in_smem():
    return pl.BlockSpec(memory_space=pltpu.SMEM)


def anywhere():
    return pl.BlockSpec(memory_space=pl.ANY)


def cost(microseconds):
    return pl.CostEstimate(
        flops=int(microseconds * 1.1e9), bytes_accessed=1 << 20, transcendentals=0
    )


def drive(intervals, rates, kernel_t, frames):
    return pl.pallas_call(
        drive_kernel,
        out_shape=jax.ShapeDtypeStruct((ZS, ROWS // 2 + 1, WIDE, LANES), BF16),
        in_specs=[anywhere()] * 4,
        out_specs=in_vmem(),
        scratch_shapes=[
            pltpu.SMEM((FRAMES,), F32),
            pltpu.VMEM((1, OWN), F32),
            pltpu.VMEM((9, OWN, CH), BF16),
            pltpu.VMEM((FRAMES, ROWS + 2, WIDE, CH), BF16),
            pltpu.VMEM((2, 3 * CH, CH), BF16),
            pltpu.VMEM((2, HALF, WIDE, LANES), F32),
            pltpu.VMEM((ROWS, WIDE, LANES), F32),
            pltpu.SemaphoreType.DMA((CHUNKS, 2)),
            pltpu.SemaphoreType.DMA((3,)),
        ],
        compiler_params=pltpu.CompilerParams(vmem_limit_bytes=60 << 20),
        cost_estimate=cost(8),
        name="drive",
    )(intervals, rates, kernel_t, frames)


def hold_kernel(value, one, two, three, result, sem):
    copy = pltpu.make_async_copy(value, result, sem)
    copy.start()
    copy.wait()


def hold(value, others):
    return pl.pallas_call(
        hold_kernel,
        out_shape=jax.ShapeDtypeStruct(value.shape, value.dtype),
        in_specs=[anywhere()] * (1 + len(others)),
        out_specs=anywhere(),
        scratch_shapes=[pltpu.SemaphoreType.DMA],
        compiler_params=pltpu.CompilerParams(vmem_limit_bytes=16 << 20),
        cost_estimate=cost(1),
        name="hold",
    )(value, *others)


def window(place, kernels, frames):
    return pl.pallas_call(
        window_kernel,
        out_shape=[
            jax.ShapeDtypeStruct((FRAMES, WINDOW, WIDE, CH), BF16),
            jax.ShapeDtypeStruct((8, LANES), F32),
        ],
        in_specs=[in_smem()] + [in_vmem()] * CHANS + [anywhere()],
        out_specs=[anywhere(), in_vmem()],
        scratch_shapes=[
            pltpu.VMEM((FRAMES, TALL, WIDE, CH), BF16),
            pltpu.VMEM((FRAMES, WINDOW, WIDE, CH), BF16),
            pltpu.SemaphoreType.DMA((WINDOW_CHUNKS,)),
            pltpu.SemaphoreType.DMA((WINDOW_CHUNKS,)),
        ],
        compiler_params=pltpu.CompilerParams(vmem_limit_bytes=52 << 20),
        cost_estimate=cost(6),
        name="window",
    )(place, *kernels, frames)


def relay(place, rates, received, token):
    return pl.pallas_call(
        relay_kernel,
        out_shape=jax.ShapeDtypeStruct((XS * CHANS, WINDOW // 2 + 1, WIDE, LANES), BF16),
        in_specs=[in_smem(), anywhere(), in_vmem(), anywhere()],
        out_specs=in_vmem(),
        scratch_shapes=[pltpu.VMEM((1, OWN), F32), pltpu.SemaphoreType.DMA],
        compiler_params=pltpu.CompilerParams(vmem_limit_bytes=16 << 20),
        cost_estimate=cost(1),
        name="relay",
    )(place, rates, received, token)


def read_out(place, intervals, skip_gain, received, drives, kernels, frames):
    return pl.pallas_call(
        readout_kernel,
        out_shape=jax.ShapeDtypeStruct((FRAMES, CHANS, WIDE, CH), BF16),
        in_specs=[in_smem(), anywhere(), anywhere(), in_vmem(), anywhere()]
        + [in_vmem()] * CHANS
        + [anywhere()],
        out_specs=anywhere(),
        scratch_shapes=[
            pltpu.SMEM((FRAMES,), F32),
            pltpu.VMEM((1, CH), F32),
            pltpu.VMEM((FRAMES, CHANS, WIDE, CH), BF16),
            pltpu.VMEM((FRAMES, WINDOW, WIDE, CH), BF16),
            pltpu.VMEM((FRAMES, WINDOW, WIDE, CH), BF16),
            pltpu.VMEM((FRAMES, CHANS, WIDE, CH), BF16),
            pltpu.VMEM((2, FRAMES, WIDE, CH), F32),
            pltpu.VMEM((WINDOW, WIDE, CH), F32),
            pltpu.SemaphoreType.DMA((OUT_CHUNKS,)),
            pltpu.SemaphoreType.DMA((OUT_CHUNKS,)),
            pltpu.SemaphoreType.DMA((OUT_CHUNKS,)),
            pltpu.SemaphoreType.DMA((2,)),
        ],
        compiler_params=pltpu.CompilerParams(vmem_limit_bytes=52 << 20),
        cost_estimate=cost(6),
        name="read_out",
    )(place, intervals, skip_gain, received, drives, *kernels, frames)


def around(value):
    routes = [[(c, (c + step) % CHANS) for c in range(CHANS)] for step in range(1, CHANS)]
    return [value] + [lax.ppermute(value, "chan", route) for route in routes]


def local(frames, intervals, decay_rates, in_kernel, out_kernel, skip_gain):
    place = jnp.stack([lax.axis_index(name) for name in ("chan", "x", "z")]).astype(jnp.int32)
    rates = decay_rates.reshape(1, OWN)
    kernel_t = jnp.transpose(in_kernel.reshape(9, CH, OWN), (0, 2, 1))
    in_kernels = around(kernel_t)
    message = drive(intervals, rates, kernel_t, frames)
    out_kernels = around(hold(out_kernel.reshape(9, OWN, CH), in_kernels[1:]))
    arrived = lax.all_to_all(message, "z", 0, 0)
    drives, token = window(place, in_kernels, frames)
    onward = relay(place, rates, arrived, token)
    onward = lax.all_to_all(onward, ("x", "chan"), 0, 0)
    return read_out(
        place, intervals, skip_gain.reshape(1, CH), onward, drives, out_kernels, frames
    )


def solution(mesh):
    whole = jax.sharding.Mesh(
        mesh.devices.reshape(XS, ZS, CHANS, 2), ("x", "z", "chan", "clip")
    )
    time = ("clip", "x", "z")
    placed = (
        P(time, None, None, None),
        P(time),
        P("chan"),
        P(None, None, None, "chan"),
        P(None, None, "chan", None),
        P(),
    )
    return jax.shard_map(
        local,
        mesh=whole,
        in_specs=placed,
        out_specs=P(time, "chan", None, None),
        check_vma=False,
    )
```

```python
import functools

import jax
import jax.numpy as jnp
from jax import lax
from jax.experimental import pallas as pl
from jax.experimental.pallas import tpu as pltpu
from jax.sharding import PartitionSpec as P

F32 = jnp.float32
BF16 = jnp.bfloat16
FRAMES = 32
HALF = 16
ROWS = 16
WIDE = 16
CH = 256
OWN = 64
LANES = 128
CHANS = 4
ZS = 8
XS = 4
WINDOW = 6
STEP = 4
PIECES = ((0, 4), (4, 4), (8, 4), (12, 4))
CHUNKS = len(PIECES)


def split3(value):
    high = value.astype(BF16)
    rest = value - high.astype(F32)
    middle = rest.astype(BF16)
    low = (rest - middle.astype(F32)).astype(BF16)
    return high, middle, low


def join3(block, start):
    parts = block.astype(F32)
    return parts[start : start + 1] + parts[start + 1 : start + 2] + parts[start + 2 : start + 3]


def low_half(shape):
    return lax.broadcasted_iota(jnp.int32, shape, len(shape) - 1) < OWN


def swap_halves(value):
    return pltpu.roll(value, OWN, value.ndim - 1)


def doubled(rates):
    row = jnp.concatenate([rates, rates], axis=1)
    return row


def table(low_values, high_values):
    row = lax.broadcasted_iota(jnp.int32, (HALF, LANES), 0)
    low = low_half((HALF, LANES))
    result = jnp.zeros((HALF, LANES), F32)
    for t in range(HALF):
        result = jnp.where(row == t, jnp.where(low, low_values[t], high_values[t]), result)
    return result


def spread(target, index, lanes, rows):
    for t in range(HALF):
        target[index, t, :, lanes] = jnp.broadcast_to(rows[t : t + 1], (WIDE, LANES))


def one_minus_exp(value):
    series = value * (
        1.0 - value * (0.5 - value * (1.0 / 6 - value * (1.0 / 24 - value * (1.0 / 120))))
    )
    return jnp.where(value < 0.125, series, 1.0 - jnp.exp(-value))


def beside(left, centre, right):
    column = lax.broadcasted_iota(jnp.int32, centre.shape, 1)
    total = centre + jnp.where(column == 0, 0.0, pltpu.roll(left, 1, 1))
    return total + jnp.where(column == WIDE - 1, 0.0, pltpu.roll(right, WIDE - 1, 1))


def running(values):
    sums = [values[0]]
    for value in values[1:]:
        sums.append(sums[-1] + value)
    return sums


def drive_kernel(
    intervals_far, rates_far, kernel_far, frames,
    message, token,
    intervals, rates, kernel_t, padded, weights, factors, state, load_sem, small_sem,
):
    small = [
        pltpu.make_async_copy(source, target, small_sem.at[index])
        for index, (source, target) in enumerate(
            ((kernel_far, kernel_t), (intervals_far, intervals), (rates_far, rates))
        )
    ]
    for copy in small:
        copy.start()
    token[...] = jnp.zeros_like(token)

    def load(chunk, half):
        first, size = PIECES[chunk]
        part = pl.ds(half * HALF + first, size)
        return pltpu.make_async_copy(
            frames.at[part],
            padded.at[part, pl.ds(1, ROWS)],
            load_sem.at[chunk, half],
        )

    load(0, 0).start()
    load(0, 1).start()

    empty = jnp.zeros((FRAMES, 1, WIDE, CH), BF16)
    padded[:, 0:1] = empty
    padded[:, ROWS + 1 : ROWS + 2] = empty
    nothing = jnp.zeros((CH, OWN), BF16)
    for copy in small:
        copy.wait()
    for chunk in range(1, CHUNKS):
        load(chunk, 0).start()
        load(chunk, 1).start()
    for i in range(3):
        tap = [kernel_t[3 * i + j].astype(F32).T.astype(BF16) for j in range(3)]
        weights[0, CH * i : CH * (i + 1), :] = jnp.concatenate([tap[0], tap[1], tap[2], nothing], 1)
        weights[1, CH * i : CH * (i + 1), :] = jnp.concatenate([tap[1], tap[0], nothing, tap[2]], 1)

    values = [intervals[t] for t in range(FRAMES)]
    rate = doubled(rates[...])
    scaled = table(values[:HALF], values[HALF:]) * rate
    spread(factors, 0, slice(None), jnp.exp(-scaled))
    spread(factors, 1, slice(None), jnp.sqrt(one_minus_exp(2.0 * scaled)))
    state[...] = jnp.zeros_like(state)

    def products(chunk):
        load(chunk, 0).wait()
        load(chunk, 1).wait()
        begin, size = PIECES[chunk]
        both = []
        for half in range(2):
            block = padded[pl.ds(half * HALF + begin, size)]
            taps = [block[:, i : i + ROWS].reshape(size * ROWS * WIDE, CH) for i in range(3)]
            both.append(
                jnp.dot(jnp.concatenate(taps, axis=1), weights[half], preferred_element_type=F32)
            )
        return both

    def advance(chunk, first, second):
        begin, size = PIECES[chunk]
        low = low_half((size * ROWS * WIDE, LANES))
        left = jnp.where(low, first[:, :LANES], second[:, :LANES])
        centre = swap_halves(jnp.where(low, second[:, :LANES], first[:, :LANES]))
        right = first[:, LANES:] + second[:, LANES:]
        shape = (size * ROWS, WIDE, LANES)
        drives = beside(left.reshape(shape), centre.reshape(shape), right.reshape(shape))
        drives = drives.reshape(size, ROWS, WIDE, LANES)
        carried = state[...]
        for step in range(size):
            now = begin + step
            carried = factors[0, now] * carried + factors[1, now] * drives[step]
        state[...] = carried

    waiting = products(0)
    for chunk in range(CHUNKS):
        ready = waiting
        if chunk + 1 < CHUNKS:
            waiting = products(chunk + 1)
        advance(chunk, *ready)

    late = functools.reduce(lambda a, b: a + b, values[HALF:])
    total = functools.reduce(lambda a, b: a + b, values[:HALF]) + late
    carried = state[...]
    end = carried + jnp.exp(-late * rate).reshape(1, 1, LANES) * swap_halves(carried)
    other = swap_halves(end)
    low = low_half((ROWS // 2, WIDE, LANES))
    packed = jnp.where(low, other[: ROWS // 2], end[ROWS // 2 :]).astype(BF16)
    row = lax.broadcasted_iota(jnp.int32, (WIDE, LANES), 0)
    pieces = split3(jnp.full((WIDE, LANES), total, F32))
    extra = jnp.zeros((WIDE, LANES), F32)
    for index, piece in enumerate(pieces):
        extra = jnp.where(row == index, piece.astype(F32), extra)
    extra = extra.astype(BF16)
    for z in range(ZS):
        message[z, : ROWS // 2] = packed
        message[z, ROWS // 2] = extra


def whole(own, pairs, use_left, tap):
    parts = [own[tap]] + [jnp.where(use_left, left[tap], right[tap]) for left, right in pairs]
    return jnp.concatenate(parts, axis=0)


WINDOW_STEP = 8
WINDOW_CHUNKS = FRAMES // WINDOW_STEP
TALL = 12


def window_kernel(
    place, kernel_own, *rest
):
    direct, swapped = rest[: CHANS - 1], rest[CHANS - 1 : 2 * CHANS - 2]
    (frames, drives, token, rows, written, load_sem, store_sem) = rest[2 * CHANS - 2 :]
    pairs = list(zip(direct, swapped))
    chan, first = place[0], place[3] == 0
    source = jnp.clip(CHANS * chan - 2, 0, 8)
    target = source - CHANS * chan + 4

    def load(chunk):
        part = pl.ds(chunk * WINDOW_STEP, WINDOW_STEP)
        return pltpu.make_async_copy(
            frames.at[part, pl.ds(source, 8)], rows.at[part, pl.ds(target, 8)], load_sem.at[chunk]
        )

    def store(chunk):
        part = pl.ds(chunk * WINDOW_STEP, WINDOW_STEP)
        return pltpu.make_async_copy(written.at[part], drives.at[part], store_sem.at[chunk])

    token[...] = jnp.zeros_like(token)
    for chunk in range(WINDOW_CHUNKS):
        load(chunk).start()
    empty = jnp.zeros((FRAMES, 2, WIDE, CH), BF16)

    @pl.when(chan == 0)
    def _():
        rows[:, 2:4] = empty

    @pl.when(chan == CHANS - 1)
    def _():
        rows[:, 8:10] = empty

    def convolve(chunk, carry):
        load(chunk).wait()
        start = pl.multiple_of(chunk * WINDOW_STEP, WINDOW_STEP)
        block = rows[pl.ds(start, WINDOW_STEP)]
        size = WINDOW_STEP * WINDOW * WIDE
        taps = [block[:, 2 + i : 2 + i + WINDOW].reshape(size, CH) for i in range(3)]
        operand = jnp.concatenate(taps, axis=1)
        shape = (WINDOW_STEP * WINDOW, WIDE, CH)
        parts = []
        for j in range(3):
            weight = jnp.concatenate([whole(kernel_own, pairs, first, 3 * i + j) for i in range(3)], axis=1)
            parts.append(
                lax.dot_general(
                    operand, weight, (((1,), (1,)), ((), ())), preferred_element_type=F32
                ).reshape(shape)
            )
        total = beside(*parts).reshape(WINDOW_STEP, WINDOW, WIDE, CH)
        for r in range(WINDOW):
            kept = total[:, r]
            if r == 0:
                kept = jnp.where(chan == 0, 0.0, kept)
            if r == WINDOW - 1:
                kept = jnp.where(chan == CHANS - 1, 0.0, kept)
            written[pl.ds(start, WINDOW_STEP), r] = kept.astype(BF16)
        store(chunk).start()
        return carry

    lax.fori_loop(0, WINDOW_CHUNKS, convolve, 0)
    for chunk in range(WINDOW_CHUNKS):
        store(chunk).wait()


def relay_kernel(place, rates, received, token, message):
    x, z = place[1], place[2]
    rate = doubled(rates[...])
    total = jnp.zeros((ROWS // 2, WIDE, LANES), F32)
    before = total
    elapsed = jnp.zeros((1, LANES), F32)
    elapsed_before = elapsed
    for other in range(ZS):
        mine = z == other
        before = jnp.where(mine, total, before)
        elapsed_before = jnp.where(mine, elapsed, elapsed_before)
        spent = join3(received[other, ROWS // 2], 0)
        decay = jnp.exp(-spent * rate).reshape(1, 1, LANES)
        total = decay * total + received[other, : ROWS // 2].astype(F32)
        elapsed = elapsed + spent

    low = low_half((WIDE, LANES))
    blank = jnp.zeros((WIDE, LANES), F32)

    def rows_of(value):
        swapped = swap_halves(value)
        top = [jnp.where(low, value[r], swapped[r]) for r in range(ROWS // 2)]
        bottom = [jnp.where(low, swapped[r], value[r]) for r in range(ROWS // 2)]
        return [blank] + top + bottom + [blank]

    totals, befores = rows_of(total), rows_of(before)
    row = lax.broadcasted_iota(jnp.int32, (WIDE, LANES), 0)
    extra = blank
    pieces = split3(elapsed) + split3(elapsed_before) + split3(rate)
    for index, piece in enumerate(pieces):
        extra = jnp.where(row == index, piece.astype(F32), extra)
    extra = extra.astype(BF16)
    for chan in range(CHANS):
        for q in range(WINDOW // 2):
            here = CHANS * chan + q
            there = here + WINDOW // 2
            later = jnp.where(low, totals[here], totals[there]).astype(BF16)
            level = jnp.where(low, befores[here], befores[there]).astype(BF16)
            for to in range(XS):
                message[to * CHANS + chan, q] = jnp.where(x == to, level, later)
        for to in range(XS):
            message[to * CHANS + chan, WINDOW // 2] = extra


OUT_STEP = 8
OUT_CHUNKS = FRAMES // OUT_STEP


def readout_kernel(
    place, intervals_far, skip_gain, received, drives_far, kernel_own, *rest
):
    pairs = list(zip(rest[: CHANS - 1], rest[CHANS - 1 : 2 * CHANS - 2]))
    (
        frames, result, intervals, direct, drives, states, written, factors, state,
        load_sem, drive_sem, store_sem, small_sem,
    ) = rest[2 * CHANS - 2 :]
    small = [pltpu.make_async_copy(intervals_far, intervals, small_sem)]
    for copy in small:
        copy.start()
    chan, x, second = place[0], place[1], place[3] == 1

    def load(chunk):
        part = pl.ds(chunk * OUT_STEP, OUT_STEP)
        return pltpu.make_async_copy(
            frames.at[part, pl.ds(CHANS * chan, CHANS)], direct.at[part], load_sem.at[chunk]
        )

    def arrive(chunk):
        part = pl.ds(chunk * OUT_STEP, OUT_STEP)
        return pltpu.make_async_copy(drives_far.at[part], drives.at[part], drive_sem.at[chunk])

    def store(chunk):
        part = pl.ds(chunk * OUT_STEP, OUT_STEP)
        return pltpu.make_async_copy(written.at[part], result.at[part], store_sem.at[chunk])

    for chunk in range(OUT_CHUNKS):
        arrive(chunk).start()
        load(chunk).start()

    low = low_half((WIDE, LANES))
    rates, entering = [], []
    for step in range(CHANS):
        source = lax.rem(chan + CHANS - step, CHANS)
        level = received[x * CHANS + source]
        rate = join3(level[WINDOW // 2], 6)
        spent = join3(level[WINDOW // 2], 3)
        total = jnp.zeros((WINDOW // 2, WIDE, LANES), F32)
        for other in range(XS - 1):
            earlier = received[other * CHANS + source]
            decay = jnp.exp(-join3(earlier[WINDOW // 2], 0) * rate).reshape(1, 1, LANES)
            added = decay * total + earlier[: WINDOW // 2].astype(F32)
            total = jnp.where(other < x, added, total)
        decay = jnp.exp(-spent * rate).reshape(1, 1, LANES)
        total = level[: WINDOW // 2].astype(F32) + decay * total
        swapped = swap_halves(total)
        rates.append(rate)
        entering.append(
            [jnp.where(low, total[r], swapped[r]) for r in range(WINDOW // 2)]
            + [jnp.where(low, swapped[r], total[r]) for r in range(WINDOW // 2)]
        )

    for copy in small:
        copy.wait()
    values = [intervals[t] for t in range(FRAMES)]
    low_row = low_half((1, LANES))
    for pair in range(2):
        rate = jnp.where(low_row, rates[2 * pair], rates[2 * pair + 1])
        part = slice(LANES * pair, LANES * (pair + 1))
        for half in range(2):
            some = values[HALF * half : HALF * (half + 1)]
            scaled = table(some, some) * rate
            rest = pl.ds(HALF * half, HALF)
            spread(factors.at[:, rest], 0, part, jnp.exp(-scaled))
            spread(factors.at[:, rest], 1, part, jnp.sqrt(one_minus_exp(2.0 * scaled)))
        for r in range(WINDOW):
            state[r, :, part] = jnp.where(low, entering[2 * pair][r], entering[2 * pair + 1][r])

    def convolve(chunk, carry):
        start = pl.multiple_of(chunk * OUT_STEP, OUT_STEP)
        arrive(chunk).wait()
        carried = state[...]
        for step in range(OUT_STEP):
            decay, gain = factors[0, start + step], factors[1, start + step]
            carried = decay * carried + gain * drives[start + step].astype(F32)
            states[start + step] = carried.astype(BF16)
        state[...] = carried
        size = OUT_STEP * CHANS * WIDE
        block = states[pl.ds(start, OUT_STEP)]
        taps = [block[:, i : i + CHANS].reshape(size, CH) for i in range(3)]
        operand = jnp.concatenate(taps, axis=1)
        shape = (OUT_STEP * CHANS, WIDE, CH)
        parts = []
        for j in range(3):
            weight = jnp.concatenate([whole(kernel_own, pairs, second, 3 * i + j) for i in range(3)], axis=0)
            parts.append(jnp.dot(operand, weight, preferred_element_type=F32).reshape(shape))
        load(chunk).wait()
        passed = direct[pl.ds(start, OUT_STEP)].astype(F32).reshape(shape)
        total = beside(*parts) + skip_gain[...].reshape(1, 1, CH) * passed
        written[pl.ds(start, OUT_STEP)] = total.astype(BF16).reshape(OUT_STEP, CHANS, WIDE, CH)
        store(chunk).start()
        return carry

    lax.fori_loop(0, OUT_CHUNKS, convolve, 0)
    for chunk in range(OUT_CHUNKS):
        store(chunk).wait()


def in_vmem():
    return pl.BlockSpec(memory_space=pltpu.VMEM)


def in_smem():
    return pl.BlockSpec(memory_space=pltpu.SMEM)


def anywhere():
    return pl.BlockSpec(memory_space=pl.ANY)


def cost(microseconds):
    return pl.CostEstimate(
        flops=int(microseconds * 1.1e9), bytes_accessed=1 << 20, transcendentals=0
    )


def drive(intervals, rates, kernel_t, frames):
    return pl.pallas_call(
        drive_kernel,
        out_shape=[
            jax.ShapeDtypeStruct((ZS, ROWS // 2 + 1, WIDE, LANES), BF16),
            jax.ShapeDtypeStruct((8, LANES), F32),
        ],
        in_specs=[anywhere()] * 4,
        out_specs=[in_vmem()] * 2,
        scratch_shapes=[
            pltpu.SMEM((FRAMES,), F32),
            pltpu.VMEM((1, OWN), F32),
            pltpu.VMEM((9, OWN, CH), BF16),
            pltpu.VMEM((FRAMES, ROWS + 2, WIDE, CH), BF16),
            pltpu.VMEM((2, 3 * CH, CH), BF16),
            pltpu.VMEM((2, HALF, WIDE, LANES), F32),
            pltpu.VMEM((ROWS, WIDE, LANES), F32),
            pltpu.SemaphoreType.DMA((CHUNKS, 2)),
            pltpu.SemaphoreType.DMA((3,)),
        ],
        compiler_params=pltpu.CompilerParams(vmem_limit_bytes=60 << 20),
        cost_estimate=cost(8),
        name="drive",
    )(intervals, rates, kernel_t, frames)


def hold_kernel(*refs):
    del refs


def hold(values, other):
    return pl.pallas_call(
        hold_kernel,
        out_shape=[jax.ShapeDtypeStruct(value.shape, value.dtype) for value in values],
        in_specs=[anywhere()] * (len(values) + 1),
        out_specs=[anywhere()] * len(values),
        input_output_aliases={index: index for index in range(len(values))},
        compiler_params=pltpu.CompilerParams(vmem_limit_bytes=16 << 20),
        cost_estimate=cost(0),
        name="hold",
    )(*values, other)


def window(place, own, direct, swapped, frames):
    return pl.pallas_call(
        window_kernel,
        out_shape=[
            jax.ShapeDtypeStruct((FRAMES, WINDOW, WIDE, CH), BF16),
            jax.ShapeDtypeStruct((8, LANES), F32),
        ],
        in_specs=[in_smem()] + [in_vmem()] * (2 * CHANS - 1) + [anywhere()],
        out_specs=[anywhere(), in_vmem()],
        scratch_shapes=[
            pltpu.VMEM((FRAMES, TALL, WIDE, CH), BF16),
            pltpu.VMEM((FRAMES, WINDOW, WIDE, CH), BF16),
            pltpu.SemaphoreType.DMA((WINDOW_CHUNKS,)),
            pltpu.SemaphoreType.DMA((WINDOW_CHUNKS,)),
        ],
        compiler_params=pltpu.CompilerParams(vmem_limit_bytes=51 << 20),
        cost_estimate=cost(1),
        name="window",
    )(place, own, *direct, *swapped, frames)


def relay(place, rates, received, token):
    return pl.pallas_call(
        relay_kernel,
        out_shape=jax.ShapeDtypeStruct((XS * CHANS, WINDOW // 2 + 1, WIDE, LANES), BF16),
        in_specs=[in_smem(), in_vmem(), in_vmem(), anywhere()],
        out_specs=in_vmem(),
        compiler_params=pltpu.CompilerParams(vmem_limit_bytes=16 << 20),
        cost_estimate=cost(1),
        name="relay",
    )(place, rates, received, token)


def read_out(place, intervals, skip_gain, received, drives, own, direct, swapped, frames):
    return pl.pallas_call(
        readout_kernel,
        out_shape=jax.ShapeDtypeStruct((FRAMES, CHANS, WIDE, CH), BF16),
        in_specs=[in_smem(), anywhere(), in_vmem(), in_vmem(), anywhere()]
        + [in_vmem()] * (2 * CHANS - 1)
        + [anywhere()],
        out_specs=anywhere(),
        scratch_shapes=[
            pltpu.SMEM((FRAMES,), F32),
            pltpu.VMEM((FRAMES, CHANS, WIDE, CH), BF16),
            pltpu.VMEM((FRAMES, WINDOW, WIDE, CH), BF16),
            pltpu.VMEM((FRAMES, WINDOW, WIDE, CH), BF16),
            pltpu.VMEM((FRAMES, CHANS, WIDE, CH), BF16),
            pltpu.VMEM((2, FRAMES, WIDE, CH), F32),
            pltpu.VMEM((WINDOW, WIDE, CH), F32),
            pltpu.SemaphoreType.DMA((OUT_CHUNKS,)),
            pltpu.SemaphoreType.DMA((OUT_CHUNKS,)),
            pltpu.SemaphoreType.DMA((OUT_CHUNKS,)),
            pltpu.SemaphoreType.DMA,
        ],
        compiler_params=pltpu.CompilerParams(vmem_limit_bytes=52 << 20),
        cost_estimate=cost(6),
        name="read_out",
    )(place, intervals, skip_gain, received, drives, own, *direct, *swapped, frames)


def around(value):
    routes = [[(c, (c + step) % CHANS) for c in range(CHANS)] for step in range(1, CHANS)]
    return [lax.ppermute(value, "chan", route) for route in routes]


def local(frames, intervals, decay_rates, in_kernel, out_kernel, skip_gain):
    axes = ("chan", "x", "z", "clip")
    place = jnp.stack([lax.axis_index(name) for name in axes]).astype(jnp.int32)
    rates = decay_rates.reshape(1, OWN)
    kernel_t = jnp.transpose(in_kernel.reshape(9, CH, OWN), (0, 2, 1))
    out_own = out_kernel.reshape(9, OWN, CH)
    direct = around(jnp.where(lax.axis_index("clip") == 0, kernel_t, out_own))
    message, done = drive(intervals, rates, kernel_t, frames)
    direct = hold(direct, done)
    swapped = [lax.ppermute(piece, "clip", [(0, 1), (1, 0)]) for piece in direct]
    arrived = lax.all_to_all(message, "z", 0, 0)
    drives, token = window(place, kernel_t, direct, swapped, frames)
    onward = relay(place, rates, arrived, token)
    onward = lax.all_to_all(onward, ("x", "chan"), 0, 0)
    skip = skip_gain.reshape(1, CH)
    return read_out(place, intervals, skip, onward, drives, out_own, direct, swapped, frames)


def solution(mesh):
    whole = jax.sharding.Mesh(
        mesh.devices.reshape(XS, ZS, CHANS, 2), ("x", "z", "chan", "clip")
    )
    time = ("clip", "x", "z")
    placed = (
        P(time, None, None, None),
        P(time),
        P("chan"),
        P(None, None, None, "chan"),
        P(None, None, "chan", None),
        P(),
    )
    return jax.shard_map(
        local,
        mesh=whole,
        in_specs=placed,
        out_specs=P(time, "chan", None, None),
        check_vma=False,
    )
```

```python
import functools

import jax
import jax.numpy as jnp
from jax import lax
from jax.experimental import pallas as pl
from jax.experimental.pallas import tpu as pltpu
from jax.sharding import PartitionSpec as P

F32 = jnp.float32
BF16 = jnp.bfloat16
FRAMES = 32
HALF = 16
ROWS = 16
WIDE = 16
CH = 256
OWN = 64
LANES = 128
CHANS = 4
ZS = 8
XS = 4
WINDOW = 6
STEP = 4
PIECES = ((0, 4), (4, 4), (8, 4), (12, 4))
CHUNKS = len(PIECES)


def split3(value):
    high = value.astype(BF16)
    rest = value - high.astype(F32)
    middle = rest.astype(BF16)
    low = (rest - middle.astype(F32)).astype(BF16)
    return high, middle, low


def join3(block, start):
    parts = block.astype(F32)
    return parts[start : start + 1] + parts[start + 1 : start + 2] + parts[start + 2 : start + 3]


def low_half(shape):
    return lax.broadcasted_iota(jnp.int32, shape, len(shape) - 1) < OWN


def swap_halves(value):
    return pltpu.roll(value, OWN, value.ndim - 1)


def doubled(rates):
    row = jnp.concatenate([rates, rates], axis=1)
    return row


def table(low_values, high_values):
    row = lax.broadcasted_iota(jnp.int32, (HALF, LANES), 0)
    low = low_half((HALF, LANES))
    result = jnp.zeros((HALF, LANES), F32)
    for t in range(HALF):
        result = jnp.where(row == t, jnp.where(low, low_values[t], high_values[t]), result)
    return result


def spread(target, index, lanes, rows):
    for t in range(HALF):
        target[index, t, :, lanes] = jnp.broadcast_to(rows[t : t + 1], (WIDE, LANES))


def one_minus_exp(value):
    series = value * (
        1.0 - value * (0.5 - value * (1.0 / 6 - value * (1.0 / 24 - value * (1.0 / 120))))
    )
    return jnp.where(value < 0.125, series, 1.0 - jnp.exp(-value))


def beside(left, centre, right):
    column = lax.broadcasted_iota(jnp.int32, centre.shape, 1)
    total = centre + jnp.where(column == 0, 0.0, pltpu.roll(left, 1, 1))
    return total + jnp.where(column == WIDE - 1, 0.0, pltpu.roll(right, WIDE - 1, 1))


def running(values):
    sums = [values[0]]
    for value in values[1:]:
        sums.append(sums[-1] + value)
    return sums


def drive_kernel(
    intervals_far, rates_far, kernel_far, frames,
    message,
    intervals, rates, kernel_t, padded, weights, factors, state, load_sem, small_sem,
):
    small = [
        pltpu.make_async_copy(source, target, small_sem.at[index])
        for index, (source, target) in enumerate(
            ((kernel_far, kernel_t), (intervals_far, intervals), (rates_far, rates))
        )
    ]
    for copy in small:
        copy.start()

    def load(chunk, half):
        first, size = PIECES[chunk]
        part = pl.ds(half * HALF + first, size)
        return pltpu.make_async_copy(
            frames.at[part],
            padded.at[part, pl.ds(1, ROWS)],
            load_sem.at[chunk, half],
        )

    load(0, 0).start()
    load(0, 1).start()

    empty = jnp.zeros((FRAMES, 1, WIDE, CH), BF16)
    padded[:, 0:1] = empty
    padded[:, ROWS + 1 : ROWS + 2] = empty
    nothing = jnp.zeros((CH, OWN), BF16)
    for copy in small:
        copy.wait()
    for chunk in range(1, CHUNKS):
        load(chunk, 0).start()
        load(chunk, 1).start()
    for i in range(3):
        tap = [kernel_t[3 * i + j].astype(F32).T.astype(BF16) for j in range(3)]
        weights[0, CH * i : CH * (i + 1), :] = jnp.concatenate([tap[0], tap[1], tap[2], nothing], 1)
        weights[1, CH * i : CH * (i + 1), :] = jnp.concatenate([tap[1], tap[0], nothing, tap[2]], 1)

    values = [intervals[t] for t in range(FRAMES)]
    rate = doubled(rates[...])
    scaled = table(values[:HALF], values[HALF:]) * rate
    spread(factors, 0, slice(None), jnp.exp(-scaled))
    spread(factors, 1, slice(None), jnp.sqrt(one_minus_exp(2.0 * scaled)))
    state[...] = jnp.zeros_like(state)

    def products(chunk):
        load(chunk, 0).wait()
        load(chunk, 1).wait()
        begin, size = PIECES[chunk]
        both = []
        for half in range(2):
            block = padded[pl.ds(half * HALF + begin, size)]
            taps = [block[:, i : i + ROWS].reshape(size * ROWS * WIDE, CH) for i in range(3)]
            both.append(
                jnp.dot(jnp.concatenate(taps, axis=1), weights[half], preferred_element_type=F32)
            )
        return both

    def advance(chunk, first, second):
        begin, size = PIECES[chunk]
        low = low_half((size * ROWS * WIDE, LANES))
        left = jnp.where(low, first[:, :LANES], second[:, :LANES])
        centre = swap_halves(jnp.where(low, second[:, :LANES], first[:, :LANES]))
        right = first[:, LANES:] + second[:, LANES:]
        shape = (size * ROWS, WIDE, LANES)
        drives = beside(left.reshape(shape), centre.reshape(shape), right.reshape(shape))
        drives = drives.reshape(size, ROWS, WIDE, LANES)
        carried = state[...]
        for step in range(size):
            now = begin + step
            carried = factors[0, now] * carried + factors[1, now] * drives[step]
        state[...] = carried

    waiting = products(0)
    for chunk in range(CHUNKS):
        ready = waiting
        if chunk + 1 < CHUNKS:
            waiting = products(chunk + 1)
        advance(chunk, *ready)

    late = functools.reduce(lambda a, b: a + b, values[HALF:])
    total = functools.reduce(lambda a, b: a + b, values[:HALF]) + late
    carried = state[...]
    end = carried + jnp.exp(-late * rate).reshape(1, 1, LANES) * swap_halves(carried)
    other = swap_halves(end)
    low = low_half((ROWS // 2, WIDE, LANES))
    packed = jnp.where(low, other[: ROWS // 2], end[ROWS // 2 :]).astype(BF16)
    row = lax.broadcasted_iota(jnp.int32, (WIDE, LANES), 0)
    pieces = split3(jnp.full((WIDE, LANES), total, F32))
    extra = jnp.zeros((WIDE, LANES), F32)
    for index, piece in enumerate(pieces):
        extra = jnp.where(row == index, piece.astype(F32), extra)
    extra = extra.astype(BF16)
    for z in range(ZS):
        message[z, : ROWS // 2] = packed
        message[z, ROWS // 2] = extra


WINDOW_STEP = 8
WINDOW_CHUNKS = HALF // WINDOW_STEP
TALL = 12


def assemble(target, own, pairs, use_left):
    def tap(index, carry):
        parts = [own[index]]
        parts += [jnp.where(use_left, left[index], right[index]) for left, right in pairs]
        target[index] = jnp.concatenate(parts, axis=0)
        return carry

    lax.fori_loop(0, 9, tap, 0)


def window_kernel(half, place, own, *rest):
    others = CHANS - 1
    pairs = list(zip(rest[:others], rest[others : 2 * others]))
    frames, out_own, _, drives, result = rest[2 * others : 2 * others + 5]
    weights, rows, written, load_sem, store_sem = rest[2 * others + 5 :]
    chan, first = place[0], place[3] == 0
    source = jnp.clip(CHANS * chan - 2, 0, 8)
    target = source - CHANS * chan + 4

    def load(chunk):
        part = pl.ds(chunk * WINDOW_STEP, WINDOW_STEP)
        where = pl.ds(half * HALF + chunk * WINDOW_STEP, WINDOW_STEP)
        return pltpu.make_async_copy(
            frames.at[where, pl.ds(source, 8)], rows.at[part, pl.ds(target, 8)], load_sem.at[chunk]
        )

    def store(chunk):
        part = pl.ds(chunk * WINDOW_STEP, WINDOW_STEP)
        return pltpu.make_async_copy(written.at[part], drives.at[part], store_sem.at[chunk])

    for chunk in range(WINDOW_CHUNKS):
        load(chunk).start()
    empty = jnp.zeros((HALF, 2, WIDE, CH), BF16)

    @pl.when(chan == 0)
    def _():
        rows[:, 2:4] = empty

    @pl.when(chan == CHANS - 1)
    def _():
        rows[:, 8:10] = empty

    assemble(weights, own, pairs, first)
    if half == 0:
        result[...] = jnp.zeros_like(result)
    else:
        assemble(result, out_own, pairs, jnp.logical_not(first))

    def convolve(chunk, carry):
        load(chunk).wait()
        start = pl.multiple_of(chunk * WINDOW_STEP, WINDOW_STEP)
        block = rows[pl.ds(start, WINDOW_STEP)]
        size = WINDOW_STEP * WINDOW * WIDE
        taps = [block[:, 2 + i : 2 + i + WINDOW].reshape(size, CH) for i in range(3)]
        operand = jnp.concatenate(taps, axis=1)
        shape = (WINDOW_STEP * WINDOW, WIDE, CH)
        dims = (((1,), (1,)), ((), ()))
        parts = []
        for j in range(3):
            weight = jnp.concatenate([weights[3 * i + j] for i in range(3)], axis=1)
            parts.append(
                lax.dot_general(operand, weight, dims, preferred_element_type=F32).reshape(shape)
            )
        total = beside(*parts).reshape(WINDOW_STEP, WINDOW, WIDE, CH)
        for r in range(WINDOW):
            kept = total[:, r]
            if r == 0:
                kept = jnp.where(chan == 0, 0.0, kept)
            if r == WINDOW - 1:
                kept = jnp.where(chan == CHANS - 1, 0.0, kept)
            written[pl.ds(start, WINDOW_STEP), r] = kept.astype(BF16)
        store(chunk).start()
        return carry

    lax.fori_loop(0, WINDOW_CHUNKS, convolve, 0)
    for chunk in range(WINDOW_CHUNKS):
        store(chunk).wait()


def relay_kernel(place, rates, received, token, message, done):
    x, z = place[1], place[2]
    done[...] = jnp.zeros_like(done)
    rate = doubled(rates[...])
    total = jnp.zeros((ROWS // 2, WIDE, LANES), F32)
    before = total
    elapsed = jnp.zeros((1, LANES), F32)
    elapsed_before = elapsed
    for other in range(ZS):
        mine = z == other
        before = jnp.where(mine, total, before)
        elapsed_before = jnp.where(mine, elapsed, elapsed_before)
        spent = join3(received[other, ROWS // 2], 0)
        decay = jnp.exp(-spent * rate).reshape(1, 1, LANES)
        total = decay * total + received[other, : ROWS // 2].astype(F32)
        elapsed = elapsed + spent

    low = low_half((WIDE, LANES))
    blank = jnp.zeros((WIDE, LANES), F32)

    def rows_of(value):
        swapped = swap_halves(value)
        top = [jnp.where(low, value[r], swapped[r]) for r in range(ROWS // 2)]
        bottom = [jnp.where(low, swapped[r], value[r]) for r in range(ROWS // 2)]
        return [blank] + top + bottom + [blank]

    totals, befores = rows_of(total), rows_of(before)
    row = lax.broadcasted_iota(jnp.int32, (WIDE, LANES), 0)
    extra = blank
    pieces = split3(elapsed) + split3(elapsed_before) + split3(rate)
    for index, piece in enumerate(pieces):
        extra = jnp.where(row == index, piece.astype(F32), extra)
    extra = extra.astype(BF16)
    for chan in range(CHANS):
        for q in range(WINDOW // 2):
            here = CHANS * chan + q
            there = here + WINDOW // 2
            later = jnp.where(low, totals[here], totals[there]).astype(BF16)
            level = jnp.where(low, befores[here], befores[there]).astype(BF16)
            for to in range(XS):
                message[to * CHANS + chan, q] = jnp.where(x == to, level, later)
        for to in range(XS):
            message[to * CHANS + chan, WINDOW // 2] = extra


OUT_STEP = 8
OUT_CHUNKS = FRAMES // OUT_STEP


def readout_kernel(
    place, intervals_far, skip_gain, received, early_drives, late_drives, weights, frames,
    result,
    intervals, direct, drives, states, written, factors, state,
    load_sem, drive_sem, store_sem, small_sem,
):
    small = [pltpu.make_async_copy(intervals_far, intervals, small_sem)]
    for copy in small:
        copy.start()
    chan, x = place[0], place[1]

    def load(chunk):
        part = pl.ds(chunk * OUT_STEP, OUT_STEP)
        return pltpu.make_async_copy(
            frames.at[part, pl.ds(CHANS * chan, CHANS)], direct.at[part], load_sem.at[chunk]
        )

    def arrive(chunk, source=early_drives):
        part = pl.ds(chunk * OUT_STEP, OUT_STEP)
        where = pl.ds(chunk % (HALF // OUT_STEP) * OUT_STEP, OUT_STEP)
        return pltpu.make_async_copy(source.at[where], drives.at[part], drive_sem.at[chunk])

    def store(chunk):
        part = pl.ds(chunk * OUT_STEP, OUT_STEP)
        return pltpu.make_async_copy(written.at[part], result.at[part], store_sem.at[chunk])

    for chunk in range(OUT_CHUNKS):
        arrive(chunk, late_drives if chunk * OUT_STEP >= HALF else early_drives).start()
        load(chunk).start()

    low = low_half((WIDE, LANES))
    rates, entering = [], []
    for step in range(CHANS):
        source = lax.rem(chan + CHANS - step, CHANS)
        level = received[x * CHANS + source]
        rate = join3(level[WINDOW // 2], 6)
        spent = join3(level[WINDOW // 2], 3)
        total = jnp.zeros((WINDOW // 2, WIDE, LANES), F32)
        for other in range(XS - 1):
            earlier = received[other * CHANS + source]
            decay = jnp.exp(-join3(earlier[WINDOW // 2], 0) * rate).reshape(1, 1, LANES)
            added = decay * total + earlier[: WINDOW // 2].astype(F32)
            total = jnp.where(other < x, added, total)
        decay = jnp.exp(-spent * rate).reshape(1, 1, LANES)
        total = level[: WINDOW // 2].astype(F32) + decay * total
        swapped = swap_halves(total)
        rates.append(rate)
        entering.append(
            [jnp.where(low, total[r], swapped[r]) for r in range(WINDOW // 2)]
            + [jnp.where(low, swapped[r], total[r]) for r in range(WINDOW // 2)]
        )

    for copy in small:
        copy.wait()
    values = [intervals[t] for t in range(FRAMES)]
    low_row = low_half((1, LANES))
    for pair in range(2):
        rate = jnp.where(low_row, rates[2 * pair], rates[2 * pair + 1])
        part = slice(LANES * pair, LANES * (pair + 1))
        for half in range(2):
            some = values[HALF * half : HALF * (half + 1)]
            scaled = table(some, some) * rate
            rest = pl.ds(HALF * half, HALF)
            spread(factors.at[:, rest], 0, part, jnp.exp(-scaled))
            spread(factors.at[:, rest], 1, part, jnp.sqrt(one_minus_exp(2.0 * scaled)))
        for r in range(WINDOW):
            state[r, :, part] = jnp.where(low, entering[2 * pair][r], entering[2 * pair + 1][r])

    def convolve(chunk, carry):
        start = pl.multiple_of(chunk * OUT_STEP, OUT_STEP)
        arrive(chunk).wait()
        carried = state[...]
        for step in range(OUT_STEP):
            decay, gain = factors[0, start + step], factors[1, start + step]
            carried = decay * carried + gain * drives[start + step].astype(F32)
            states[start + step] = carried.astype(BF16)
        state[...] = carried
        size = OUT_STEP * CHANS * WIDE
        block = states[pl.ds(start, OUT_STEP)]
        taps = [block[:, i : i + CHANS].reshape(size, CH) for i in range(3)]
        operand = jnp.concatenate(taps, axis=1)
        shape = (OUT_STEP * CHANS, WIDE, CH)
        parts = []
        for j in range(3):
            weight = jnp.concatenate([weights[3 * i + j] for i in range(3)], axis=0)
            parts.append(jnp.dot(operand, weight, preferred_element_type=F32).reshape(shape))
        load(chunk).wait()
        passed = direct[pl.ds(start, OUT_STEP)].astype(F32).reshape(shape)
        total = beside(*parts) + skip_gain[...].reshape(1, 1, CH) * passed
        written[pl.ds(start, OUT_STEP)] = total.astype(BF16).reshape(OUT_STEP, CHANS, WIDE, CH)
        store(chunk).start()
        return carry

    lax.fori_loop(0, OUT_CHUNKS, convolve, 0)
    for chunk in range(OUT_CHUNKS):
        store(chunk).wait()


def in_vmem():
    return pl.BlockSpec(memory_space=pltpu.VMEM)


def in_smem():
    return pl.BlockSpec(memory_space=pltpu.SMEM)


def anywhere():
    return pl.BlockSpec(memory_space=pl.ANY)


def cost(microseconds):
    return pl.CostEstimate(
        flops=int(microseconds * 1.1e9), bytes_accessed=1 << 20, transcendentals=0
    )


def drive(intervals, rates, kernel_t, frames):
    return pl.pallas_call(
        drive_kernel,
        out_shape=jax.ShapeDtypeStruct((ZS, ROWS // 2 + 1, WIDE, LANES), BF16),
        in_specs=[anywhere()] * 4,
        out_specs=in_vmem(),
        scratch_shapes=[
            pltpu.SMEM((FRAMES,), F32),
            pltpu.VMEM((1, OWN), F32),
            pltpu.VMEM((9, OWN, CH), BF16),
            pltpu.VMEM((FRAMES, ROWS + 2, WIDE, CH), BF16),
            pltpu.VMEM((2, 3 * CH, CH), BF16),
            pltpu.VMEM((2, HALF, WIDE, LANES), F32),
            pltpu.VMEM((ROWS, WIDE, LANES), F32),
            pltpu.SemaphoreType.DMA((CHUNKS, 2)),
            pltpu.SemaphoreType.DMA((3,)),
        ],
        compiler_params=pltpu.CompilerParams(vmem_limit_bytes=60 << 20),
        cost_estimate=cost(8),
        name="drive",
    )(intervals, rates, kernel_t, frames)


def window(half, place, own, direct, swapped, frames, out_own, after):
    token = jax.ShapeDtypeStruct((8, LANES), F32)
    laid = jax.ShapeDtypeStruct((9, CHANS * OWN, CH), BF16)
    return pl.pallas_call(
        functools.partial(window_kernel, half),
        out_shape=[
            jax.ShapeDtypeStruct((HALF, WINDOW, WIDE, CH), BF16),
            token if half == 0 else laid,
        ],
        in_specs=[in_smem()]
        + [in_vmem()] * (2 * CHANS - 1)
        + [anywhere(), anywhere() if half == 0 else in_vmem(), anywhere()],
        out_specs=[anywhere(), in_vmem()],
        scratch_shapes=[
            pltpu.VMEM((9, CHANS * OWN, CH), BF16),
            pltpu.VMEM((HALF, TALL, WIDE, CH), BF16),
            pltpu.VMEM((HALF, WINDOW, WIDE, CH), BF16),
            pltpu.SemaphoreType.DMA((WINDOW_CHUNKS,)),
            pltpu.SemaphoreType.DMA((WINDOW_CHUNKS,)),
        ],
        compiler_params=pltpu.CompilerParams(vmem_limit_bytes=51 << 20),
        cost_estimate=cost(1 if half == 0 else 3),
        name="window",
    )(place, own, *direct, *swapped, frames, out_own, after)


def relay(place, rates, received, token):
    return pl.pallas_call(
        relay_kernel,
        out_shape=[
            jax.ShapeDtypeStruct((XS * CHANS, WINDOW // 2 + 1, WIDE, LANES), BF16),
            jax.ShapeDtypeStruct((8, LANES), F32),
        ],
        in_specs=[in_smem(), in_vmem(), in_vmem(), anywhere()],
        out_specs=[in_vmem()] * 2,
        compiler_params=pltpu.CompilerParams(vmem_limit_bytes=16 << 20),
        cost_estimate=cost(1),
        name="relay",
    )(place, rates, received, token)


def read_out(place, intervals, skip_gain, received, early, late, weights, frames):
    return pl.pallas_call(
        readout_kernel,
        out_shape=jax.ShapeDtypeStruct((FRAMES, CHANS, WIDE, CH), BF16),
        in_specs=[in_smem(), anywhere(), in_vmem(), in_vmem(), anywhere(), anywhere()]
        + [in_vmem(), anywhere()],
        out_specs=anywhere(),
        scratch_shapes=[
            pltpu.SMEM((FRAMES,), F32),
            pltpu.VMEM((FRAMES, CHANS, WIDE, CH), BF16),
            pltpu.VMEM((FRAMES, WINDOW, WIDE, CH), BF16),
            pltpu.VMEM((FRAMES, WINDOW, WIDE, CH), BF16),
            pltpu.VMEM((FRAMES, CHANS, WIDE, CH), BF16),
            pltpu.VMEM((2, FRAMES, WIDE, CH), F32),
            pltpu.VMEM((WINDOW, WIDE, CH), F32),
            pltpu.SemaphoreType.DMA((OUT_CHUNKS,)),
            pltpu.SemaphoreType.DMA((OUT_CHUNKS,)),
            pltpu.SemaphoreType.DMA((OUT_CHUNKS,)),
            pltpu.SemaphoreType.DMA,
        ],
        compiler_params=pltpu.CompilerParams(vmem_limit_bytes=53 << 20),
        cost_estimate=cost(6),
        name="read_out",
    )(place, intervals, skip_gain, received, early, late, weights, frames)


def around(value):
    routes = [[(c, (c + step) % CHANS) for c in range(CHANS)] for step in range(1, CHANS)]
    return [lax.ppermute(value, "chan", route) for route in routes]


def local(frames, intervals, decay_rates, in_kernel, out_kernel, skip_gain):
    axes = ("chan", "x", "z", "clip")
    place = jnp.stack([lax.axis_index(name) for name in axes]).astype(jnp.int32)
    rates = decay_rates.reshape(1, OWN)
    kernel_t = jnp.transpose(in_kernel.reshape(9, CH, OWN), (0, 2, 1))
    out_own = out_kernel.reshape(9, OWN, CH)
    direct = around(jnp.where(lax.axis_index("clip") == 0, kernel_t, out_own))
    message = drive(intervals, rates, kernel_t, frames)
    swapped = [lax.ppermute(piece, "clip", [(0, 1), (1, 0)]) for piece in direct]
    arrived = lax.all_to_all(message, "z", 0, 0)
    early, done = window(0, place, kernel_t, direct, swapped, frames, out_own, place)
    onward, done = relay(place, rates, arrived, done)
    received = lax.all_to_all(onward, ("x", "chan"), 0, 0)
    late, weights = window(1, place, kernel_t, direct, swapped, frames, out_own, done)
    skip = skip_gain.reshape(1, CH)
    return read_out(place, intervals, skip, received, early, late, weights, frames)


def solution(mesh):
    whole = jax.sharding.Mesh(
        mesh.devices.reshape(XS, ZS, CHANS, 2), ("x", "z", "chan", "clip")
    )
    time = ("clip", "x", "z")
    placed = (
        P(time, None, None, None),
        P(time),
        P("chan"),
        P(None, None, None, "chan"),
        P(None, None, "chan", None),
        P(),
    )
    return jax.shard_map(
        local,
        mesh=whole,
        in_specs=placed,
        out_specs=P(time, "chan", None, None),
        check_vma=False,
    )
```

```python
import functools

import jax
import jax.numpy as jnp
from jax import lax
from jax.experimental import pallas as pl
from jax.experimental.pallas import tpu as pltpu
from jax.sharding import PartitionSpec as P

F32 = jnp.float32
BF16 = jnp.bfloat16
FRAMES = 32
HALF = 16
ROWS = 16
WIDE = 16
CH = 256
OWN = 64
LANES = 128
CHANS = 4
ZS = 8
XS = 4
WINDOW = 6
STEP = 4
PIECES = ((0, 4), (4, 4), (8, 4), (12, 4))
CHUNKS = len(PIECES)


def split3(value):
    high = value.astype(BF16)
    rest = value - high.astype(F32)
    middle = rest.astype(BF16)
    low = (rest - middle.astype(F32)).astype(BF16)
    return high, middle, low


def join3(block, start):
    parts = block.astype(F32)
    return parts[start : start + 1] + parts[start + 1 : start + 2] + parts[start + 2 : start + 3]


def low_half(shape):
    return lax.broadcasted_iota(jnp.int32, shape, len(shape) - 1) < OWN


def swap_halves(value):
    return pltpu.roll(value, OWN, value.ndim - 1)


def doubled(rates):
    row = jnp.concatenate([rates, rates], axis=1)
    return row


def table(low_values, high_values):
    row = lax.broadcasted_iota(jnp.int32, (HALF, LANES), 0)
    low = low_half((HALF, LANES))
    result = jnp.zeros((HALF, LANES), F32)
    for t in range(HALF):
        result = jnp.where(row == t, jnp.where(low, low_values[t], high_values[t]), result)
    return result


def spread(target, index, lanes, rows):
    for t in range(HALF):
        target[index, t, :, lanes] = jnp.broadcast_to(rows[t : t + 1], (WIDE, LANES))


def one_minus_exp(value):
    series = value * (
        1.0 - value * (0.5 - value * (1.0 / 6 - value * (1.0 / 24 - value * (1.0 / 120))))
    )
    return jnp.where(value < 0.125, series, 1.0 - jnp.exp(-value))


def beside(left, centre, right):
    column = lax.broadcasted_iota(jnp.int32, centre.shape, 1)
    total = centre + jnp.where(column == 0, 0.0, pltpu.roll(left, 1, 1))
    return total + jnp.where(column == WIDE - 1, 0.0, pltpu.roll(right, WIDE - 1, 1))


def running(values):
    sums = [values[0]]
    for value in values[1:]:
        sums.append(sums[-1] + value)
    return sums


def drive_kernel(
    intervals_far, rates_far, kernel_far, frames,
    message,
    intervals, rates, kernel_t, padded, weights, factors, state, load_sem, small_sem,
):
    small = [
        pltpu.make_async_copy(source, target, small_sem.at[index])
        for index, (source, target) in enumerate(
            ((kernel_far, kernel_t), (intervals_far, intervals), (rates_far, rates))
        )
    ]
    for copy in small:
        copy.start()

    def load(chunk, half):
        first, size = PIECES[chunk]
        part = pl.ds(half * HALF + first, size)
        return pltpu.make_async_copy(
            frames.at[part],
            padded.at[part, pl.ds(1, ROWS)],
            load_sem.at[chunk, half],
        )

    load(0, 0).start()
    load(0, 1).start()

    empty = jnp.zeros((FRAMES, 1, WIDE, CH), BF16)
    padded[:, 0:1] = empty
    padded[:, ROWS + 1 : ROWS + 2] = empty
    nothing = jnp.zeros((CH, OWN), BF16)
    for copy in small:
        copy.wait()
    for chunk in range(1, CHUNKS):
        load(chunk, 0).start()
        load(chunk, 1).start()
    for i in range(3):
        tap = [kernel_t[3 * i + j].astype(F32).T.astype(BF16) for j in range(3)]
        weights[0, CH * i : CH * (i + 1), :] = jnp.concatenate([tap[0], tap[1], tap[2], nothing], 1)
        weights[1, CH * i : CH * (i + 1), :] = jnp.concatenate([tap[1], tap[0], nothing, tap[2]], 1)

    values = [intervals[t] for t in range(FRAMES)]
    rate = doubled(rates[...])
    scaled = table(values[:HALF], values[HALF:]) * rate
    spread(factors, 0, slice(None), jnp.exp(-scaled))
    spread(factors, 1, slice(None), jnp.sqrt(one_minus_exp(2.0 * scaled)))
    state[...] = jnp.zeros_like(state)

    def products(chunk):
        load(chunk, 0).wait()
        load(chunk, 1).wait()
        begin, size = PIECES[chunk]
        both = []
        for half in range(2):
            block = padded[pl.ds(half * HALF + begin, size)]
            taps = [block[:, i : i + ROWS].reshape(size * ROWS * WIDE, CH) for i in range(3)]
            both.append(
                jnp.dot(jnp.concatenate(taps, axis=1), weights[half], preferred_element_type=F32)
            )
        return both

    def advance(chunk, first, second):
        begin, size = PIECES[chunk]
        low = low_half((size * ROWS * WIDE, LANES))
        left = jnp.where(low, first[:, :LANES], second[:, :LANES])
        centre = swap_halves(jnp.where(low, second[:, :LANES], first[:, :LANES]))
        right = first[:, LANES:] + second[:, LANES:]
        shape = (size * ROWS, WIDE, LANES)
        drives = beside(left.reshape(shape), centre.reshape(shape), right.reshape(shape))
        drives = drives.reshape(size, ROWS, WIDE, LANES)
        carried = state[...]
        for step in range(size):
            now = begin + step
            carried = factors[0, now] * carried + factors[1, now] * drives[step]
        state[...] = carried

    waiting = products(0)
    for chunk in range(CHUNKS):
        ready = waiting
        if chunk + 1 < CHUNKS:
            waiting = products(chunk + 1)
        advance(chunk, *ready)

    late = functools.reduce(lambda a, b: a + b, values[HALF:])
    total = functools.reduce(lambda a, b: a + b, values[:HALF]) + late
    carried = state[...]
    end = carried + jnp.exp(-late * rate).reshape(1, 1, LANES) * swap_halves(carried)
    other = swap_halves(end)
    low = low_half((ROWS // 2, WIDE, LANES))
    packed = jnp.where(low, other[: ROWS // 2], end[ROWS // 2 :]).astype(BF16)
    row = lax.broadcasted_iota(jnp.int32, (WIDE, LANES), 0)
    pieces = split3(jnp.full((WIDE, LANES), total, F32))
    extra = jnp.zeros((WIDE, LANES), F32)
    for index, piece in enumerate(pieces):
        extra = jnp.where(row == index, piece.astype(F32), extra)
    extra = extra.astype(BF16)
    for z in range(ZS):
        message[z, : ROWS // 2] = packed
        message[z, ROWS // 2] = extra


WINDOW_STEP = 8
WINDOW_CHUNKS = FRAMES // WINDOW_STEP
TALL = 12


def assemble(target, own, near, swapped, far, first):
    def tap(index, carry):
        left = jnp.where(first, near[index], swapped[index])
        right = jnp.where(first, swapped[index], near[index])
        target[index] = jnp.concatenate([own[index], left, far[index], right], axis=0)
        return carry

    lax.fori_loop(0, 9, tap, 0)


def window_kernel(
    place, own, near, swapped, far, frames,
    drives, token,
    weights, rows, written, load_sem, store_sem,
):
    chan, first = place[0], place[3] == 0
    source = jnp.clip(CHANS * chan - 2, 0, 8)
    target = source - CHANS * chan + 4

    def load(chunk):
        part = pl.ds(chunk * WINDOW_STEP, WINDOW_STEP)
        return pltpu.make_async_copy(
            frames.at[part, pl.ds(source, 8)], rows.at[part, pl.ds(target, 8)], load_sem.at[chunk]
        )

    def store(chunk):
        part = pl.ds(chunk * WINDOW_STEP, WINDOW_STEP)
        return pltpu.make_async_copy(written.at[part], drives.at[part], store_sem.at[chunk])

    for chunk in range(WINDOW_CHUNKS):
        load(chunk).start()
    empty = jnp.zeros((FRAMES, 2, WIDE, CH), BF16)

    @pl.when(chan == 0)
    def _():
        rows[:, 2:4] = empty

    @pl.when(chan == CHANS - 1)
    def _():
        rows[:, 8:10] = empty

    token[...] = jnp.zeros_like(token)
    assemble(weights, own, near, swapped, far, first)

    def convolve(chunk, carry):
        load(chunk).wait()
        start = pl.multiple_of(chunk * WINDOW_STEP, WINDOW_STEP)
        block = rows[pl.ds(start, WINDOW_STEP)]
        size = WINDOW_STEP * WINDOW * WIDE
        taps = [block[:, 2 + i : 2 + i + WINDOW].reshape(size, CH) for i in range(3)]
        operand = jnp.concatenate(taps, axis=1)
        shape = (WINDOW_STEP * WINDOW, WIDE, CH)
        dims = (((1,), (1,)), ((), ()))
        parts = []
        for j in range(3):
            weight = jnp.concatenate([weights[3 * i + j] for i in range(3)], axis=1)
            parts.append(
                lax.dot_general(operand, weight, dims, preferred_element_type=F32).reshape(shape)
            )
        total = beside(*parts).reshape(WINDOW_STEP, WINDOW, WIDE, CH)
        for r in range(WINDOW):
            kept = total[:, r]
            if r == 0:
                kept = jnp.where(chan == 0, 0.0, kept)
            if r == WINDOW - 1:
                kept = jnp.where(chan == CHANS - 1, 0.0, kept)
            written[pl.ds(start, WINDOW_STEP), r] = kept.astype(BF16)
        store(chunk).start()
        return carry

    lax.fori_loop(0, WINDOW_CHUNKS, convolve, 0)
    for chunk in range(WINDOW_CHUNKS):
        store(chunk).wait()


def relay_kernel(place, rates, received, token, message, done):
    x, z = place[1], place[2]
    done[...] = jnp.zeros_like(done)
    rate = doubled(rates[...])
    total = jnp.zeros((ROWS // 2, WIDE, LANES), F32)
    before = total
    elapsed = jnp.zeros((1, LANES), F32)
    elapsed_before = elapsed
    for other in range(ZS):
        mine = z == other
        before = jnp.where(mine, total, before)
        elapsed_before = jnp.where(mine, elapsed, elapsed_before)
        spent = join3(received[other, ROWS // 2], 0)
        decay = jnp.exp(-spent * rate).reshape(1, 1, LANES)
        total = decay * total + received[other, : ROWS // 2].astype(F32)
        elapsed = elapsed + spent

    low = low_half((WIDE, LANES))
    blank = jnp.zeros((WIDE, LANES), F32)

    def rows_of(value):
        swapped = swap_halves(value)
        top = [jnp.where(low, value[r], swapped[r]) for r in range(ROWS // 2)]
        bottom = [jnp.where(low, swapped[r], value[r]) for r in range(ROWS // 2)]
        return [blank] + top + bottom + [blank]

    totals, befores = rows_of(total), rows_of(before)
    row = lax.broadcasted_iota(jnp.int32, (WIDE, LANES), 0)
    extra = blank
    pieces = split3(elapsed) + split3(elapsed_before) + split3(rate)
    for index, piece in enumerate(pieces):
        extra = jnp.where(row == index, piece.astype(F32), extra)
    extra = extra.astype(BF16)
    for chan in range(CHANS):
        for q in range(WINDOW // 2):
            here = CHANS * chan + q
            there = here + WINDOW // 2
            later = jnp.where(low, totals[here], totals[there]).astype(BF16)
            level = jnp.where(low, befores[here], befores[there]).astype(BF16)
            for to in range(XS):
                message[to * CHANS + chan, q] = jnp.where(x == to, level, later)
        for to in range(XS):
            message[to * CHANS + chan, WINDOW // 2] = extra


OUT_STEP = 8
OUT_CHUNKS = FRAMES // OUT_STEP


def readout_kernel(
    place, intervals_far, skip_gain, received, drives_far, weights, frames,
    result,
    intervals, direct, drives, states, written, factors, state,
    load_sem, drive_sem, store_sem, small_sem,
):
    small = [pltpu.make_async_copy(intervals_far, intervals, small_sem)]
    for copy in small:
        copy.start()
    chan, x = place[0], place[1]

    def load(chunk):
        part = pl.ds(chunk * OUT_STEP, OUT_STEP)
        return pltpu.make_async_copy(
            frames.at[part, pl.ds(CHANS * chan, CHANS)], direct.at[part], load_sem.at[chunk]
        )

    def arrive(chunk):
        part = pl.ds(chunk * OUT_STEP, OUT_STEP)
        return pltpu.make_async_copy(drives_far.at[part], drives.at[part], drive_sem.at[chunk])

    def store(chunk):
        part = pl.ds(chunk * OUT_STEP, OUT_STEP)
        return pltpu.make_async_copy(written.at[part], result.at[part], store_sem.at[chunk])

    for chunk in range(OUT_CHUNKS):
        arrive(chunk).start()
        load(chunk).start()

    low = low_half((WIDE, LANES))
    rates, entering = [], []
    for step in range(CHANS):
        source = lax.rem(chan + CHANS - step, CHANS)
        level = received[x * CHANS + source]
        rate = join3(level[WINDOW // 2], 6)
        spent = join3(level[WINDOW // 2], 3)
        total = jnp.zeros((WINDOW // 2, WIDE, LANES), F32)
        for other in range(XS - 1):
            earlier = received[other * CHANS + source]
            decay = jnp.exp(-join3(earlier[WINDOW // 2], 0) * rate).reshape(1, 1, LANES)
            added = decay * total + earlier[: WINDOW // 2].astype(F32)
            total = jnp.where(other < x, added, total)
        decay = jnp.exp(-spent * rate).reshape(1, 1, LANES)
        total = level[: WINDOW // 2].astype(F32) + decay * total
        swapped = swap_halves(total)
        rates.append(rate)
        entering.append(
            [jnp.where(low, total[r], swapped[r]) for r in range(WINDOW // 2)]
            + [jnp.where(low, swapped[r], total[r]) for r in range(WINDOW // 2)]
        )

    for copy in small:
        copy.wait()
    values = [intervals[t] for t in range(FRAMES)]
    low_row = low_half((1, LANES))
    for pair in range(2):
        rate = jnp.where(low_row, rates[2 * pair], rates[2 * pair + 1])
        part = slice(LANES * pair, LANES * (pair + 1))
        for half in range(2):
            some = values[HALF * half : HALF * (half + 1)]
            scaled = table(some, some) * rate
            rest = pl.ds(HALF * half, HALF)
            spread(factors.at[:, rest], 0, part, jnp.exp(-scaled))
            spread(factors.at[:, rest], 1, part, jnp.sqrt(one_minus_exp(2.0 * scaled)))
        for r in range(WINDOW):
            state[r, :, part] = jnp.where(low, entering[2 * pair][r], entering[2 * pair + 1][r])

    def convolve(chunk, carry):
        start = pl.multiple_of(chunk * OUT_STEP, OUT_STEP)
        arrive(chunk).wait()
        carried = state[...]
        for step in range(OUT_STEP):
            decay, gain = factors[0, start + step], factors[1, start + step]
            carried = decay * carried + gain * drives[start + step].astype(F32)
            states[start + step] = carried.astype(BF16)
        state[...] = carried
        size = OUT_STEP * CHANS * WIDE
        block = states[pl.ds(start, OUT_STEP)]
        taps = [block[:, i : i + CHANS].reshape(size, CH) for i in range(3)]
        operand = jnp.concatenate(taps, axis=1)
        shape = (OUT_STEP * CHANS, WIDE, CH)
        parts = []
        for j in range(3):
            weight = jnp.concatenate([weights[3 * i + j] for i in range(3)], axis=0)
            parts.append(jnp.dot(operand, weight, preferred_element_type=F32).reshape(shape))
        load(chunk).wait()
        passed = direct[pl.ds(start, OUT_STEP)].astype(F32).reshape(shape)
        total = beside(*parts) + skip_gain[...].reshape(1, 1, CH) * passed
        written[pl.ds(start, OUT_STEP)] = total.astype(BF16).reshape(OUT_STEP, CHANS, WIDE, CH)
        store(chunk).start()
        return carry

    lax.fori_loop(0, OUT_CHUNKS, convolve, 0)
    for chunk in range(OUT_CHUNKS):
        store(chunk).wait()


def in_vmem():
    return pl.BlockSpec(memory_space=pltpu.VMEM)


def in_smem():
    return pl.BlockSpec(memory_space=pltpu.SMEM)


def anywhere():
    return pl.BlockSpec(memory_space=pl.ANY)


def cost(microseconds):
    return pl.CostEstimate(
        flops=int(microseconds * 1.1e9), bytes_accessed=1 << 20, transcendentals=0
    )


def drive(intervals, rates, kernel_t, frames):
    return pl.pallas_call(
        drive_kernel,
        out_shape=jax.ShapeDtypeStruct((ZS, ROWS // 2 + 1, WIDE, LANES), BF16),
        in_specs=[anywhere()] * 4,
        out_specs=in_vmem(),
        scratch_shapes=[
            pltpu.SMEM((FRAMES,), F32),
            pltpu.VMEM((1, OWN), F32),
            pltpu.VMEM((9, OWN, CH), BF16),
            pltpu.VMEM((FRAMES, ROWS + 2, WIDE, CH), BF16),
            pltpu.VMEM((2, 3 * CH, CH), BF16),
            pltpu.VMEM((2, HALF, WIDE, LANES), F32),
            pltpu.VMEM((ROWS, WIDE, LANES), F32),
            pltpu.SemaphoreType.DMA((CHUNKS, 2)),
            pltpu.SemaphoreType.DMA((3,)),
        ],
        compiler_params=pltpu.CompilerParams(vmem_limit_bytes=60 << 20),
        cost_estimate=cost(8),
        name="drive",
    )(intervals, rates, kernel_t, frames)


def window(place, own, near, swapped, far, frames):
    return pl.pallas_call(
        window_kernel,
        out_shape=[
            jax.ShapeDtypeStruct((FRAMES, WINDOW, WIDE, CH), BF16),
            jax.ShapeDtypeStruct((8, LANES), F32),
        ],
        in_specs=[in_smem()] + [in_vmem()] * CHANS + [anywhere()],
        out_specs=[anywhere(), in_vmem()],
        scratch_shapes=[
            pltpu.VMEM((9, CHANS * OWN, CH), BF16),
            pltpu.VMEM((FRAMES, TALL, WIDE, CH), BF16),
            pltpu.VMEM((FRAMES, WINDOW, WIDE, CH), BF16),
            pltpu.SemaphoreType.DMA((WINDOW_CHUNKS,)),
            pltpu.SemaphoreType.DMA((WINDOW_CHUNKS,)),
        ],
        compiler_params=pltpu.CompilerParams(vmem_limit_bytes=52 << 20),
        cost_estimate=cost(1),
        name="window",
    )(place, own, near, swapped, far, frames)


def lay_kernel(place, own, near, swapped, far, result):
    assemble(result, own, near, swapped, far, place[3] == 0)


def lay(place, own, near, swapped, far):
    return pl.pallas_call(
        lay_kernel,
        out_shape=jax.ShapeDtypeStruct((9, CHANS * OWN, CH), BF16),
        in_specs=[in_smem()] + [in_vmem()] * CHANS,
        out_specs=in_vmem(),
        compiler_params=pltpu.CompilerParams(vmem_limit_bytes=16 << 20),
        cost_estimate=cost(1),
        name="lay",
    )(place, own, near, swapped, far)


def hold_kernel(value, *refs):
    result, sem = refs[-2:]
    copy = pltpu.make_async_copy(value, result, sem)
    copy.start()
    copy.wait()


def hold(value, others):
    return pl.pallas_call(
        hold_kernel,
        out_shape=jax.ShapeDtypeStruct(value.shape, value.dtype),
        in_specs=[anywhere()] * (1 + len(others)),
        out_specs=anywhere(),
        scratch_shapes=[pltpu.SemaphoreType.DMA],
        compiler_params=pltpu.CompilerParams(vmem_limit_bytes=16 << 20),
        cost_estimate=cost(1),
        name="hold",
    )(value, *others)


def relay(place, rates, received, token):
    return pl.pallas_call(
        relay_kernel,
        out_shape=[
            jax.ShapeDtypeStruct((XS * CHANS, WINDOW // 2 + 1, WIDE, LANES), BF16),
            jax.ShapeDtypeStruct((8, LANES), F32),
        ],
        in_specs=[in_smem(), in_vmem(), in_vmem(), anywhere()],
        out_specs=[in_vmem()] * 2,
        compiler_params=pltpu.CompilerParams(vmem_limit_bytes=16 << 20),
        cost_estimate=cost(1),
        name="relay",
    )(place, rates, received, token)


def read_out(place, intervals, skip_gain, received, drives, weights, frames):
    return pl.pallas_call(
        readout_kernel,
        out_shape=jax.ShapeDtypeStruct((FRAMES, CHANS, WIDE, CH), BF16),
        in_specs=[in_smem(), anywhere(), in_vmem(), in_vmem(), anywhere(), in_vmem(), anywhere()],
        out_specs=anywhere(),
        scratch_shapes=[
            pltpu.SMEM((FRAMES,), F32),
            pltpu.VMEM((FRAMES, CHANS, WIDE, CH), BF16),
            pltpu.VMEM((FRAMES, WINDOW, WIDE, CH), BF16),
            pltpu.VMEM((FRAMES, WINDOW, WIDE, CH), BF16),
            pltpu.VMEM((FRAMES, CHANS, WIDE, CH), BF16),
            pltpu.VMEM((2, FRAMES, WIDE, CH), F32),
            pltpu.VMEM((WINDOW, WIDE, CH), F32),
            pltpu.SemaphoreType.DMA((OUT_CHUNKS,)),
            pltpu.SemaphoreType.DMA((OUT_CHUNKS,)),
            pltpu.SemaphoreType.DMA((OUT_CHUNKS,)),
            pltpu.SemaphoreType.DMA,
        ],
        compiler_params=pltpu.CompilerParams(vmem_limit_bytes=52 << 20),
        cost_estimate=cost(6),
        name="read_out",
    )(place, intervals, skip_gain, received, drives, weights, frames)


def around(value):
    near = [
        (2 * c + core, 2 * ((c + step) % CHANS) + core)
        for c in range(CHANS)
        for core, step in ((0, 1), (1, CHANS - 1))
    ]
    far = [(c, (c + 2) % CHANS) for c in range(CHANS)]
    return lax.ppermute(value, ("chan", "clip"), near), lax.ppermute(value, "chan", far)


def after_kernel(*refs):
    del refs


def after(value, other):
    return pl.pallas_call(
        after_kernel,
        out_shape=jax.ShapeDtypeStruct(value.shape, value.dtype),
        in_specs=[anywhere()] * 2,
        out_specs=anywhere(),
        input_output_aliases={0: 0},
        compiler_params=pltpu.CompilerParams(vmem_limit_bytes=16 << 20),
        cost_estimate=cost(0),
        name="after",
    )(value, other)


def swap(value):
    return lax.ppermute(value, "clip", [(0, 1), (1, 0)])


def local(frames, intervals, decay_rates, in_kernel, out_kernel, skip_gain):
    axes = ("chan", "x", "z", "clip")
    place = jnp.stack([lax.axis_index(name) for name in axes]).astype(jnp.int32)
    rates = decay_rates.reshape(1, OWN)
    kernel_t = jnp.transpose(in_kernel.reshape(9, CH, OWN), (0, 2, 1))
    out_own = out_kernel.reshape(9, OWN, CH)
    in_near, in_far = around(kernel_t)
    message = drive(intervals, rates, kernel_t, frames)
    arrived = lax.all_to_all(message, "z", 0, 0)
    out_near, out_far = around(hold(out_own, (in_near, in_far)))
    drives, done = window(place, kernel_t, in_near, swap(in_near), in_far, frames)
    onward, done = relay(place, rates, arrived, done)
    out_near = after(out_near, done)
    received = lax.all_to_all(onward, ("x", "chan"), 0, 0)
    weights = lay(place, out_own, out_near, swap(out_near), out_far)
    skip = skip_gain.reshape(1, CH)
    return read_out(place, intervals, skip, received, drives, weights, frames)


def solution(mesh):
    whole = jax.sharding.Mesh(
        mesh.devices.reshape(XS, ZS, CHANS, 2), ("x", "z", "chan", "clip")
    )
    time = ("clip", "x", "z")
    placed = (
        P(time, None, None, None),
        P(time),
        P("chan"),
        P(None, None, None, "chan"),
        P(None, None, "chan", None),
        P(),
    )
    return jax.shard_map(
        local,
        mesh=whole,
        in_specs=placed,
        out_specs=P(time, "chan", None, None),
        check_vma=False,
    )
```

```python
import functools

import jax
import jax.numpy as jnp
from jax import lax
from jax.experimental import pallas as pl
from jax.experimental.pallas import tpu as pltpu
from jax.sharding import PartitionSpec as P

F32 = jnp.float32
BF16 = jnp.bfloat16
FRAMES = 32
HALF = 16
ROWS = 16
WIDE = 16
CH = 256
OWN = 64
LANES = 128
CHANS = 4
ZS = 8
XS = 4
WINDOW = 6
STEP = 4
PIECES = ((0, 4), (4, 4), (8, 4), (12, 4))
CHUNKS = len(PIECES)


def split3(value):
    high = value.astype(BF16)
    rest = value - high.astype(F32)
    middle = rest.astype(BF16)
    low = (rest - middle.astype(F32)).astype(BF16)
    return high, middle, low


def join3(block, start):
    parts = block.astype(F32)
    return parts[start : start + 1] + parts[start + 1 : start + 2] + parts[start + 2 : start + 3]


def low_half(shape):
    return lax.broadcasted_iota(jnp.int32, shape, len(shape) - 1) < OWN


def swap_halves(value):
    return pltpu.roll(value, OWN, value.ndim - 1)


def doubled(rates):
    row = jnp.concatenate([rates, rates], axis=1)
    return row


def table(low_values, high_values):
    row = lax.broadcasted_iota(jnp.int32, (HALF, LANES), 0)
    low = low_half((HALF, LANES))
    result = jnp.zeros((HALF, LANES), F32)
    for t in range(HALF):
        result = jnp.where(row == t, jnp.where(low, low_values[t], high_values[t]), result)
    return result


def spread(target, index, lanes, rows):
    for t in range(HALF):
        target[index, t, :, lanes] = jnp.broadcast_to(rows[t : t + 1], (WIDE, LANES))


def one_minus_exp(value):
    series = value * (
        1.0 - value * (0.5 - value * (1.0 / 6 - value * (1.0 / 24 - value * (1.0 / 120))))
    )
    return jnp.where(value < 0.125, series, 1.0 - jnp.exp(-value))


def beside(left, centre, right):
    column = lax.broadcasted_iota(jnp.int32, centre.shape, 1)
    total = centre + jnp.where(column == 0, 0.0, pltpu.roll(left, 1, 1))
    return total + jnp.where(column == WIDE - 1, 0.0, pltpu.roll(right, WIDE - 1, 1))


def running(values):
    sums = [values[0]]
    for value in values[1:]:
        sums.append(sums[-1] + value)
    return sums


def drive_kernel(
    intervals_far, rates_far, kernel_far, frames,
    message,
    intervals, rates, kernel_t, padded, weights, factors, state, load_sem, small_sem,
):
    small = [
        pltpu.make_async_copy(source, target, small_sem.at[index])
        for index, (source, target) in enumerate(
            ((kernel_far, kernel_t), (intervals_far, intervals), (rates_far, rates))
        )
    ]
    for copy in small:
        copy.start()

    def load(chunk, half):
        first, size = PIECES[chunk]
        part = pl.ds(half * HALF + first, size)
        return pltpu.make_async_copy(
            frames.at[part],
            padded.at[part, pl.ds(1, ROWS)],
            load_sem.at[chunk, half],
        )

    load(0, 0).start()
    load(0, 1).start()

    empty = jnp.zeros((FRAMES, 1, WIDE, CH), BF16)
    padded[:, 0:1] = empty
    padded[:, ROWS + 1 : ROWS + 2] = empty
    nothing = jnp.zeros((CH, OWN), BF16)
    for copy in small:
        copy.wait()
    for chunk in range(1, CHUNKS):
        load(chunk, 0).start()
        load(chunk, 1).start()
    for i in range(3):
        tap = [kernel_t[3 * i + j].astype(F32).T.astype(BF16) for j in range(3)]
        weights[0, CH * i : CH * (i + 1), :] = jnp.concatenate([tap[0], tap[1], tap[2], nothing], 1)
        weights[1, CH * i : CH * (i + 1), :] = jnp.concatenate([tap[1], tap[0], nothing, tap[2]], 1)

    values = [intervals[t] for t in range(FRAMES)]
    rate = doubled(rates[...])
    scaled = table(values[:HALF], values[HALF:]) * rate
    spread(factors, 0, slice(None), jnp.exp(-scaled))
    spread(factors, 1, slice(None), jnp.sqrt(one_minus_exp(2.0 * scaled)))
    state[...] = jnp.zeros_like(state)

    def products(chunk):
        load(chunk, 0).wait()
        load(chunk, 1).wait()
        begin, size = PIECES[chunk]
        both = []
        for half in range(2):
            block = padded[pl.ds(half * HALF + begin, size)]
            taps = [block[:, i : i + ROWS].reshape(size * ROWS * WIDE, CH) for i in range(3)]
            both.append(
                jnp.dot(jnp.concatenate(taps, axis=1), weights[half], preferred_element_type=F32)
            )
        return both

    def advance(chunk, first, second):
        begin, size = PIECES[chunk]
        low = low_half((size * ROWS * WIDE, LANES))
        left = jnp.where(low, first[:, :LANES], second[:, :LANES])
        centre = swap_halves(jnp.where(low, second[:, :LANES], first[:, :LANES]))
        right = first[:, LANES:] + second[:, LANES:]
        shape = (size * ROWS, WIDE, LANES)
        drives = beside(left.reshape(shape), centre.reshape(shape), right.reshape(shape))
        drives = drives.reshape(size, ROWS, WIDE, LANES)
        carried = state[...]
        for step in range(size):
            now = begin + step
            carried = factors[0, now] * carried + factors[1, now] * drives[step]
        state[...] = carried

    waiting = products(0)
    for chunk in range(CHUNKS):
        ready = waiting
        if chunk + 1 < CHUNKS:
            waiting = products(chunk + 1)
        advance(chunk, *ready)

    late = functools.reduce(lambda a, b: a + b, values[HALF:])
    total = functools.reduce(lambda a, b: a + b, values[:HALF]) + late
    carried = state[...]
    end = carried + jnp.exp(-late * rate).reshape(1, 1, LANES) * swap_halves(carried)
    other = swap_halves(end)
    low = low_half((ROWS // 2, WIDE, LANES))
    packed = jnp.where(low, other[: ROWS // 2], end[ROWS // 2 :]).astype(BF16)
    row = lax.broadcasted_iota(jnp.int32, (WIDE, LANES), 0)
    pieces = split3(jnp.full((WIDE, LANES), total, F32))
    extra = jnp.zeros((WIDE, LANES), F32)
    for index, piece in enumerate(pieces):
        extra = jnp.where(row == index, piece.astype(F32), extra)
    extra = extra.astype(BF16)
    for z in range(ZS):
        message[z, : ROWS // 2] = packed
        message[z, ROWS // 2] = extra


WINDOW_STEP = 8
WINDOW_CHUNKS = FRAMES // WINDOW_STEP
TALL = 12


def assemble(target, own, near, swapped, far, first):
    def tap(index, carry):
        left = jnp.where(first, near[index], swapped[index])
        right = jnp.where(first, swapped[index], near[index])
        target[index] = jnp.concatenate([own[index], left, far[index], right], axis=0)
        return carry

    lax.fori_loop(0, 9, tap, 0)


def window_kernel(
    place, own, near, swapped, far, frames, later,
    drives, token,
    weights, rows, written, load_sem, store_sem,
):
    chan, first = place[0], place[3] == 0
    source = jnp.clip(CHANS * chan - 2, 0, 8)
    target = source - CHANS * chan + 4

    def load(chunk):
        part = pl.ds(chunk * WINDOW_STEP, WINDOW_STEP)
        return pltpu.make_async_copy(
            frames.at[part, pl.ds(source, 8)], rows.at[part, pl.ds(target, 8)], load_sem.at[chunk]
        )

    def store(chunk):
        part = pl.ds(chunk * WINDOW_STEP, WINDOW_STEP)
        return pltpu.make_async_copy(written.at[part], drives.at[part], store_sem.at[chunk])

    for chunk in range(WINDOW_CHUNKS):
        load(chunk).start()
    empty = jnp.zeros((FRAMES, 2, WIDE, CH), BF16)

    @pl.when(chan == 0)
    def _():
        rows[:, 2:4] = empty

    @pl.when(chan == CHANS - 1)
    def _():
        rows[:, 8:10] = empty

    token[...] = jnp.zeros_like(token)
    assemble(weights, own, near, swapped, far, first)

    def convolve(chunk, carry):
        load(chunk).wait()
        start = pl.multiple_of(chunk * WINDOW_STEP, WINDOW_STEP)
        block = rows[pl.ds(start, WINDOW_STEP)]
        size = WINDOW_STEP * WINDOW * WIDE
        taps = [block[:, 2 + i : 2 + i + WINDOW].reshape(size, CH) for i in range(3)]
        operand = jnp.concatenate(taps, axis=1)
        shape = (WINDOW_STEP * WINDOW, WIDE, CH)
        dims = (((1,), (1,)), ((), ()))
        parts = []
        for j in range(3):
            weight = jnp.concatenate([weights[3 * i + j] for i in range(3)], axis=1)
            parts.append(
                lax.dot_general(operand, weight, dims, preferred_element_type=F32).reshape(shape)
            )
        total = beside(*parts).reshape(WINDOW_STEP, WINDOW, WIDE, CH)
        for r in range(WINDOW):
            kept = total[:, r]
            if r == 0:
                kept = jnp.where(chan == 0, 0.0, kept)
            if r == WINDOW - 1:
                kept = jnp.where(chan == CHANS - 1, 0.0, kept)
            written[pl.ds(start, WINDOW_STEP), r] = kept.astype(BF16)
        store(chunk).start()
        return carry

    lax.fori_loop(0, WINDOW_CHUNKS, convolve, 0)
    for chunk in range(WINDOW_CHUNKS):
        store(chunk).wait()


def relay_kernel(place, rates, received, token, later, message):
    x, z = place[1], place[2]
    rate = doubled(rates[...])
    total = jnp.zeros((ROWS // 2, WIDE, LANES), F32)
    before = total
    elapsed = jnp.zeros((1, LANES), F32)
    elapsed_before = elapsed
    for other in range(ZS):
        mine = z == other
        before = jnp.where(mine, total, before)
        elapsed_before = jnp.where(mine, elapsed, elapsed_before)
        spent = join3(received[other, ROWS // 2], 0)
        decay = jnp.exp(-spent * rate).reshape(1, 1, LANES)
        total = decay * total + received[other, : ROWS // 2].astype(F32)
        elapsed = elapsed + spent

    low = low_half((WIDE, LANES))
    blank = jnp.zeros((WIDE, LANES), F32)

    def rows_of(value):
        swapped = swap_halves(value)
        top = [jnp.where(low, value[r], swapped[r]) for r in range(ROWS // 2)]
        bottom = [jnp.where(low, swapped[r], value[r]) for r in range(ROWS // 2)]
        return [blank] + top + bottom + [blank]

    totals, befores = rows_of(total), rows_of(before)
    row = lax.broadcasted_iota(jnp.int32, (WIDE, LANES), 0)
    extra = blank
    pieces = split3(elapsed) + split3(elapsed_before) + split3(rate)
    for index, piece in enumerate(pieces):
        extra = jnp.where(row == index, piece.astype(F32), extra)
    extra = extra.astype(BF16)
    for chan in range(CHANS):
        for q in range(WINDOW // 2):
            here = CHANS * chan + q
            there = here + WINDOW // 2
            later = jnp.where(low, totals[here], totals[there]).astype(BF16)
            level = jnp.where(low, befores[here], befores[there]).astype(BF16)
            for to in range(XS):
                message[to * CHANS + chan, q] = jnp.where(x == to, level, later)
        for to in range(XS):
            message[to * CHANS + chan, WINDOW // 2] = extra


OUT_STEP = 8
OUT_CHUNKS = FRAMES // OUT_STEP


def readout_kernel(
    place, intervals_far, skip_gain, received, drives_far,
    own, near, swapped, far, frames,
    result,
    intervals, weights, direct, drives, states, written, factors, state,
    load_sem, drive_sem, store_sem, small_sem,
):
    small = [pltpu.make_async_copy(intervals_far, intervals, small_sem)]
    for copy in small:
        copy.start()
    chan, x, first = place[0], place[1], place[3] == 0

    def load(chunk):
        part = pl.ds(chunk * OUT_STEP, OUT_STEP)
        return pltpu.make_async_copy(
            frames.at[part, pl.ds(CHANS * chan, CHANS)], direct.at[part], load_sem.at[chunk]
        )

    def arrive(chunk):
        part = pl.ds(chunk * OUT_STEP, OUT_STEP)
        return pltpu.make_async_copy(drives_far.at[part], drives.at[part], drive_sem.at[chunk])

    def store(chunk):
        part = pl.ds(chunk * OUT_STEP, OUT_STEP)
        return pltpu.make_async_copy(written.at[part], result.at[part], store_sem.at[chunk])

    for chunk in range(OUT_CHUNKS):
        arrive(chunk).start()
        load(chunk).start()

    assemble(weights, own, near, swapped, far, first)
    low = low_half((WIDE, LANES))
    rates, entering = [], []
    for step in range(CHANS):
        source = lax.rem(chan + CHANS - step, CHANS)
        level = received[x * CHANS + source]
        rate = join3(level[WINDOW // 2], 6)
        spent = join3(level[WINDOW // 2], 3)
        total = jnp.zeros((WINDOW // 2, WIDE, LANES), F32)
        for other in range(XS - 1):
            earlier = received[other * CHANS + source]
            decay = jnp.exp(-join3(earlier[WINDOW // 2], 0) * rate).reshape(1, 1, LANES)
            added = decay * total + earlier[: WINDOW // 2].astype(F32)
            total = jnp.where(other < x, added, total)
        decay = jnp.exp(-spent * rate).reshape(1, 1, LANES)
        total = level[: WINDOW // 2].astype(F32) + decay * total
        swapped = swap_halves(total)
        rates.append(rate)
        entering.append(
            [jnp.where(low, total[r], swapped[r]) for r in range(WINDOW // 2)]
            + [jnp.where(low, swapped[r], total[r]) for r in range(WINDOW // 2)]
        )

    for copy in small:
        copy.wait()
    values = [intervals[t] for t in range(FRAMES)]
    low_row = low_half((1, LANES))
    for pair in range(2):
        rate = jnp.where(low_row, rates[2 * pair], rates[2 * pair + 1])
        part = slice(LANES * pair, LANES * (pair + 1))
        for half in range(2):
            some = values[HALF * half : HALF * (half + 1)]
            scaled = table(some, some) * rate
            rest = pl.ds(HALF * half, HALF)
            spread(factors.at[:, rest], 0, part, jnp.exp(-scaled))
            spread(factors.at[:, rest], 1, part, jnp.sqrt(one_minus_exp(2.0 * scaled)))
        for r in range(WINDOW):
            state[r, :, part] = jnp.where(low, entering[2 * pair][r], entering[2 * pair + 1][r])

    def convolve(chunk, carry):
        start = pl.multiple_of(chunk * OUT_STEP, OUT_STEP)
        arrive(chunk).wait()
        carried = state[...]
        for step in range(OUT_STEP):
            decay, gain = factors[0, start + step], factors[1, start + step]
            carried = decay * carried + gain * drives[start + step].astype(F32)
            states[start + step] = carried.astype(BF16)
        state[...] = carried
        size = OUT_STEP * CHANS * WIDE
        block = states[pl.ds(start, OUT_STEP)]
        taps = [block[:, i : i + CHANS].reshape(size, CH) for i in range(3)]
        operand = jnp.concatenate(taps, axis=1)
        shape = (OUT_STEP * CHANS, WIDE, CH)
        parts = []
        for j in range(3):
            weight = jnp.concatenate([weights[3 * i + j] for i in range(3)], axis=0)
            parts.append(jnp.dot(operand, weight, preferred_element_type=F32).reshape(shape))
        load(chunk).wait()
        passed = direct[pl.ds(start, OUT_STEP)].astype(F32).reshape(shape)
        total = beside(*parts) + skip_gain[...].reshape(1, 1, CH) * passed
        written[pl.ds(start, OUT_STEP)] = total.astype(BF16).reshape(OUT_STEP, CHANS, WIDE, CH)
        store(chunk).start()
        return carry

    lax.fori_loop(0, OUT_CHUNKS, convolve, 0)
    for chunk in range(OUT_CHUNKS):
        store(chunk).wait()


def in_vmem():
    return pl.BlockSpec(memory_space=pltpu.VMEM)


def in_smem():
    return pl.BlockSpec(memory_space=pltpu.SMEM)


def anywhere():
    return pl.BlockSpec(memory_space=pl.ANY)


def cost(microseconds):
    return pl.CostEstimate(
        flops=int(microseconds * 1.1e9), bytes_accessed=1 << 20, transcendentals=0
    )


def drive(intervals, rates, kernel_t, frames):
    return pl.pallas_call(
        drive_kernel,
        out_shape=jax.ShapeDtypeStruct((ZS, ROWS // 2 + 1, WIDE, LANES), BF16),
        in_specs=[anywhere()] * 4,
        out_specs=in_vmem(),
        scratch_shapes=[
            pltpu.SMEM((FRAMES,), F32),
            pltpu.VMEM((1, OWN), F32),
            pltpu.VMEM((9, OWN, CH), BF16),
            pltpu.VMEM((FRAMES, ROWS + 2, WIDE, CH), BF16),
            pltpu.VMEM((2, 3 * CH, CH), BF16),
            pltpu.VMEM((2, HALF, WIDE, LANES), F32),
            pltpu.VMEM((ROWS, WIDE, LANES), F32),
            pltpu.SemaphoreType.DMA((CHUNKS, 2)),
            pltpu.SemaphoreType.DMA((3,)),
        ],
        compiler_params=pltpu.CompilerParams(vmem_limit_bytes=60 << 20),
        cost_estimate=cost(8),
        name="drive",
    )(intervals, rates, kernel_t, frames)


def window(place, own, near, swapped, far, frames, later):
    return pl.pallas_call(
        window_kernel,
        out_shape=[
            jax.ShapeDtypeStruct((FRAMES, WINDOW, WIDE, CH), BF16),
            jax.ShapeDtypeStruct((8, LANES), F32),
        ],
        in_specs=[in_smem()] + [in_vmem()] * CHANS + [anywhere()] * 2,
        out_specs=[anywhere(), in_vmem()],
        scratch_shapes=[
            pltpu.VMEM((9, CHANS * OWN, CH), BF16),
            pltpu.VMEM((FRAMES, TALL, WIDE, CH), BF16),
            pltpu.VMEM((FRAMES, WINDOW, WIDE, CH), BF16),
            pltpu.SemaphoreType.DMA((WINDOW_CHUNKS,)),
            pltpu.SemaphoreType.DMA((WINDOW_CHUNKS,)),
        ],
        compiler_params=pltpu.CompilerParams(vmem_limit_bytes=52 << 20),
        cost_estimate=cost(1),
        name="window",
    )(place, own, near, swapped, far, frames, later)


def relay(place, rates, received, token, later):
    return pl.pallas_call(
        relay_kernel,
        out_shape=jax.ShapeDtypeStruct((XS * CHANS, WINDOW // 2 + 1, WIDE, LANES), BF16),
        in_specs=[in_smem(), in_vmem(), in_vmem(), anywhere(), anywhere()],
        out_specs=in_vmem(),
        compiler_params=pltpu.CompilerParams(vmem_limit_bytes=16 << 20),
        cost_estimate=cost(1),
        name="relay",
    )(place, rates, received, token, later)


def read_out(place, intervals, skip_gain, received, drives, kernels, frames):
    return pl.pallas_call(
        readout_kernel,
        out_shape=jax.ShapeDtypeStruct((FRAMES, CHANS, WIDE, CH), BF16),
        in_specs=[in_smem(), anywhere(), in_vmem(), in_vmem(), anywhere()]
        + [in_vmem()] * CHANS
        + [anywhere()],
        out_specs=anywhere(),
        scratch_shapes=[
            pltpu.SMEM((FRAMES,), F32),
            pltpu.VMEM((9, CHANS * OWN, CH), BF16),
            pltpu.VMEM((FRAMES, CHANS, WIDE, CH), BF16),
            pltpu.VMEM((FRAMES, WINDOW, WIDE, CH), BF16),
            pltpu.VMEM((FRAMES, WINDOW, WIDE, CH), BF16),
            pltpu.VMEM((FRAMES, CHANS, WIDE, CH), BF16),
            pltpu.VMEM((2, FRAMES, WIDE, CH), F32),
            pltpu.VMEM((WINDOW, WIDE, CH), F32),
            pltpu.SemaphoreType.DMA((OUT_CHUNKS,)),
            pltpu.SemaphoreType.DMA((OUT_CHUNKS,)),
            pltpu.SemaphoreType.DMA((OUT_CHUNKS,)),
            pltpu.SemaphoreType.DMA,
        ],
        compiler_params=pltpu.CompilerParams(vmem_limit_bytes=52 << 20),
        cost_estimate=cost(6),
        name="read_out",
    )(place, intervals, skip_gain, received, drives, *kernels, frames)


def neighbour(value):
    route = [
        (2 * c + core, 2 * ((c + step) % CHANS) + core)
        for c in range(CHANS)
        for core, step in ((0, 1), (1, CHANS - 1))
    ]
    return lax.ppermute(value, ("chan", "clip"), route)


def swap(value):
    return lax.ppermute(value, "clip", [(0, 1), (1, 0)])


def local(frames, intervals, decay_rates, in_kernel, out_kernel, skip_gain):
    axes = ("chan", "x", "z", "clip")
    place = jnp.stack([lax.axis_index(name) for name in axes]).astype(jnp.int32)
    rates = decay_rates.reshape(1, OWN)
    kernel_t = jnp.transpose(in_kernel.reshape(9, CH, OWN), (0, 2, 1))
    out_own = out_kernel.reshape(9, OWN, CH)
    near, out_near = neighbour(kernel_t), neighbour(out_own)
    message = drive(intervals, rates, kernel_t, frames)
    arrived = lax.all_to_all(message, "z", 0, 0)
    pieces = (kernel_t, near, swap(near), neighbour(near))
    out_pieces = (out_own, out_near, swap(out_near), neighbour(out_near))
    drives, done = window(place, *pieces, frames, out_pieces[2])
    onward = relay(place, rates, arrived, done, out_pieces[3])
    received = lax.all_to_all(onward, ("x", "chan"), 0, 0)
    skip = skip_gain.reshape(1, CH)
    return read_out(place, intervals, skip, received, drives, out_pieces, frames)


def solution(mesh):
    whole = jax.sharding.Mesh(
        mesh.devices.reshape(XS, ZS, CHANS, 2), ("x", "z", "chan", "clip")
    )
    time = ("clip", "x", "z")
    placed = (
        P(time, None, None, None),
        P(time),
        P("chan"),
        P(None, None, None, "chan"),
        P(None, None, "chan", None),
        P(),
    )
    return jax.shard_map(
        local,
        mesh=whole,
        in_specs=placed,
        out_specs=P(time, "chan", None, None),
        check_vma=False,
    )
```

```python
import functools

import jax
import jax.numpy as jnp
from jax import lax
from jax.experimental import pallas as pl
from jax.experimental.pallas import tpu as pltpu
from jax.sharding import PartitionSpec as P

F32 = jnp.float32
BF16 = jnp.bfloat16
FRAMES = 32
HALF = 16
ROWS = 16
WIDE = 16
CH = 256
OWN = 64
LANES = 128
CHANS = 4
ZS = 8
XS = 4
WINDOW = 6
STEP = 4
PIECES = ((0, 4), (4, 4), (8, 4), (12, 4))
CHUNKS = len(PIECES)


def split3(value):
    high = value.astype(BF16)
    rest = value - high.astype(F32)
    middle = rest.astype(BF16)
    low = (rest - middle.astype(F32)).astype(BF16)
    return high, middle, low


def join3(block, start):
    parts = block.astype(F32)
    return parts[start : start + 1] + parts[start + 1 : start + 2] + parts[start + 2 : start + 3]


def low_half(shape):
    return lax.broadcasted_iota(jnp.int32, shape, len(shape) - 1) < OWN


def swap_halves(value):
    return pltpu.roll(value, OWN, value.ndim - 1)


def doubled(rates):
    row = jnp.concatenate([rates, rates], axis=1)
    return row


def table(low_values, high_values):
    row = lax.broadcasted_iota(jnp.int32, (HALF, LANES), 0)
    low = low_half((HALF, LANES))
    result = jnp.zeros((HALF, LANES), F32)
    for t in range(HALF):
        result = jnp.where(row == t, jnp.where(low, low_values[t], high_values[t]), result)
    return result


def spread(target, index, lanes, rows):
    for t in range(HALF):
        target[index, t, :, lanes] = jnp.broadcast_to(rows[t : t + 1], (WIDE, LANES))


def one_minus_exp(value):
    series = value * (
        1.0 - value * (0.5 - value * (1.0 / 6 - value * (1.0 / 24 - value * (1.0 / 120))))
    )
    return jnp.where(value < 0.125, series, 1.0 - jnp.exp(-value))


def beside(left, centre, right):
    column = lax.broadcasted_iota(jnp.int32, centre.shape, 1)
    total = centre + jnp.where(column == 0, 0.0, pltpu.roll(left, 1, 1))
    return total + jnp.where(column == WIDE - 1, 0.0, pltpu.roll(right, WIDE - 1, 1))


def running(values):
    sums = [values[0]]
    for value in values[1:]:
        sums.append(sums[-1] + value)
    return sums


def drive_kernel(
    intervals_far, rates_far, kernel_far, frames,
    message,
    intervals, rates, kernel_t, padded, weights, factors, state, load_sem, small_sem,
):
    small = [
        pltpu.make_async_copy(source, target, small_sem.at[index])
        for index, (source, target) in enumerate(
            ((kernel_far, kernel_t), (intervals_far, intervals), (rates_far, rates))
        )
    ]
    for copy in small:
        copy.start()

    def load(chunk, half):
        first, size = PIECES[chunk]
        part = pl.ds(half * HALF + first, size)
        return pltpu.make_async_copy(
            frames.at[part],
            padded.at[part, pl.ds(1, ROWS)],
            load_sem.at[chunk, half],
        )

    load(0, 0).start()
    load(0, 1).start()

    empty = jnp.zeros((FRAMES, 1, WIDE, CH), BF16)
    padded[:, 0:1] = empty
    padded[:, ROWS + 1 : ROWS + 2] = empty
    nothing = jnp.zeros((CH, OWN), BF16)
    for copy in small:
        copy.wait()
    for chunk in range(1, CHUNKS):
        load(chunk, 0).start()
        load(chunk, 1).start()
    for i in range(3):
        tap = [kernel_t[3 * i + j].astype(F32).T.astype(BF16) for j in range(3)]
        weights[0, CH * i : CH * (i + 1), :] = jnp.concatenate([tap[0], tap[1], tap[2], nothing], 1)
        weights[1, CH * i : CH * (i + 1), :] = jnp.concatenate([tap[1], tap[0], nothing, tap[2]], 1)

    values = [intervals[t] for t in range(FRAMES)]
    rate = doubled(rates[...])
    scaled = table(values[:HALF], values[HALF:]) * rate
    spread(factors, 0, slice(None), jnp.exp(-scaled))
    spread(factors, 1, slice(None), jnp.sqrt(one_minus_exp(2.0 * scaled)))
    state[...] = jnp.zeros_like(state)

    def products(chunk):
        load(chunk, 0).wait()
        load(chunk, 1).wait()
        begin, size = PIECES[chunk]
        both = []
        for half in range(2):
            block = padded[pl.ds(half * HALF + begin, size)]
            taps = [block[:, i : i + ROWS].reshape(size * ROWS * WIDE, CH) for i in range(3)]
            both.append(
                jnp.dot(jnp.concatenate(taps, axis=1), weights[half], preferred_element_type=F32)
            )
        return both

    def advance(chunk, first, second):
        begin, size = PIECES[chunk]
        low = low_half((size * ROWS * WIDE, LANES))
        left = jnp.where(low, first[:, :LANES], second[:, :LANES])
        centre = swap_halves(jnp.where(low, second[:, :LANES], first[:, :LANES]))
        right = first[:, LANES:] + second[:, LANES:]
        shape = (size * ROWS, WIDE, LANES)
        drives = beside(left.reshape(shape), centre.reshape(shape), right.reshape(shape))
        drives = drives.reshape(size, ROWS, WIDE, LANES)
        carried = state[...]
        for step in range(size):
            now = begin + step
            carried = factors[0, now] * carried + factors[1, now] * drives[step]
        state[...] = carried

    waiting = products(0)
    for chunk in range(CHUNKS):
        ready = waiting
        if chunk + 1 < CHUNKS:
            waiting = products(chunk + 1)
        advance(chunk, *ready)

    late = functools.reduce(lambda a, b: a + b, values[HALF:])
    total = functools.reduce(lambda a, b: a + b, values[:HALF]) + late
    carried = state[...]
    end = carried + jnp.exp(-late * rate).reshape(1, 1, LANES) * swap_halves(carried)
    other = swap_halves(end)
    low = low_half((ROWS // 2, WIDE, LANES))
    packed = jnp.where(low, other[: ROWS // 2], end[ROWS // 2 :]).astype(BF16)
    row = lax.broadcasted_iota(jnp.int32, (WIDE, LANES), 0)
    pieces = split3(jnp.full((WIDE, LANES), total, F32))
    extra = jnp.zeros((WIDE, LANES), F32)
    for index, piece in enumerate(pieces):
        extra = jnp.where(row == index, piece.astype(F32), extra)
    extra = extra.astype(BF16)
    for z in range(ZS):
        message[z, : ROWS // 2] = packed
        message[z, ROWS // 2] = extra


WINDOW_STEP = 8
WINDOW_CHUNKS = FRAMES // WINDOW_STEP
TALL = 12


def assemble(target, own, near, swapped, far, first):
    def tap(index, carry):
        left = jnp.where(first, near[index], swapped[index])
        right = jnp.where(first, swapped[index], near[index])
        target[index] = jnp.concatenate([own[index], left, far[index], right], axis=0)
        return carry

    lax.fori_loop(0, 9, tap, 0)


def window_kernel(
    place, own, near, swapped, far, frames, later,
    drives, token,
    weights, rows, written, load_sem, store_sem,
):
    chan, first = place[0], place[3] == 0
    source = jnp.clip(CHANS * chan - 2, 0, 8)
    target = source - CHANS * chan + 4

    def load(chunk):
        part = pl.ds(chunk * WINDOW_STEP, WINDOW_STEP)
        return pltpu.make_async_copy(
            frames.at[part, pl.ds(source, 8)], rows.at[part, pl.ds(target, 8)], load_sem.at[chunk]
        )

    def store(chunk):
        part = pl.ds(chunk * WINDOW_STEP, WINDOW_STEP)
        return pltpu.make_async_copy(written.at[part], drives.at[part], store_sem.at[chunk])

    for chunk in range(WINDOW_CHUNKS):
        load(chunk).start()
    empty = jnp.zeros((FRAMES, 2, WIDE, CH), BF16)

    @pl.when(chan == 0)
    def _():
        rows[:, 2:4] = empty

    @pl.when(chan == CHANS - 1)
    def _():
        rows[:, 8:10] = empty

    token[...] = jnp.zeros_like(token)
    assemble(weights, own, near, swapped, far, first)

    def convolve(chunk, carry):
        load(chunk).wait()
        start = pl.multiple_of(chunk * WINDOW_STEP, WINDOW_STEP)
        block = rows[pl.ds(start, WINDOW_STEP)]
        size = WINDOW_STEP * WINDOW * WIDE
        taps = [block[:, 2 + i : 2 + i + WINDOW].reshape(size, CH) for i in range(3)]
        operand = jnp.concatenate(taps, axis=1)
        shape = (WINDOW_STEP * WINDOW, WIDE, CH)
        dims = (((1,), (1,)), ((), ()))
        parts = []
        for j in range(3):
            weight = jnp.concatenate([weights[3 * i + j] for i in range(3)], axis=1)
            parts.append(
                lax.dot_general(operand, weight, dims, preferred_element_type=F32).reshape(shape)
            )
        total = beside(*parts).reshape(WINDOW_STEP, WINDOW, WIDE, CH)
        for r in range(WINDOW):
            kept = total[:, r]
            if r == 0:
                kept = jnp.where(chan == 0, 0.0, kept)
            if r == WINDOW - 1:
                kept = jnp.where(chan == CHANS - 1, 0.0, kept)
            written[pl.ds(start, WINDOW_STEP), r] = kept.astype(BF16)
        store(chunk).start()
        return carry

    lax.fori_loop(0, WINDOW_CHUNKS, convolve, 0)
    for chunk in range(WINDOW_CHUNKS):
        store(chunk).wait()


def relay_kernel(place, rates, received, token, message):
    x, z = place[1], place[2]
    rate = doubled(rates[...])
    total = jnp.zeros((ROWS // 2, WIDE, LANES), F32)
    before = total
    elapsed = jnp.zeros((1, LANES), F32)
    elapsed_before = elapsed
    for other in range(ZS):
        mine = z == other
        before = jnp.where(mine, total, before)
        elapsed_before = jnp.where(mine, elapsed, elapsed_before)
        spent = join3(received[other, ROWS // 2], 0)
        decay = jnp.exp(-spent * rate).reshape(1, 1, LANES)
        total = decay * total + received[other, : ROWS // 2].astype(F32)
        elapsed = elapsed + spent

    low = low_half((WIDE, LANES))
    blank = jnp.zeros((WIDE, LANES), F32)

    def rows_of(value):
        swapped = swap_halves(value)
        top = [jnp.where(low, value[r], swapped[r]) for r in range(ROWS // 2)]
        bottom = [jnp.where(low, swapped[r], value[r]) for r in range(ROWS // 2)]
        return [blank] + top + bottom + [blank]

    totals, befores = rows_of(total), rows_of(before)
    row = lax.broadcasted_iota(jnp.int32, (WIDE, LANES), 0)
    extra = blank
    pieces = split3(elapsed) + split3(elapsed_before) + split3(rate)
    for index, piece in enumerate(pieces):
        extra = jnp.where(row == index, piece.astype(F32), extra)
    extra = extra.astype(BF16)
    for chan in range(CHANS):
        for q in range(WINDOW // 2):
            here = CHANS * chan + q
            there = here + WINDOW // 2
            later = jnp.where(low, totals[here], totals[there]).astype(BF16)
            level = jnp.where(low, befores[here], befores[there]).astype(BF16)
            for to in range(XS):
                message[to * CHANS + chan, q] = jnp.where(x == to, level, later)
        for to in range(XS):
            message[to * CHANS + chan, WINDOW // 2] = extra


OUT_STEP = 8
OUT_CHUNKS = FRAMES // OUT_STEP


def readout_kernel(
    place, intervals_far, skip_gain, received, drives_far,
    own, near, swapped, far, frames,
    result,
    intervals, weights, direct, drives, states, written, factors, state,
    load_sem, drive_sem, store_sem, small_sem,
):
    small = [pltpu.make_async_copy(intervals_far, intervals, small_sem)]
    for copy in small:
        copy.start()
    chan, x, first = place[0], place[1], place[3] == 0

    def load(chunk):
        part = pl.ds(chunk * OUT_STEP, OUT_STEP)
        return pltpu.make_async_copy(
            frames.at[part, pl.ds(CHANS * chan, CHANS)], direct.at[part], load_sem.at[chunk]
        )

    def arrive(chunk):
        part = pl.ds(chunk * OUT_STEP, OUT_STEP)
        return pltpu.make_async_copy(drives_far.at[part], drives.at[part], drive_sem.at[chunk])

    def store(chunk):
        part = pl.ds(chunk * OUT_STEP, OUT_STEP)
        return pltpu.make_async_copy(written.at[part], result.at[part], store_sem.at[chunk])

    for chunk in range(OUT_CHUNKS):
        arrive(chunk).start()
        load(chunk).start()

    assemble(weights, own, near, swapped, far, first)
    low = low_half((WIDE, LANES))
    rates, entering = [], []
    for step in range(CHANS):
        source = lax.rem(chan + CHANS - step, CHANS)
        level = received[x * CHANS + source]
        rate = join3(level[WINDOW // 2], 6)
        spent = join3(level[WINDOW // 2], 3)
        total = jnp.zeros((WINDOW // 2, WIDE, LANES), F32)
        for other in range(XS - 1):
            earlier = received[other * CHANS + source]
            decay = jnp.exp(-join3(earlier[WINDOW // 2], 0) * rate).reshape(1, 1, LANES)
            added = decay * total + earlier[: WINDOW // 2].astype(F32)
            total = jnp.where(other < x, added, total)
        decay = jnp.exp(-spent * rate).reshape(1, 1, LANES)
        total = level[: WINDOW // 2].astype(F32) + decay * total
        swapped = swap_halves(total)
        rates.append(rate)
        entering.append(
            [jnp.where(low, total[r], swapped[r]) for r in range(WINDOW // 2)]
            + [jnp.where(low, swapped[r], total[r]) for r in range(WINDOW // 2)]
        )

    for copy in small:
        copy.wait()
    values = [intervals[t] for t in range(FRAMES)]
    low_row = low_half((1, LANES))
    for pair in range(2):
        rate = jnp.where(low_row, rates[2 * pair], rates[2 * pair + 1])
        part = slice(LANES * pair, LANES * (pair + 1))
        for half in range(2):
            some = values[HALF * half : HALF * (half + 1)]
            scaled = table(some, some) * rate
            rest = pl.ds(HALF * half, HALF)
            spread(factors.at[:, rest], 0, part, jnp.exp(-scaled))
            spread(factors.at[:, rest], 1, part, jnp.sqrt(one_minus_exp(2.0 * scaled)))
        for r in range(WINDOW):
            state[r, :, part] = jnp.where(low, entering[2 * pair][r], entering[2 * pair + 1][r])

    def convolve(chunk, carry):
        start = pl.multiple_of(chunk * OUT_STEP, OUT_STEP)
        arrive(chunk).wait()
        carried = state[...]
        for step in range(OUT_STEP):
            decay, gain = factors[0, start + step], factors[1, start + step]
            carried = decay * carried + gain * drives[start + step].astype(F32)
            states[start + step] = carried.astype(BF16)
        state[...] = carried
        size = OUT_STEP * CHANS * WIDE
        block = states[pl.ds(start, OUT_STEP)]
        taps = [block[:, i : i + CHANS].reshape(size, CH) for i in range(3)]
        operand = jnp.concatenate(taps, axis=1)
        shape = (OUT_STEP * CHANS, WIDE, CH)
        parts = []
        for j in range(3):
            weight = jnp.concatenate([weights[3 * i + j] for i in range(3)], axis=0)
            parts.append(jnp.dot(operand, weight, preferred_element_type=F32).reshape(shape))
        load(chunk).wait()
        passed = direct[pl.ds(start, OUT_STEP)].astype(F32).reshape(shape)
        total = beside(*parts) + skip_gain[...].reshape(1, 1, CH) * passed
        written[pl.ds(start, OUT_STEP)] = total.astype(BF16).reshape(OUT_STEP, CHANS, WIDE, CH)
        store(chunk).start()
        return carry

    lax.fori_loop(0, OUT_CHUNKS, convolve, 0)
    for chunk in range(OUT_CHUNKS):
        store(chunk).wait()


def in_vmem():
    return pl.BlockSpec(memory_space=pltpu.VMEM)


def in_smem():
    return pl.BlockSpec(memory_space=pltpu.SMEM)


def anywhere():
    return pl.BlockSpec(memory_space=pl.ANY)


def cost(microseconds):
    return pl.CostEstimate(
        flops=int(microseconds * 1.1e9), bytes_accessed=1 << 20, transcendentals=0
    )


def drive(intervals, rates, kernel_t, frames):
    return pl.pallas_call(
        drive_kernel,
        out_shape=jax.ShapeDtypeStruct((ZS, ROWS // 2 + 1, WIDE, LANES), BF16),
        in_specs=[anywhere()] * 4,
        out_specs=in_vmem(),
        scratch_shapes=[
            pltpu.SMEM((FRAMES,), F32),
            pltpu.VMEM((1, OWN), F32),
            pltpu.VMEM((9, OWN, CH), BF16),
            pltpu.VMEM((FRAMES, ROWS + 2, WIDE, CH), BF16),
            pltpu.VMEM((2, 3 * CH, CH), BF16),
            pltpu.VMEM((2, HALF, WIDE, LANES), F32),
            pltpu.VMEM((ROWS, WIDE, LANES), F32),
            pltpu.SemaphoreType.DMA((CHUNKS, 2)),
            pltpu.SemaphoreType.DMA((3,)),
        ],
        compiler_params=pltpu.CompilerParams(vmem_limit_bytes=60 << 20),
        cost_estimate=cost(8),
        name="drive",
    )(intervals, rates, kernel_t, frames)


def window(place, own, near, swapped, far, frames, later):
    return pl.pallas_call(
        window_kernel,
        out_shape=[
            jax.ShapeDtypeStruct((FRAMES, WINDOW, WIDE, CH), BF16),
            jax.ShapeDtypeStruct((8, LANES), F32),
        ],
        in_specs=[in_smem()] + [in_vmem()] * CHANS + [anywhere()] * 2,
        out_specs=[anywhere(), in_vmem()],
        scratch_shapes=[
            pltpu.VMEM((9, CHANS * OWN, CH), BF16),
            pltpu.VMEM((FRAMES, TALL, WIDE, CH), BF16),
            pltpu.VMEM((FRAMES, WINDOW, WIDE, CH), BF16),
            pltpu.SemaphoreType.DMA((WINDOW_CHUNKS,)),
            pltpu.SemaphoreType.DMA((WINDOW_CHUNKS,)),
        ],
        compiler_params=pltpu.CompilerParams(vmem_limit_bytes=52 << 20),
        cost_estimate=cost(1),
        name="window",
    )(place, own, near, swapped, far, frames, later)


def relay(place, rates, received, token):
    return pl.pallas_call(
        relay_kernel,
        out_shape=jax.ShapeDtypeStruct((XS * CHANS, WINDOW // 2 + 1, WIDE, LANES), BF16),
        in_specs=[in_smem(), in_vmem(), in_vmem(), anywhere()],
        out_specs=in_vmem(),
        compiler_params=pltpu.CompilerParams(vmem_limit_bytes=16 << 20),
        cost_estimate=cost(1),
        name="relay",
    )(place, rates, received, token)


def read_out(place, intervals, skip_gain, received, drives, kernels, frames):
    return pl.pallas_call(
        readout_kernel,
        out_shape=jax.ShapeDtypeStruct((FRAMES, CHANS, WIDE, CH), BF16),
        in_specs=[in_smem(), anywhere(), in_vmem(), in_vmem(), anywhere()]
        + [in_vmem()] * CHANS
        + [anywhere()],
        out_specs=anywhere(),
        scratch_shapes=[
            pltpu.SMEM((FRAMES,), F32),
            pltpu.VMEM((9, CHANS * OWN, CH), BF16),
            pltpu.VMEM((FRAMES, CHANS, WIDE, CH), BF16),
            pltpu.VMEM((FRAMES, WINDOW, WIDE, CH), BF16),
            pltpu.VMEM((FRAMES, WINDOW, WIDE, CH), BF16),
            pltpu.VMEM((FRAMES, CHANS, WIDE, CH), BF16),
            pltpu.VMEM((2, FRAMES, WIDE, CH), F32),
            pltpu.VMEM((WINDOW, WIDE, CH), F32),
            pltpu.SemaphoreType.DMA((OUT_CHUNKS,)),
            pltpu.SemaphoreType.DMA((OUT_CHUNKS,)),
            pltpu.SemaphoreType.DMA((OUT_CHUNKS,)),
            pltpu.SemaphoreType.DMA,
        ],
        compiler_params=pltpu.CompilerParams(vmem_limit_bytes=52 << 20),
        cost_estimate=cost(6),
        name="read_out",
    )(place, intervals, skip_gain, received, drives, *kernels, frames)


def neighbour(value):
    route = [
        (2 * c + core, 2 * ((c + step) % CHANS) + core)
        for c in range(CHANS)
        for core, step in ((0, 1), (1, CHANS - 1))
    ]
    return lax.ppermute(value, ("chan", "clip"), route)


def after_kernel(*refs):
    del refs


def after(value, other):
    return pl.pallas_call(
        after_kernel,
        out_shape=jax.ShapeDtypeStruct(value.shape, value.dtype),
        in_specs=[anywhere()] * 2,
        out_specs=anywhere(),
        input_output_aliases={0: 0},
        compiler_params=pltpu.CompilerParams(vmem_limit_bytes=16 << 20),
        cost_estimate=cost(0),
        name="after",
    )(value, other)


def swap(value):
    return lax.ppermute(value, "clip", [(0, 1), (1, 0)])


def local(frames, intervals, decay_rates, in_kernel, out_kernel, skip_gain):
    axes = ("chan", "x", "z", "clip")
    place = jnp.stack([lax.axis_index(name) for name in axes]).astype(jnp.int32)
    rates = decay_rates.reshape(1, OWN)
    kernel_t = jnp.transpose(in_kernel.reshape(9, CH, OWN), (0, 2, 1))
    out_own = out_kernel.reshape(9, OWN, CH)
    near, out_near = neighbour(kernel_t), neighbour(out_own)
    message = drive(intervals, rates, kernel_t, frames)
    arrived = lax.all_to_all(message, "z", 0, 0)
    pieces = (kernel_t, near, swap(near), neighbour(near))
    out_swapped = swap(out_near)
    out_near = after(out_near, pieces[3])
    out_far = neighbour(out_near)
    out_pieces = (out_own, out_near, out_swapped, out_far)
    drives, done = window(place, *pieces, frames, out_pieces[2])
    onward = relay(place, rates, arrived, done)
    received = lax.all_to_all(onward, ("x", "chan"), 0, 0)
    skip = skip_gain.reshape(1, CH)
    return read_out(place, intervals, skip, received, drives, out_pieces, frames)


def solution(mesh):
    whole = jax.sharding.Mesh(
        mesh.devices.reshape(XS, ZS, CHANS, 2), ("x", "z", "chan", "clip")
    )
    time = ("clip", "x", "z")
    placed = (
        P(time, None, None, None),
        P(time),
        P("chan"),
        P(None, None, None, "chan"),
        P(None, None, "chan", None),
        P(),
    )
    return jax.shard_map(
        local,
        mesh=whole,
        in_specs=placed,
        out_specs=P(time, "chan", None, None),
        check_vma=False,
    )
```

```python
import functools

import jax
import jax.numpy as jnp
from jax import lax
from jax.experimental import pallas as pl
from jax.experimental.pallas import tpu as pltpu
from jax.sharding import PartitionSpec as P

F32 = jnp.float32
BF16 = jnp.bfloat16
FRAMES = 32
HALF = 16
ROWS = 16
WIDE = 16
CH = 256
OWN = 64
LANES = 128
CHANS = 4
ZS = 8
XS = 4
WINDOW = 6
STEP = 4
PIECES = ((0, 4), (4, 4), (8, 4), (12, 4))
CHUNKS = len(PIECES)


def split3(value):
    high = value.astype(BF16)
    rest = value - high.astype(F32)
    middle = rest.astype(BF16)
    low = (rest - middle.astype(F32)).astype(BF16)
    return high, middle, low


def join3(block, start):
    parts = block.astype(F32)
    return parts[start : start + 1] + parts[start + 1 : start + 2] + parts[start + 2 : start + 3]


def low_half(shape):
    return lax.broadcasted_iota(jnp.int32, shape, len(shape) - 1) < OWN


def swap_halves(value):
    return pltpu.roll(value, OWN, value.ndim - 1)


def doubled(rates):
    row = jnp.concatenate([rates, rates], axis=1)
    return row


def table(low_values, high_values):
    row = lax.broadcasted_iota(jnp.int32, (HALF, LANES), 0)
    low = low_half((HALF, LANES))
    result = jnp.zeros((HALF, LANES), F32)
    for t in range(HALF):
        result = jnp.where(row == t, jnp.where(low, low_values[t], high_values[t]), result)
    return result


def spread(target, index, lanes, rows):
    for t in range(HALF):
        target[index, t, :, lanes] = jnp.broadcast_to(rows[t : t + 1], (WIDE, LANES))


def one_minus_exp(value):
    series = value * (
        1.0 - value * (0.5 - value * (1.0 / 6 - value * (1.0 / 24 - value * (1.0 / 120))))
    )
    return jnp.where(value < 0.125, series, 1.0 - jnp.exp(-value))


def beside(left, centre, right):
    column = lax.broadcasted_iota(jnp.int32, centre.shape, 1)
    total = centre + jnp.where(column == 0, 0.0, pltpu.roll(left, 1, 1))
    return total + jnp.where(column == WIDE - 1, 0.0, pltpu.roll(right, WIDE - 1, 1))


def running(values):
    sums = [values[0]]
    for value in values[1:]:
        sums.append(sums[-1] + value)
    return sums


def drive_kernel(
    intervals_far, rates_far, kernel_far, frames,
    message,
    intervals, rates, kernel_t, padded, weights, factors, state, load_sem, small_sem,
):
    small = [
        pltpu.make_async_copy(source, target, small_sem.at[index])
        for index, (source, target) in enumerate(
            ((kernel_far, kernel_t), (intervals_far, intervals), (rates_far, rates))
        )
    ]
    for copy in small:
        copy.start()

    def load(chunk, half):
        first, size = PIECES[chunk]
        part = pl.ds(half * HALF + first, size)
        return pltpu.make_async_copy(
            frames.at[part],
            padded.at[part, pl.ds(1, ROWS)],
            load_sem.at[chunk, half],
        )

    load(0, 0).start()
    load(0, 1).start()

    empty = jnp.zeros((FRAMES, 1, WIDE, CH), BF16)
    padded[:, 0:1] = empty
    padded[:, ROWS + 1 : ROWS + 2] = empty
    nothing = jnp.zeros((CH, OWN), BF16)
    for copy in small:
        copy.wait()
    for chunk in range(1, CHUNKS):
        load(chunk, 0).start()
        load(chunk, 1).start()
    for i in range(3):
        tap = [kernel_t[3 * i + j].astype(F32).T.astype(BF16) for j in range(3)]
        weights[0, CH * i : CH * (i + 1), :] = jnp.concatenate([tap[0], tap[1], tap[2], nothing], 1)
        weights[1, CH * i : CH * (i + 1), :] = jnp.concatenate([tap[1], tap[0], nothing, tap[2]], 1)

    values = [intervals[t] for t in range(FRAMES)]
    rate = doubled(rates[...])
    scaled = table(values[:HALF], values[HALF:]) * rate
    spread(factors, 0, slice(None), jnp.exp(-scaled))
    spread(factors, 1, slice(None), jnp.sqrt(one_minus_exp(2.0 * scaled)))
    state[...] = jnp.zeros_like(state)

    def products(chunk):
        load(chunk, 0).wait()
        load(chunk, 1).wait()
        begin, size = PIECES[chunk]
        both = []
        for half in range(2):
            block = padded[pl.ds(half * HALF + begin, size)]
            taps = [block[:, i : i + ROWS].reshape(size * ROWS * WIDE, CH) for i in range(3)]
            both.append(
                jnp.dot(jnp.concatenate(taps, axis=1), weights[half], preferred_element_type=F32)
            )
        return both

    def advance(chunk, first, second):
        begin, size = PIECES[chunk]
        low = low_half((size * ROWS * WIDE, LANES))
        left = jnp.where(low, first[:, :LANES], second[:, :LANES])
        centre = swap_halves(jnp.where(low, second[:, :LANES], first[:, :LANES]))
        right = first[:, LANES:] + second[:, LANES:]
        shape = (size * ROWS, WIDE, LANES)
        drives = beside(left.reshape(shape), centre.reshape(shape), right.reshape(shape))
        drives = drives.reshape(size, ROWS, WIDE, LANES)
        carried = state[...]
        for step in range(size):
            now = begin + step
            carried = factors[0, now] * carried + factors[1, now] * drives[step]
        state[...] = carried

    waiting = products(0)
    for chunk in range(CHUNKS):
        ready = waiting
        if chunk + 1 < CHUNKS:
            waiting = products(chunk + 1)
        advance(chunk, *ready)

    late = functools.reduce(lambda a, b: a + b, values[HALF:])
    total = functools.reduce(lambda a, b: a + b, values[:HALF]) + late
    carried = state[...]
    end = carried + jnp.exp(-late * rate).reshape(1, 1, LANES) * swap_halves(carried)
    other = swap_halves(end)
    low = low_half((ROWS // 2, WIDE, LANES))
    packed = jnp.where(low, other[: ROWS // 2], end[ROWS // 2 :]).astype(BF16)
    row = lax.broadcasted_iota(jnp.int32, (WIDE, LANES), 0)
    pieces = split3(jnp.full((WIDE, LANES), total, F32))
    extra = jnp.zeros((WIDE, LANES), F32)
    for index, piece in enumerate(pieces):
        extra = jnp.where(row == index, piece.astype(F32), extra)
    extra = extra.astype(BF16)
    for z in range(ZS):
        message[z, : ROWS // 2] = packed
        message[z, ROWS // 2] = extra


WINDOW_STEP = 8
WINDOW_CHUNKS = FRAMES // WINDOW_STEP
TALL = 12


def assemble(target, own, near, swapped, far, first):
    def tap(index, carry):
        left = jnp.where(first, near[index], swapped[index])
        right = jnp.where(first, swapped[index], near[index])
        target[index] = jnp.concatenate([own[index], left, far[index], right], axis=0)
        return carry

    lax.fori_loop(0, 9, tap, 0)


def window_kernel(
    place, own, near, swapped, far, frames, later,
    drives, token,
    weights, rows, written, load_sem, store_sem,
):
    chan, first = place[0], place[3] == 0
    source = jnp.clip(CHANS * chan - 2, 0, 8)
    target = source - CHANS * chan + 4

    def load(chunk):
        part = pl.ds(chunk * WINDOW_STEP, WINDOW_STEP)
        return pltpu.make_async_copy(
            frames.at[part, pl.ds(source, 8)], rows.at[part, pl.ds(target, 8)], load_sem.at[chunk]
        )

    def store(chunk):
        part = pl.ds(chunk * WINDOW_STEP, WINDOW_STEP)
        return pltpu.make_async_copy(written.at[part], drives.at[part], store_sem.at[chunk])

    for chunk in range(WINDOW_CHUNKS):
        load(chunk).start()
    empty = jnp.zeros((FRAMES, 2, WIDE, CH), BF16)

    @pl.when(chan == 0)
    def _():
        rows[:, 2:4] = empty

    @pl.when(chan == CHANS - 1)
    def _():
        rows[:, 8:10] = empty

    token[...] = jnp.zeros_like(token)
    assemble(weights, own, near, swapped, far, first)

    def convolve(chunk, carry):
        load(chunk).wait()
        start = pl.multiple_of(chunk * WINDOW_STEP, WINDOW_STEP)
        block = rows[pl.ds(start, WINDOW_STEP)]
        size = WINDOW_STEP * WINDOW * WIDE
        taps = [block[:, 2 + i : 2 + i + WINDOW].reshape(size, CH) for i in range(3)]
        operand = jnp.concatenate(taps, axis=1)
        shape = (WINDOW_STEP * WINDOW, WIDE, CH)
        dims = (((1,), (1,)), ((), ()))
        parts = []
        for j in range(3):
            weight = jnp.concatenate([weights[3 * i + j] for i in range(3)], axis=1)
            parts.append(
                lax.dot_general(operand, weight, dims, preferred_element_type=F32).reshape(shape)
            )
        total = beside(*parts).reshape(WINDOW_STEP, WINDOW, WIDE, CH)
        for r in range(WINDOW):
            kept = total[:, r]
            if r == 0:
                kept = jnp.where(chan == 0, 0.0, kept)
            if r == WINDOW - 1:
                kept = jnp.where(chan == CHANS - 1, 0.0, kept)
            written[pl.ds(start, WINDOW_STEP), r] = kept.astype(BF16)
        store(chunk).start()
        return carry

    lax.fori_loop(0, WINDOW_CHUNKS, convolve, 0)
    for chunk in range(WINDOW_CHUNKS):
        store(chunk).wait()


def relay_kernel(place, rates, received, token, later, message):
    x, z = place[1], place[2]
    rate = doubled(rates[...])
    total = jnp.zeros((ROWS // 2, WIDE, LANES), F32)
    before = total
    elapsed = jnp.zeros((1, LANES), F32)
    elapsed_before = elapsed
    for other in range(ZS):
        mine = z == other
        before = jnp.where(mine, total, before)
        elapsed_before = jnp.where(mine, elapsed, elapsed_before)
        spent = join3(received[other, ROWS // 2], 0)
        decay = jnp.exp(-spent * rate).reshape(1, 1, LANES)
        total = decay * total + received[other, : ROWS // 2].astype(F32)
        elapsed = elapsed + spent

    low = low_half((WIDE, LANES))
    blank = jnp.zeros((WIDE, LANES), F32)

    def rows_of(value):
        swapped = swap_halves(value)
        top = [jnp.where(low, value[r], swapped[r]) for r in range(ROWS // 2)]
        bottom = [jnp.where(low, swapped[r], value[r]) for r in range(ROWS // 2)]
        return [blank] + top + bottom + [blank]

    totals, befores = rows_of(total), rows_of(before)
    row = lax.broadcasted_iota(jnp.int32, (WIDE, LANES), 0)
    extra = blank
    pieces = split3(elapsed) + split3(elapsed_before) + split3(rate)
    for index, piece in enumerate(pieces):
        extra = jnp.where(row == index, piece.astype(F32), extra)
    extra = extra.astype(BF16)
    for chan in range(CHANS):
        for q in range(WINDOW // 2):
            here = CHANS * chan + q
            there = here + WINDOW // 2
            later = jnp.where(low, totals[here], totals[there]).astype(BF16)
            level = jnp.where(low, befores[here], befores[there]).astype(BF16)
            for to in range(XS):
                message[to * CHANS + chan, q] = jnp.where(x == to, level, later)
        for to in range(XS):
            message[to * CHANS + chan, WINDOW // 2] = extra


OUT_STEP = 8
OUT_CHUNKS = FRAMES // OUT_STEP


def readout_kernel(
    place, intervals_far, skip_gain, received, drives_far,
    own, near, swapped, far, frames,
    result,
    intervals, weights, direct, drives, states, written, factors, state,
    load_sem, drive_sem, store_sem, small_sem,
):
    small = [pltpu.make_async_copy(intervals_far, intervals, small_sem)]
    for copy in small:
        copy.start()
    chan, x, first = place[0], place[1], place[3] == 0

    def load(chunk):
        part = pl.ds(chunk * OUT_STEP, OUT_STEP)
        return pltpu.make_async_copy(
            frames.at[part, pl.ds(CHANS * chan, CHANS)], direct.at[part], load_sem.at[chunk]
        )

    def arrive(chunk):
        part = pl.ds(chunk * OUT_STEP, OUT_STEP)
        return pltpu.make_async_copy(drives_far.at[part], drives.at[part], drive_sem.at[chunk])

    def store(chunk):
        part = pl.ds(chunk * OUT_STEP, OUT_STEP)
        return pltpu.make_async_copy(written.at[part], result.at[part], store_sem.at[chunk])

    for chunk in range(OUT_CHUNKS):
        arrive(chunk).start()
        load(chunk).start()

    assemble(weights, own, near, swapped, far, first)
    low = low_half((WIDE, LANES))
    rates, entering = [], []
    for step in range(CHANS):
        source = lax.rem(chan + CHANS - step, CHANS)
        level = received[x * CHANS + source]
        rate = join3(level[WINDOW // 2], 6)
        spent = join3(level[WINDOW // 2], 3)
        total = jnp.zeros((WINDOW // 2, WIDE, LANES), F32)
        for other in range(XS - 1):
            earlier = received[other * CHANS + source]
            decay = jnp.exp(-join3(earlier[WINDOW // 2], 0) * rate).reshape(1, 1, LANES)
            added = decay * total + earlier[: WINDOW // 2].astype(F32)
            total = jnp.where(other < x, added, total)
        decay = jnp.exp(-spent * rate).reshape(1, 1, LANES)
        total = level[: WINDOW // 2].astype(F32) + decay * total
        swapped = swap_halves(total)
        rates.append(rate)
        entering.append(
            [jnp.where(low, total[r], swapped[r]) for r in range(WINDOW // 2)]
            + [jnp.where(low, swapped[r], total[r]) for r in range(WINDOW // 2)]
        )

    for copy in small:
        copy.wait()
    values = [intervals[t] for t in range(FRAMES)]
    low_row = low_half((1, LANES))
    for pair in range(2):
        rate = jnp.where(low_row, rates[2 * pair], rates[2 * pair + 1])
        part = slice(LANES * pair, LANES * (pair + 1))
        for half in range(2):
            some = values[HALF * half : HALF * (half + 1)]
            scaled = table(some, some) * rate
            rest = pl.ds(HALF * half, HALF)
            spread(factors.at[:, rest], 0, part, jnp.exp(-scaled))
            spread(factors.at[:, rest], 1, part, jnp.sqrt(one_minus_exp(2.0 * scaled)))
        for r in range(WINDOW):
            state[r, :, part] = jnp.where(low, entering[2 * pair][r], entering[2 * pair + 1][r])

    def convolve(chunk, carry):
        start = pl.multiple_of(chunk * OUT_STEP, OUT_STEP)
        arrive(chunk).wait()
        carried = state[...]
        for step in range(OUT_STEP):
            decay, gain = factors[0, start + step], factors[1, start + step]
            carried = decay * carried + gain * drives[start + step].astype(F32)
            states[start + step] = carried.astype(BF16)
        state[...] = carried
        size = OUT_STEP * CHANS * WIDE
        block = states[pl.ds(start, OUT_STEP)]
        taps = [block[:, i : i + CHANS].reshape(size, CH) for i in range(3)]
        operand = jnp.concatenate(taps, axis=1)
        shape = (OUT_STEP * CHANS, WIDE, CH)
        parts = []
        for j in range(3):
            weight = jnp.concatenate([weights[3 * i + j] for i in range(3)], axis=0)
            parts.append(jnp.dot(operand, weight, preferred_element_type=F32).reshape(shape))
        load(chunk).wait()
        passed = direct[pl.ds(start, OUT_STEP)].astype(F32).reshape(shape)
        total = beside(*parts) + skip_gain[...].reshape(1, 1, CH) * passed
        written[pl.ds(start, OUT_STEP)] = total.astype(BF16).reshape(OUT_STEP, CHANS, WIDE, CH)
        store(chunk).start()
        return carry

    lax.fori_loop(0, OUT_CHUNKS, convolve, 0)
    for chunk in range(OUT_CHUNKS):
        store(chunk).wait()


def in_vmem():
    return pl.BlockSpec(memory_space=pltpu.VMEM)


def in_smem():
    return pl.BlockSpec(memory_space=pltpu.SMEM)


def anywhere():
    return pl.BlockSpec(memory_space=pl.ANY)


def cost(microseconds):
    return pl.CostEstimate(
        flops=int(microseconds * 1.1e9), bytes_accessed=1 << 20, transcendentals=0
    )


def drive(intervals, rates, kernel_t, frames):
    return pl.pallas_call(
        drive_kernel,
        out_shape=jax.ShapeDtypeStruct((ZS, ROWS // 2 + 1, WIDE, LANES), BF16),
        in_specs=[anywhere()] * 4,
        out_specs=in_vmem(),
        scratch_shapes=[
            pltpu.SMEM((FRAMES,), F32),
            pltpu.VMEM((1, OWN), F32),
            pltpu.VMEM((9, OWN, CH), BF16),
            pltpu.VMEM((FRAMES, ROWS + 2, WIDE, CH), BF16),
            pltpu.VMEM((2, 3 * CH, CH), BF16),
            pltpu.VMEM((2, HALF, WIDE, LANES), F32),
            pltpu.VMEM((ROWS, WIDE, LANES), F32),
            pltpu.SemaphoreType.DMA((CHUNKS, 2)),
            pltpu.SemaphoreType.DMA((3,)),
        ],
        compiler_params=pltpu.CompilerParams(vmem_limit_bytes=60 << 20),
        cost_estimate=cost(8),
        name="drive",
    )(intervals, rates, kernel_t, frames)


def window(place, own, near, swapped, far, frames, later):
    return pl.pallas_call(
        window_kernel,
        out_shape=[
            jax.ShapeDtypeStruct((FRAMES, WINDOW, WIDE, CH), BF16),
            jax.ShapeDtypeStruct((8, LANES), F32),
        ],
        in_specs=[in_smem()] + [in_vmem()] * CHANS + [anywhere()] * 2,
        out_specs=[anywhere(), in_vmem()],
        scratch_shapes=[
            pltpu.VMEM((9, CHANS * OWN, CH), BF16),
            pltpu.VMEM((FRAMES, TALL, WIDE, CH), BF16),
            pltpu.VMEM((FRAMES, WINDOW, WIDE, CH), BF16),
            pltpu.SemaphoreType.DMA((WINDOW_CHUNKS,)),
            pltpu.SemaphoreType.DMA((WINDOW_CHUNKS,)),
        ],
        compiler_params=pltpu.CompilerParams(vmem_limit_bytes=52 << 20),
        cost_estimate=cost(1),
        name="window",
    )(place, own, near, swapped, far, frames, later)


def relay(place, rates, received, token, later):
    return pl.pallas_call(
        relay_kernel,
        out_shape=jax.ShapeDtypeStruct((XS * CHANS, WINDOW // 2 + 1, WIDE, LANES), BF16),
        in_specs=[in_smem(), in_vmem(), in_vmem(), anywhere(), anywhere()],
        out_specs=in_vmem(),
        compiler_params=pltpu.CompilerParams(vmem_limit_bytes=16 << 20),
        cost_estimate=cost(1),
        name="relay",
    )(place, rates, received, token, later)


def read_out(place, intervals, skip_gain, received, drives, kernels, frames):
    return pl.pallas_call(
        readout_kernel,
        out_shape=jax.ShapeDtypeStruct((FRAMES, CHANS, WIDE, CH), BF16),
        in_specs=[in_smem(), anywhere(), in_vmem(), in_vmem(), anywhere()]
        + [in_vmem()] * CHANS
        + [anywhere()],
        out_specs=anywhere(),
        scratch_shapes=[
            pltpu.SMEM((FRAMES,), F32),
            pltpu.VMEM((9, CHANS * OWN, CH), BF16),
            pltpu.VMEM((FRAMES, CHANS, WIDE, CH), BF16),
            pltpu.VMEM((FRAMES, WINDOW, WIDE, CH), BF16),
            pltpu.VMEM((FRAMES, WINDOW, WIDE, CH), BF16),
            pltpu.VMEM((FRAMES, CHANS, WIDE, CH), BF16),
            pltpu.VMEM((2, FRAMES, WIDE, CH), F32),
            pltpu.VMEM((WINDOW, WIDE, CH), F32),
            pltpu.SemaphoreType.DMA((OUT_CHUNKS,)),
            pltpu.SemaphoreType.DMA((OUT_CHUNKS,)),
            pltpu.SemaphoreType.DMA((OUT_CHUNKS,)),
            pltpu.SemaphoreType.DMA,
        ],
        compiler_params=pltpu.CompilerParams(vmem_limit_bytes=52 << 20),
        cost_estimate=cost(6),
        name="read_out",
    )(place, intervals, skip_gain, received, drives, *kernels, frames)


def neighbour(value):
    route = [
        (2 * c + core, 2 * ((c + step) % CHANS) + core)
        for c in range(CHANS)
        for core, step in ((0, 1), (1, CHANS - 1))
    ]
    return lax.ppermute(value, ("chan", "clip"), route)


def opposite(value):
    return lax.ppermute(value, "chan", [(c, (c + 2) % CHANS) for c in range(CHANS)])


def after_kernel(*refs):
    del refs


def after(value, other, length=2):
    return pl.pallas_call(
        after_kernel,
        out_shape=jax.ShapeDtypeStruct(value.shape, value.dtype),
        in_specs=[anywhere()] * 2,
        out_specs=anywhere(),
        input_output_aliases={0: 0},
        compiler_params=pltpu.CompilerParams(vmem_limit_bytes=16 << 20),
        cost_estimate=cost(length),
        name="after",
    )(value, other)


def swap(value):
    return lax.ppermute(value, "clip", [(0, 1), (1, 0)])


def local(frames, intervals, decay_rates, in_kernel, out_kernel, skip_gain):
    axes = ("chan", "x", "z", "clip")
    place = jnp.stack([lax.axis_index(name) for name in axes]).astype(jnp.int32)
    rates = decay_rates.reshape(1, OWN)
    kernel_t = jnp.transpose(in_kernel.reshape(9, CH, OWN), (0, 2, 1))
    out_own = out_kernel.reshape(9, OWN, CH)
    near, out_near = neighbour(kernel_t), neighbour(out_own)
    message = drive(intervals, rates, kernel_t, frames)
    arrived = lax.all_to_all(message, "z", 0, 0)
    pieces = (kernel_t, near, swap(near), after(opposite(kernel_t), near))
    out_swapped, out_far = swap(out_near), opposite(out_own)
    drives, done = window(place, *pieces, frames, out_swapped)
    out_far = after(out_far, done, 2)
    out_pieces = (out_own, out_near, out_swapped, out_far)
    onward = relay(place, rates, arrived, done, out_pieces[3])
    received = lax.all_to_all(onward, ("x", "chan"), 0, 0)
    skip = skip_gain.reshape(1, CH)
    return read_out(place, intervals, skip, received, drives, out_pieces, frames)


def solution(mesh):
    whole = jax.sharding.Mesh(
        mesh.devices.reshape(XS, ZS, CHANS, 2), ("x", "z", "chan", "clip")
    )
    time = ("clip", "x", "z")
    placed = (
        P(time, None, None, None),
        P(time),
        P("chan"),
        P(None, None, None, "chan"),
        P(None, None, "chan", None),
        P(),
    )
    return jax.shard_map(
        local,
        mesh=whole,
        in_specs=placed,
        out_specs=P(time, "chan", None, None),
        check_vma=False,
    )
```

```python
import functools

import jax
import jax.numpy as jnp
from jax import lax
from jax.experimental import pallas as pl
from jax.experimental.pallas import tpu as pltpu
from jax.sharding import PartitionSpec as P

F32 = jnp.float32
BF16 = jnp.bfloat16
FRAMES = 32
HALF = 16
ROWS = 16
WIDE = 16
CH = 256
OWN = 64
LANES = 128
CHANS = 4
ZS = 8
XS = 4
WINDOW = 6
STEP = 4
PIECES = ((0, 4), (4, 4), (8, 4), (12, 4))
CHUNKS = len(PIECES)


def split3(value):
    high = value.astype(BF16)
    rest = value - high.astype(F32)
    middle = rest.astype(BF16)
    low = (rest - middle.astype(F32)).astype(BF16)
    return high, middle, low


def join3(block, start):
    parts = block.astype(F32)
    return parts[start : start + 1] + parts[start + 1 : start + 2] + parts[start + 2 : start + 3]


def low_half(shape):
    return lax.broadcasted_iota(jnp.int32, shape, len(shape) - 1) < OWN


def swap_halves(value):
    return pltpu.roll(value, OWN, value.ndim - 1)


def doubled(rates):
    row = jnp.concatenate([rates, rates], axis=1)
    return row


def table(low_values, high_values):
    row = lax.broadcasted_iota(jnp.int32, (HALF, LANES), 0)
    low = low_half((HALF, LANES))
    result = jnp.zeros((HALF, LANES), F32)
    for t in range(HALF):
        result = jnp.where(row == t, jnp.where(low, low_values[t], high_values[t]), result)
    return result


def spread(target, index, lanes, rows):
    for t in range(HALF):
        target[index, t, :, lanes] = jnp.broadcast_to(rows[t : t + 1], (WIDE, LANES))


def one_minus_exp(value):
    series = value * (
        1.0 - value * (0.5 - value * (1.0 / 6 - value * (1.0 / 24 - value * (1.0 / 120))))
    )
    return jnp.where(value < 0.125, series, 1.0 - jnp.exp(-value))


def beside(left, centre, right):
    column = lax.broadcasted_iota(jnp.int32, centre.shape, 1)
    total = centre + jnp.where(column == 0, 0.0, pltpu.roll(left, 1, 1))
    return total + jnp.where(column == WIDE - 1, 0.0, pltpu.roll(right, WIDE - 1, 1))


def running(values):
    sums = [values[0]]
    for value in values[1:]:
        sums.append(sums[-1] + value)
    return sums


def drive_kernel(
    intervals_far, rates_far, kernel_far, frames,
    message,
    intervals, rates, kernel_t, padded, weights, factors, state, load_sem, small_sem,
):
    small = [
        pltpu.make_async_copy(source, target, small_sem.at[index])
        for index, (source, target) in enumerate(
            ((kernel_far, kernel_t), (intervals_far, intervals), (rates_far, rates))
        )
    ]
    for copy in small:
        copy.start()

    def load(chunk, half):
        first, size = PIECES[chunk]
        part = pl.ds(half * HALF + first, size)
        return pltpu.make_async_copy(
            frames.at[part],
            padded.at[part, pl.ds(1, ROWS)],
            load_sem.at[chunk, half],
        )

    load(0, 0).start()
    load(0, 1).start()

    empty = jnp.zeros((FRAMES, 1, WIDE, CH), BF16)
    padded[:, 0:1] = empty
    padded[:, ROWS + 1 : ROWS + 2] = empty
    nothing = jnp.zeros((CH, OWN), BF16)
    for copy in small:
        copy.wait()
    for chunk in range(1, CHUNKS):
        load(chunk, 0).start()
        load(chunk, 1).start()
    for i in range(3):
        tap = [kernel_t[3 * i + j].astype(F32).T.astype(BF16) for j in range(3)]
        weights[0, CH * i : CH * (i + 1), :] = jnp.concatenate([tap[0], tap[1], tap[2], nothing], 1)
        weights[1, CH * i : CH * (i + 1), :] = jnp.concatenate([tap[1], tap[0], nothing, tap[2]], 1)

    values = [intervals[t] for t in range(FRAMES)]
    rate = doubled(rates[...])
    scaled = table(values[:HALF], values[HALF:]) * rate
    spread(factors, 0, slice(None), jnp.exp(-scaled))
    spread(factors, 1, slice(None), jnp.sqrt(one_minus_exp(2.0 * scaled)))
    state[...] = jnp.zeros_like(state)

    def products(chunk):
        load(chunk, 0).wait()
        load(chunk, 1).wait()
        begin, size = PIECES[chunk]
        both = []
        for half in range(2):
            block = padded[pl.ds(half * HALF + begin, size)]
            taps = [block[:, i : i + ROWS].reshape(size * ROWS * WIDE, CH) for i in range(3)]
            both.append(
                jnp.dot(jnp.concatenate(taps, axis=1), weights[half], preferred_element_type=F32)
            )
        return both

    def advance(chunk, first, second):
        begin, size = PIECES[chunk]
        low = low_half((size * ROWS * WIDE, LANES))
        left = jnp.where(low, first[:, :LANES], second[:, :LANES])
        centre = swap_halves(jnp.where(low, second[:, :LANES], first[:, :LANES]))
        right = first[:, LANES:] + second[:, LANES:]
        shape = (size * ROWS, WIDE, LANES)
        drives = beside(left.reshape(shape), centre.reshape(shape), right.reshape(shape))
        drives = drives.reshape(size, ROWS, WIDE, LANES)
        carried = state[...]
        for step in range(size):
            now = begin + step
            carried = factors[0, now] * carried + factors[1, now] * drives[step]
        state[...] = carried

    waiting = products(0)
    for chunk in range(CHUNKS):
        ready = waiting
        if chunk + 1 < CHUNKS:
            waiting = products(chunk + 1)
        advance(chunk, *ready)

    late = functools.reduce(lambda a, b: a + b, values[HALF:])
    total = functools.reduce(lambda a, b: a + b, values[:HALF]) + late
    carried = state[...]
    end = carried + jnp.exp(-late * rate).reshape(1, 1, LANES) * swap_halves(carried)
    other = swap_halves(end)
    low = low_half((ROWS // 2, WIDE, LANES))
    packed = jnp.where(low, other[: ROWS // 2], end[ROWS // 2 :]).astype(BF16)
    row = lax.broadcasted_iota(jnp.int32, (WIDE, LANES), 0)
    pieces = split3(jnp.full((WIDE, LANES), total, F32))
    extra = jnp.zeros((WIDE, LANES), F32)
    for index, piece in enumerate(pieces):
        extra = jnp.where(row == index, piece.astype(F32), extra)
    extra = extra.astype(BF16)
    for z in range(ZS):
        message[z, : ROWS // 2] = packed
        message[z, ROWS // 2] = extra


WINDOW_STEP = 8
WINDOW_CHUNKS = FRAMES // WINDOW_STEP
TALL = 12


def assemble(target, own, near, swapped, far, first):
    def tap(index, carry):
        left = jnp.where(first, near[index], swapped[index])
        right = jnp.where(first, swapped[index], near[index])
        target[index] = jnp.concatenate([own[index], left, far[index], right], axis=0)
        return carry

    lax.fori_loop(0, 9, tap, 0)


def window_kernel(
    place, own, near, swapped, far, frames,
    drives, token,
    weights, rows, written, load_sem, store_sem,
):
    chan, first = place[0], place[3] == 0
    source = jnp.clip(CHANS * chan - 2, 0, 8)
    target = source - CHANS * chan + 4

    def load(chunk):
        part = pl.ds(chunk * WINDOW_STEP, WINDOW_STEP)
        return pltpu.make_async_copy(
            frames.at[part, pl.ds(source, 8)], rows.at[part, pl.ds(target, 8)], load_sem.at[chunk]
        )

    def store(chunk):
        part = pl.ds(chunk * WINDOW_STEP, WINDOW_STEP)
        return pltpu.make_async_copy(written.at[part], drives.at[part], store_sem.at[chunk])

    for chunk in range(WINDOW_CHUNKS):
        load(chunk).start()
    empty = jnp.zeros((FRAMES, 2, WIDE, CH), BF16)

    @pl.when(chan == 0)
    def _():
        rows[:, 2:4] = empty

    @pl.when(chan == CHANS - 1)
    def _():
        rows[:, 8:10] = empty

    token[...] = jnp.zeros_like(token)
    assemble(weights, own, near, swapped, far, first)

    def convolve(chunk, carry):
        load(chunk).wait()
        start = pl.multiple_of(chunk * WINDOW_STEP, WINDOW_STEP)
        block = rows[pl.ds(start, WINDOW_STEP)]
        size = WINDOW_STEP * WINDOW * WIDE
        taps = [block[:, 2 + i : 2 + i + WINDOW].reshape(size, CH) for i in range(3)]
        operand = jnp.concatenate(taps, axis=1)
        shape = (WINDOW_STEP * WINDOW, WIDE, CH)
        dims = (((1,), (1,)), ((), ()))
        parts = []
        for j in range(3):
            weight = jnp.concatenate([weights[3 * i + j] for i in range(3)], axis=1)
            parts.append(
                lax.dot_general(operand, weight, dims, preferred_element_type=F32).reshape(shape)
            )
        total = beside(*parts).reshape(WINDOW_STEP, WINDOW, WIDE, CH)
        for r in range(WINDOW):
            kept = total[:, r]
            if r == 0:
                kept = jnp.where(chan == 0, 0.0, kept)
            if r == WINDOW - 1:
                kept = jnp.where(chan == CHANS - 1, 0.0, kept)
            written[pl.ds(start, WINDOW_STEP), r] = kept.astype(BF16)
        store(chunk).start()
        return carry

    lax.fori_loop(0, WINDOW_CHUNKS, convolve, 0)
    for chunk in range(WINDOW_CHUNKS):
        store(chunk).wait()


def relay_kernel(place, rates, received, token, message, done):
    x, z = place[1], place[2]
    done[...] = jnp.zeros_like(done)
    rate = doubled(rates[...])
    total = jnp.zeros((ROWS // 2, WIDE, LANES), F32)
    before = total
    elapsed = jnp.zeros((1, LANES), F32)
    elapsed_before = elapsed
    for other in range(ZS):
        mine = z == other
        before = jnp.where(mine, total, before)
        elapsed_before = jnp.where(mine, elapsed, elapsed_before)
        spent = join3(received[other, ROWS // 2], 0)
        decay = jnp.exp(-spent * rate).reshape(1, 1, LANES)
        total = decay * total + received[other, : ROWS // 2].astype(F32)
        elapsed = elapsed + spent

    low = low_half((WIDE, LANES))
    blank = jnp.zeros((WIDE, LANES), F32)

    def rows_of(value):
        swapped = swap_halves(value)
        top = [jnp.where(low, value[r], swapped[r]) for r in range(ROWS // 2)]
        bottom = [jnp.where(low, swapped[r], value[r]) for r in range(ROWS // 2)]
        return [blank] + top + bottom + [blank]

    totals, befores = rows_of(total), rows_of(before)
    row = lax.broadcasted_iota(jnp.int32, (WIDE, LANES), 0)
    extra = blank
    pieces = split3(elapsed) + split3(elapsed_before) + split3(rate)
    for index, piece in enumerate(pieces):
        extra = jnp.where(row == index, piece.astype(F32), extra)
    extra = extra.astype(BF16)
    for chan in range(CHANS):
        for q in range(WINDOW // 2):
            here = CHANS * chan + q
            there = here + WINDOW // 2
            later = jnp.where(low, totals[here], totals[there]).astype(BF16)
            level = jnp.where(low, befores[here], befores[there]).astype(BF16)
            for to in range(XS):
                message[to * CHANS + chan, q] = jnp.where(x == to, level, later)
        for to in range(XS):
            message[to * CHANS + chan, WINDOW // 2] = extra


OUT_STEP = 8
OUT_CHUNKS = FRAMES // OUT_STEP


def readout_kernel(
    place, intervals_far, skip_gain, received, drives_far,
    own, near, swapped, far, frames,
    result,
    intervals, weights, direct, drives, states, written, factors, state,
    load_sem, drive_sem, store_sem, small_sem,
):
    small = [pltpu.make_async_copy(intervals_far, intervals, small_sem)]
    for copy in small:
        copy.start()
    chan, x, first = place[0], place[1], place[3] == 0

    def load(chunk):
        part = pl.ds(chunk * OUT_STEP, OUT_STEP)
        return pltpu.make_async_copy(
            frames.at[part, pl.ds(CHANS * chan, CHANS)], direct.at[part], load_sem.at[chunk]
        )

    def arrive(chunk):
        part = pl.ds(chunk * OUT_STEP, OUT_STEP)
        return pltpu.make_async_copy(drives_far.at[part], drives.at[part], drive_sem.at[chunk])

    def store(chunk):
        part = pl.ds(chunk * OUT_STEP, OUT_STEP)
        return pltpu.make_async_copy(written.at[part], result.at[part], store_sem.at[chunk])

    for chunk in range(OUT_CHUNKS):
        arrive(chunk).start()
        load(chunk).start()

    assemble(weights, own, near, swapped, far, first)
    low = low_half((WIDE, LANES))
    rates, entering = [], []
    for step in range(CHANS):
        source = lax.rem(chan + CHANS - step, CHANS)
        level = received[x * CHANS + source]
        rate = join3(level[WINDOW // 2], 6)
        spent = join3(level[WINDOW // 2], 3)
        total = jnp.zeros((WINDOW // 2, WIDE, LANES), F32)
        for other in range(XS - 1):
            earlier = received[other * CHANS + source]
            decay = jnp.exp(-join3(earlier[WINDOW // 2], 0) * rate).reshape(1, 1, LANES)
            added = decay * total + earlier[: WINDOW // 2].astype(F32)
            total = jnp.where(other < x, added, total)
        decay = jnp.exp(-spent * rate).reshape(1, 1, LANES)
        total = level[: WINDOW // 2].astype(F32) + decay * total
        swapped = swap_halves(total)
        rates.append(rate)
        entering.append(
            [jnp.where(low, total[r], swapped[r]) for r in range(WINDOW // 2)]
            + [jnp.where(low, swapped[r], total[r]) for r in range(WINDOW // 2)]
        )

    for copy in small:
        copy.wait()
    values = [intervals[t] for t in range(FRAMES)]
    low_row = low_half((1, LANES))
    for pair in range(2):
        rate = jnp.where(low_row, rates[2 * pair], rates[2 * pair + 1])
        part = slice(LANES * pair, LANES * (pair + 1))
        for half in range(2):
            some = values[HALF * half : HALF * (half + 1)]
            scaled = table(some, some) * rate
            rest = pl.ds(HALF * half, HALF)
            spread(factors.at[:, rest], 0, part, jnp.exp(-scaled))
            spread(factors.at[:, rest], 1, part, jnp.sqrt(one_minus_exp(2.0 * scaled)))
        for r in range(WINDOW):
            state[r, :, part] = jnp.where(low, entering[2 * pair][r], entering[2 * pair + 1][r])

    def convolve(chunk, carry):
        start = pl.multiple_of(chunk * OUT_STEP, OUT_STEP)
        arrive(chunk).wait()
        carried = state[...]
        for step in range(OUT_STEP):
            decay, gain = factors[0, start + step], factors[1, start + step]
            carried = decay * carried + gain * drives[start + step].astype(F32)
            states[start + step] = carried.astype(BF16)
        state[...] = carried
        size = OUT_STEP * CHANS * WIDE
        block = states[pl.ds(start, OUT_STEP)]
        taps = [block[:, i : i + CHANS].reshape(size, CH) for i in range(3)]
        operand = jnp.concatenate(taps, axis=1)
        shape = (OUT_STEP * CHANS, WIDE, CH)
        parts = []
        for j in range(3):
            weight = jnp.concatenate([weights[3 * i + j] for i in range(3)], axis=0)
            parts.append(jnp.dot(operand, weight, preferred_element_type=F32).reshape(shape))
        load(chunk).wait()
        passed = direct[pl.ds(start, OUT_STEP)].astype(F32).reshape(shape)
        total = beside(*parts) + skip_gain[...].reshape(1, 1, CH) * passed
        written[pl.ds(start, OUT_STEP)] = total.astype(BF16).reshape(OUT_STEP, CHANS, WIDE, CH)
        store(chunk).start()
        return carry

    lax.fori_loop(0, OUT_CHUNKS, convolve, 0)
    for chunk in range(OUT_CHUNKS):
        store(chunk).wait()


def in_vmem():
    return pl.BlockSpec(memory_space=pltpu.VMEM)


def in_smem():
    return pl.BlockSpec(memory_space=pltpu.SMEM)


def anywhere():
    return pl.BlockSpec(memory_space=pl.ANY)


def cost(microseconds):
    return pl.CostEstimate(
        flops=int(microseconds * 1.1e9), bytes_accessed=1 << 20, transcendentals=0
    )


def drive(intervals, rates, kernel_t, frames):
    return pl.pallas_call(
        drive_kernel,
        out_shape=jax.ShapeDtypeStruct((ZS, ROWS // 2 + 1, WIDE, LANES), BF16),
        in_specs=[anywhere()] * 4,
        out_specs=in_vmem(),
        scratch_shapes=[
            pltpu.SMEM((FRAMES,), F32),
            pltpu.VMEM((1, OWN), F32),
            pltpu.VMEM((9, OWN, CH), BF16),
            pltpu.VMEM((FRAMES, ROWS + 2, WIDE, CH), BF16),
            pltpu.VMEM((2, 3 * CH, CH), BF16),
            pltpu.VMEM((2, HALF, WIDE, LANES), F32),
            pltpu.VMEM((ROWS, WIDE, LANES), F32),
            pltpu.SemaphoreType.DMA((CHUNKS, 2)),
            pltpu.SemaphoreType.DMA((3,)),
        ],
        compiler_params=pltpu.CompilerParams(vmem_limit_bytes=60 << 20),
        cost_estimate=cost(8),
        name="drive",
    )(intervals, rates, kernel_t, frames)


def window(place, own, near, swapped, far, frames):
    return pl.pallas_call(
        window_kernel,
        out_shape=[
            jax.ShapeDtypeStruct((FRAMES, WINDOW, WIDE, CH), BF16),
            jax.ShapeDtypeStruct((8, LANES), F32),
        ],
        in_specs=[in_smem()] + [in_vmem()] * CHANS + [anywhere()],
        out_specs=[anywhere(), in_vmem()],
        scratch_shapes=[
            pltpu.VMEM((9, CHANS * OWN, CH), BF16),
            pltpu.VMEM((FRAMES, TALL, WIDE, CH), BF16),
            pltpu.VMEM((FRAMES, WINDOW, WIDE, CH), BF16),
            pltpu.SemaphoreType.DMA((WINDOW_CHUNKS,)),
            pltpu.SemaphoreType.DMA((WINDOW_CHUNKS,)),
        ],
        compiler_params=pltpu.CompilerParams(vmem_limit_bytes=52 << 20),
        cost_estimate=cost(1),
        name="window",
    )(place, own, near, swapped, far, frames)


def hold_kernel(value, *refs):
    result, sem = refs[-2:]
    copy = pltpu.make_async_copy(value, result, sem)
    copy.start()
    copy.wait()


def hold(value, others):
    return pl.pallas_call(
        hold_kernel,
        out_shape=jax.ShapeDtypeStruct(value.shape, value.dtype),
        in_specs=[anywhere()] * (1 + len(others)),
        out_specs=anywhere(),
        scratch_shapes=[pltpu.SemaphoreType.DMA],
        compiler_params=pltpu.CompilerParams(vmem_limit_bytes=16 << 20),
        cost_estimate=cost(1),
        name="hold",
    )(value, *others)


def relay(place, rates, received, token):
    return pl.pallas_call(
        relay_kernel,
        out_shape=[
            jax.ShapeDtypeStruct((XS * CHANS, WINDOW // 2 + 1, WIDE, LANES), BF16),
            jax.ShapeDtypeStruct((8, LANES), F32),
        ],
        in_specs=[in_smem(), in_vmem(), in_vmem(), anywhere()],
        out_specs=[in_vmem()] * 2,
        compiler_params=pltpu.CompilerParams(vmem_limit_bytes=16 << 20),
        cost_estimate=cost(1),
        name="relay",
    )(place, rates, received, token)


def read_out(place, intervals, skip_gain, received, drives, kernels, frames):
    return pl.pallas_call(
        readout_kernel,
        out_shape=jax.ShapeDtypeStruct((FRAMES, CHANS, WIDE, CH), BF16),
        in_specs=[in_smem(), anywhere(), in_vmem(), in_vmem(), anywhere()]
        + [in_vmem()] * CHANS
        + [anywhere()],
        out_specs=anywhere(),
        scratch_shapes=[
            pltpu.SMEM((FRAMES,), F32),
            pltpu.VMEM((9, CHANS * OWN, CH), BF16),
            pltpu.VMEM((FRAMES, CHANS, WIDE, CH), BF16),
            pltpu.VMEM((FRAMES, WINDOW, WIDE, CH), BF16),
            pltpu.VMEM((FRAMES, WINDOW, WIDE, CH), BF16),
            pltpu.VMEM((FRAMES, CHANS, WIDE, CH), BF16),
            pltpu.VMEM((2, FRAMES, WIDE, CH), F32),
            pltpu.VMEM((WINDOW, WIDE, CH), F32),
            pltpu.SemaphoreType.DMA((OUT_CHUNKS,)),
            pltpu.SemaphoreType.DMA((OUT_CHUNKS,)),
            pltpu.SemaphoreType.DMA((OUT_CHUNKS,)),
            pltpu.SemaphoreType.DMA,
        ],
        compiler_params=pltpu.CompilerParams(vmem_limit_bytes=52 << 20),
        cost_estimate=cost(6),
        name="read_out",
    )(place, intervals, skip_gain, received, drives, *kernels, frames)


def around(value):
    near = [
        (2 * c + core, 2 * ((c + step) % CHANS) + core)
        for c in range(CHANS)
        for core, step in ((0, 1), (1, CHANS - 1))
    ]
    far = [(c, (c + 2) % CHANS) for c in range(CHANS)]
    return lax.ppermute(value, ("chan", "clip"), near), lax.ppermute(value, "chan", far)


def after_kernel(*refs):
    del refs


def after(value, other, length=0):
    return pl.pallas_call(
        after_kernel,
        out_shape=jax.ShapeDtypeStruct(value.shape, value.dtype),
        in_specs=[anywhere()] * 2,
        out_specs=anywhere(),
        input_output_aliases={0: 0},
        compiler_params=pltpu.CompilerParams(vmem_limit_bytes=16 << 20),
        cost_estimate=cost(length),
        name="after",
    )(value, other)


def swap(value):
    return lax.ppermute(value, "clip", [(0, 1), (1, 0)])


def local(frames, intervals, decay_rates, in_kernel, out_kernel, skip_gain):
    axes = ("chan", "x", "z", "clip")
    place = jnp.stack([lax.axis_index(name) for name in axes]).astype(jnp.int32)
    rates = decay_rates.reshape(1, OWN)
    kernel_t = jnp.transpose(in_kernel.reshape(9, CH, OWN), (0, 2, 1))
    out_own = out_kernel.reshape(9, OWN, CH)
    in_near, in_far = around(kernel_t)
    in_far = after(in_far, in_near, 2)
    message = drive(intervals, rates, kernel_t, frames)
    arrived = lax.all_to_all(message, "z", 0, 0)
    out_near, out_far = around(hold(out_own, (in_near, in_far)))
    drives, done = window(place, kernel_t, in_near, swap(in_near), in_far, frames)
    onward, done = relay(place, rates, arrived, done)
    out_near = after(out_near, done)
    received = lax.all_to_all(onward, ("x", "chan"), 0, 0)
    received = after(received, place, 2)
    out_far = after(out_far, done, 2)
    kernels = (out_own, out_near, swap(out_near), out_far)
    skip = skip_gain.reshape(1, CH)
    return read_out(place, intervals, skip, received, drives, kernels, frames)


def solution(mesh):
    whole = jax.sharding.Mesh(
        mesh.devices.reshape(XS, ZS, CHANS, 2), ("x", "z", "chan", "clip")
    )
    time = ("clip", "x", "z")
    placed = (
        P(time, None, None, None),
        P(time),
        P("chan"),
        P(None, None, None, "chan"),
        P(None, None, "chan", None),
        P(),
    )
    return jax.shard_map(
        local,
        mesh=whole,
        in_specs=placed,
        out_specs=P(time, "chan", None, None),
        check_vma=False,
    )
```

```python
import functools

import jax
import jax.numpy as jnp
from jax import lax
from jax.experimental import pallas as pl
from jax.experimental.pallas import tpu as pltpu
from jax.sharding import PartitionSpec as P

F32 = jnp.float32
BF16 = jnp.bfloat16
FRAMES = 32
HALF = 16
ROWS = 16
WIDE = 16
CH = 256
OWN = 64
LANES = 128
CHANS = 4
ZS = 8
XS = 4
WINDOW = 6
STEP = 4
PIECES = ((0, 4), (4, 4), (8, 4), (12, 4))
CHUNKS = len(PIECES)


def split3(value):
    high = value.astype(BF16)
    rest = value - high.astype(F32)
    middle = rest.astype(BF16)
    low = (rest - middle.astype(F32)).astype(BF16)
    return high, middle, low


def join3(block, start):
    parts = block.astype(F32)
    return parts[start : start + 1] + parts[start + 1 : start + 2] + parts[start + 2 : start + 3]


def low_half(shape):
    return lax.broadcasted_iota(jnp.int32, shape, len(shape) - 1) < OWN


def swap_halves(value):
    return pltpu.roll(value, OWN, value.ndim - 1)


def doubled(rates):
    row = jnp.concatenate([rates, rates], axis=1)
    return row


def table(low_values, high_values):
    row = lax.broadcasted_iota(jnp.int32, (HALF, LANES), 0)
    low = low_half((HALF, LANES))
    result = jnp.zeros((HALF, LANES), F32)
    for t in range(HALF):
        result = jnp.where(row == t, jnp.where(low, low_values[t], high_values[t]), result)
    return result


def spread(target, index, lanes, rows):
    for t in range(HALF):
        target[index, t, :, lanes] = jnp.broadcast_to(rows[t : t + 1], (WIDE, LANES))


def one_minus_exp(value):
    series = value * (
        1.0 - value * (0.5 - value * (1.0 / 6 - value * (1.0 / 24 - value * (1.0 / 120))))
    )
    return jnp.where(value < 0.125, series, 1.0 - jnp.exp(-value))


def beside(left, centre, right):
    column = lax.broadcasted_iota(jnp.int32, centre.shape, 1)
    total = centre + jnp.where(column == 0, 0.0, pltpu.roll(left, 1, 1))
    return total + jnp.where(column == WIDE - 1, 0.0, pltpu.roll(right, WIDE - 1, 1))


def running(values):
    sums = [values[0]]
    for value in values[1:]:
        sums.append(sums[-1] + value)
    return sums


def drive_kernel(
    intervals_far, rates_far, kernel_far, frames,
    message,
    intervals, rates, kernel_t, padded, weights, factors, state, load_sem, small_sem,
):
    small = [
        pltpu.make_async_copy(source, target, small_sem.at[index])
        for index, (source, target) in enumerate(
            ((kernel_far, kernel_t), (intervals_far, intervals), (rates_far, rates))
        )
    ]
    for copy in small:
        copy.start()

    def load(chunk, half):
        first, size = PIECES[chunk]
        part = pl.ds(half * HALF + first, size)
        return pltpu.make_async_copy(
            frames.at[part],
            padded.at[part, pl.ds(1, ROWS)],
            load_sem.at[chunk, half],
        )

    load(0, 0).start()
    load(0, 1).start()

    empty = jnp.zeros((FRAMES, 1, WIDE, CH), BF16)
    padded[:, 0:1] = empty
    padded[:, ROWS + 1 : ROWS + 2] = empty
    nothing = jnp.zeros((CH, OWN), BF16)
    for copy in small:
        copy.wait()
    for chunk in range(1, CHUNKS):
        load(chunk, 0).start()
        load(chunk, 1).start()
    for i in range(3):
        tap = [kernel_t[3 * i + j].astype(F32).T.astype(BF16) for j in range(3)]
        weights[0, CH * i : CH * (i + 1), :] = jnp.concatenate([tap[0], tap[1], tap[2], nothing], 1)
        weights[1, CH * i : CH * (i + 1), :] = jnp.concatenate([tap[1], tap[0], nothing, tap[2]], 1)

    values = [intervals[t] for t in range(FRAMES)]
    rate = doubled(rates[...])
    scaled = table(values[:HALF], values[HALF:]) * rate
    spread(factors, 0, slice(None), jnp.exp(-scaled))
    spread(factors, 1, slice(None), jnp.sqrt(one_minus_exp(2.0 * scaled)))
    state[...] = jnp.zeros_like(state)

    def products(chunk):
        load(chunk, 0).wait()
        load(chunk, 1).wait()
        begin, size = PIECES[chunk]
        both = []
        for half in range(2):
            block = padded[pl.ds(half * HALF + begin, size)]
            taps = [block[:, i : i + ROWS].reshape(size * ROWS * WIDE, CH) for i in range(3)]
            both.append(
                jnp.dot(jnp.concatenate(taps, axis=1), weights[half], preferred_element_type=F32)
            )
        return both

    def advance(chunk, first, second):
        begin, size = PIECES[chunk]
        low = low_half((size * ROWS * WIDE, LANES))
        left = jnp.where(low, first[:, :LANES], second[:, :LANES])
        centre = swap_halves(jnp.where(low, second[:, :LANES], first[:, :LANES]))
        right = first[:, LANES:] + second[:, LANES:]
        shape = (size * ROWS, WIDE, LANES)
        drives = beside(left.reshape(shape), centre.reshape(shape), right.reshape(shape))
        drives = drives.reshape(size, ROWS, WIDE, LANES)
        carried = state[...]
        for step in range(size):
            now = begin + step
            carried = factors[0, now] * carried + factors[1, now] * drives[step]
        state[...] = carried

    waiting = products(0)
    for chunk in range(CHUNKS):
        ready = waiting
        if chunk + 1 < CHUNKS:
            waiting = products(chunk + 1)
        advance(chunk, *ready)

    late = functools.reduce(lambda a, b: a + b, values[HALF:])
    total = functools.reduce(lambda a, b: a + b, values[:HALF]) + late
    carried = state[...]
    end = carried + jnp.exp(-late * rate).reshape(1, 1, LANES) * swap_halves(carried)
    other = swap_halves(end)
    low = low_half((ROWS // 2, WIDE, LANES))
    packed = jnp.where(low, other[: ROWS // 2], end[ROWS // 2 :]).astype(BF16)
    row = lax.broadcasted_iota(jnp.int32, (WIDE, LANES), 0)
    pieces = split3(jnp.full((WIDE, LANES), total, F32))
    extra = jnp.zeros((WIDE, LANES), F32)
    for index, piece in enumerate(pieces):
        extra = jnp.where(row == index, piece.astype(F32), extra)
    extra = extra.astype(BF16)
    for z in range(ZS):
        message[z, : ROWS // 2] = packed
        message[z, ROWS // 2] = extra


WINDOW_STEP = 8
EARLY = 24
TALL = 12


def assemble(target, own, near, swapped, far, first):
    def tap(index, carry):
        left = jnp.where(first, near[index], swapped[index])
        right = jnp.where(first, swapped[index], near[index])
        target[index] = jnp.concatenate([own[index], left, far[index], right], axis=0)
        return carry

    lax.fori_loop(0, 9, tap, 0)


def window_kernel(
    begin, size, place, own, near, swapped, far, frames, _,
    drives, token,
    weights, rows, written, load_sem, store_sem,
):
    chunks = size // WINDOW_STEP
    chan, first = place[0], place[3] == 0
    source = jnp.clip(CHANS * chan - 2, 0, 8)
    target = source - CHANS * chan + 4

    def load(chunk):
        part = pl.ds(chunk * WINDOW_STEP, WINDOW_STEP)
        where = pl.ds(begin + chunk * WINDOW_STEP, WINDOW_STEP)
        return pltpu.make_async_copy(
            frames.at[where, pl.ds(source, 8)], rows.at[part, pl.ds(target, 8)], load_sem.at[chunk]
        )

    def store(chunk):
        part = pl.ds(chunk * WINDOW_STEP, WINDOW_STEP)
        return pltpu.make_async_copy(written.at[part], drives.at[part], store_sem.at[chunk])

    for chunk in range(chunks):
        load(chunk).start()
    empty = jnp.zeros((size, 2, WIDE, CH), BF16)

    @pl.when(chan == 0)
    def _():
        rows[:, 2:4] = empty

    @pl.when(chan == CHANS - 1)
    def _():
        rows[:, 8:10] = empty

    token[...] = jnp.zeros_like(token)
    assemble(weights, own, near, swapped, far, first)

    def convolve(chunk, carry):
        load(chunk).wait()
        start = pl.multiple_of(chunk * WINDOW_STEP, WINDOW_STEP)
        block = rows[pl.ds(start, WINDOW_STEP)]
        pixels = WINDOW_STEP * WINDOW * WIDE
        taps = [block[:, 2 + i : 2 + i + WINDOW].reshape(pixels, CH) for i in range(3)]
        operand = jnp.concatenate(taps, axis=1)
        shape = (WINDOW_STEP * WINDOW, WIDE, CH)
        dims = (((1,), (1,)), ((), ()))
        parts = []
        for j in range(3):
            weight = jnp.concatenate([weights[3 * i + j] for i in range(3)], axis=1)
            parts.append(
                lax.dot_general(operand, weight, dims, preferred_element_type=F32).reshape(shape)
            )
        total = beside(*parts).reshape(WINDOW_STEP, WINDOW, WIDE, CH)
        for r in range(WINDOW):
            kept = total[:, r]
            if r == 0:
                kept = jnp.where(chan == 0, 0.0, kept)
            if r == WINDOW - 1:
                kept = jnp.where(chan == CHANS - 1, 0.0, kept)
            written[pl.ds(start, WINDOW_STEP), r] = kept.astype(BF16)
        store(chunk).start()
        return carry

    lax.fori_loop(0, chunks, convolve, 0)
    for chunk in range(chunks):
        store(chunk).wait()


def relay_kernel(place, rates, received, token, message, done):
    x, z = place[1], place[2]
    done[...] = jnp.zeros_like(done)
    rate = doubled(rates[...])
    total = jnp.zeros((ROWS // 2, WIDE, LANES), F32)
    before = total
    elapsed = jnp.zeros((1, LANES), F32)
    elapsed_before = elapsed
    for other in range(ZS):
        mine = z == other
        before = jnp.where(mine, total, before)
        elapsed_before = jnp.where(mine, elapsed, elapsed_before)
        spent = join3(received[other, ROWS // 2], 0)
        decay = jnp.exp(-spent * rate).reshape(1, 1, LANES)
        total = decay * total + received[other, : ROWS // 2].astype(F32)
        elapsed = elapsed + spent

    low = low_half((WIDE, LANES))
    blank = jnp.zeros((WIDE, LANES), F32)

    def rows_of(value):
        swapped = swap_halves(value)
        top = [jnp.where(low, value[r], swapped[r]) for r in range(ROWS // 2)]
        bottom = [jnp.where(low, swapped[r], value[r]) for r in range(ROWS // 2)]
        return [blank] + top + bottom + [blank]

    totals, befores = rows_of(total), rows_of(before)
    row = lax.broadcasted_iota(jnp.int32, (WIDE, LANES), 0)
    extra = blank
    pieces = split3(elapsed) + split3(elapsed_before) + split3(rate)
    for index, piece in enumerate(pieces):
        extra = jnp.where(row == index, piece.astype(F32), extra)
    extra = extra.astype(BF16)
    for chan in range(CHANS):
        for q in range(WINDOW // 2):
            here = CHANS * chan + q
            there = here + WINDOW // 2
            later = jnp.where(low, totals[here], totals[there]).astype(BF16)
            level = jnp.where(low, befores[here], befores[there]).astype(BF16)
            for to in range(XS):
                message[to * CHANS + chan, q] = jnp.where(x == to, level, later)
        for to in range(XS):
            message[to * CHANS + chan, WINDOW // 2] = extra


OUT_STEP = 8
OUT_CHUNKS = FRAMES // OUT_STEP


def readout_kernel(
    place, intervals_far, skip_gain, received, early, late,
    own, near, swapped, far, frames,
    result,
    intervals, weights, direct, drives, states, written, factors, state,
    load_sem, drive_sem, store_sem, small_sem,
):
    small = [pltpu.make_async_copy(intervals_far, intervals, small_sem)]
    for copy in small:
        copy.start()
    chan, x, first = place[0], place[1], place[3] == 0

    def load(chunk):
        part = pl.ds(chunk * OUT_STEP, OUT_STEP)
        return pltpu.make_async_copy(
            frames.at[part, pl.ds(CHANS * chan, CHANS)], direct.at[part], load_sem.at[chunk]
        )

    def arrive(chunk, source=early, skipped=0):
        part = pl.ds(chunk * OUT_STEP, OUT_STEP)
        where = pl.ds(chunk * OUT_STEP - skipped, OUT_STEP)
        return pltpu.make_async_copy(source.at[where], drives.at[part], drive_sem.at[chunk])

    def arrived(chunk):
        part = drives.at[pl.ds(chunk * OUT_STEP, OUT_STEP)]
        return pltpu.make_async_copy(part, part, drive_sem.at[chunk])

    def store(chunk):
        part = pl.ds(chunk * OUT_STEP, OUT_STEP)
        return pltpu.make_async_copy(written.at[part], result.at[part], store_sem.at[chunk])

    for chunk in range(OUT_CHUNKS):
        if chunk * OUT_STEP < EARLY:
            arrive(chunk).start()
        else:
            arrive(chunk, late, EARLY).start()
        load(chunk).start()

    assemble(weights, own, near, swapped, far, first)
    low = low_half((WIDE, LANES))
    rates, entering = [], []
    for step in range(CHANS):
        source = lax.rem(chan + CHANS - step, CHANS)
        level = received[x * CHANS + source]
        rate = join3(level[WINDOW // 2], 6)
        spent = join3(level[WINDOW // 2], 3)
        total = jnp.zeros((WINDOW // 2, WIDE, LANES), F32)
        for other in range(XS - 1):
            earlier = received[other * CHANS + source]
            decay = jnp.exp(-join3(earlier[WINDOW // 2], 0) * rate).reshape(1, 1, LANES)
            added = decay * total + earlier[: WINDOW // 2].astype(F32)
            total = jnp.where(other < x, added, total)
        decay = jnp.exp(-spent * rate).reshape(1, 1, LANES)
        total = level[: WINDOW // 2].astype(F32) + decay * total
        swapped = swap_halves(total)
        rates.append(rate)
        entering.append(
            [jnp.where(low, total[r], swapped[r]) for r in range(WINDOW // 2)]
            + [jnp.where(low, swapped[r], total[r]) for r in range(WINDOW // 2)]
        )

    for copy in small:
        copy.wait()
    values = [intervals[t] for t in range(FRAMES)]
    low_row = low_half((1, LANES))
    for pair in range(2):
        rate = jnp.where(low_row, rates[2 * pair], rates[2 * pair + 1])
        part = slice(LANES * pair, LANES * (pair + 1))
        for half in range(2):
            some = values[HALF * half : HALF * (half + 1)]
            scaled = table(some, some) * rate
            rest = pl.ds(HALF * half, HALF)
            spread(factors.at[:, rest], 0, part, jnp.exp(-scaled))
            spread(factors.at[:, rest], 1, part, jnp.sqrt(one_minus_exp(2.0 * scaled)))
        for r in range(WINDOW):
            state[r, :, part] = jnp.where(low, entering[2 * pair][r], entering[2 * pair + 1][r])

    def convolve(chunk, carry):
        start = pl.multiple_of(chunk * OUT_STEP, OUT_STEP)
        arrived(chunk).wait()
        carried = state[...]
        for step in range(OUT_STEP):
            decay, gain = factors[0, start + step], factors[1, start + step]
            carried = decay * carried + gain * drives[start + step].astype(F32)
            states[start + step] = carried.astype(BF16)
        state[...] = carried
        size = OUT_STEP * CHANS * WIDE
        block = states[pl.ds(start, OUT_STEP)]
        taps = [block[:, i : i + CHANS].reshape(size, CH) for i in range(3)]
        operand = jnp.concatenate(taps, axis=1)
        shape = (OUT_STEP * CHANS, WIDE, CH)
        parts = []
        for j in range(3):
            weight = jnp.concatenate([weights[3 * i + j] for i in range(3)], axis=0)
            parts.append(jnp.dot(operand, weight, preferred_element_type=F32).reshape(shape))
        load(chunk).wait()
        passed = direct[pl.ds(start, OUT_STEP)].astype(F32).reshape(shape)
        total = beside(*parts) + skip_gain[...].reshape(1, 1, CH) * passed
        written[pl.ds(start, OUT_STEP)] = total.astype(BF16).reshape(OUT_STEP, CHANS, WIDE, CH)
        store(chunk).start()
        return carry

    lax.fori_loop(0, OUT_CHUNKS, convolve, 0)
    for chunk in range(OUT_CHUNKS):
        store(chunk).wait()


def in_vmem():
    return pl.BlockSpec(memory_space=pltpu.VMEM)


def in_smem():
    return pl.BlockSpec(memory_space=pltpu.SMEM)


def anywhere():
    return pl.BlockSpec(memory_space=pl.ANY)


def cost(microseconds):
    return pl.CostEstimate(
        flops=int(microseconds * 1.1e9), bytes_accessed=1 << 20, transcendentals=0
    )


def drive(intervals, rates, kernel_t, frames):
    return pl.pallas_call(
        drive_kernel,
        out_shape=jax.ShapeDtypeStruct((ZS, ROWS // 2 + 1, WIDE, LANES), BF16),
        in_specs=[anywhere()] * 4,
        out_specs=in_vmem(),
        scratch_shapes=[
            pltpu.SMEM((FRAMES,), F32),
            pltpu.VMEM((1, OWN), F32),
            pltpu.VMEM((9, OWN, CH), BF16),
            pltpu.VMEM((FRAMES, ROWS + 2, WIDE, CH), BF16),
            pltpu.VMEM((2, 3 * CH, CH), BF16),
            pltpu.VMEM((2, HALF, WIDE, LANES), F32),
            pltpu.VMEM((ROWS, WIDE, LANES), F32),
            pltpu.SemaphoreType.DMA((CHUNKS, 2)),
            pltpu.SemaphoreType.DMA((3,)),
        ],
        compiler_params=pltpu.CompilerParams(vmem_limit_bytes=60 << 20),
        cost_estimate=cost(8),
        name="drive",
    )(intervals, rates, kernel_t, frames)


def window(begin, size, place, own, near, swapped, far, frames, later):
    chunks = size // WINDOW_STEP
    return pl.pallas_call(
        functools.partial(window_kernel, begin, size),
        out_shape=[
            jax.ShapeDtypeStruct((size, WINDOW, WIDE, CH), BF16),
            jax.ShapeDtypeStruct((8, LANES), F32),
        ],
        in_specs=[in_smem()] + [in_vmem()] * CHANS + [anywhere()] * 2,
        out_specs=[anywhere(), in_vmem()],
        scratch_shapes=[
            pltpu.VMEM((9, CHANS * OWN, CH), BF16),
            pltpu.VMEM((size, TALL, WIDE, CH), BF16),
            pltpu.VMEM((size, WINDOW, WIDE, CH), BF16),
            pltpu.SemaphoreType.DMA((chunks,)),
            pltpu.SemaphoreType.DMA((chunks,)),
        ],
        compiler_params=pltpu.CompilerParams(vmem_limit_bytes=52 << 20),
        cost_estimate=cost(1),
        name="window",
    )(place, own, near, swapped, far, frames, later)


def hold_kernel(value, *refs):
    result, sem = refs[-2:]
    copy = pltpu.make_async_copy(value, result, sem)
    copy.start()
    copy.wait()


def hold(value, others):
    return pl.pallas_call(
        hold_kernel,
        out_shape=jax.ShapeDtypeStruct(value.shape, value.dtype),
        in_specs=[anywhere()] * (1 + len(others)),
        out_specs=anywhere(),
        scratch_shapes=[pltpu.SemaphoreType.DMA],
        compiler_params=pltpu.CompilerParams(vmem_limit_bytes=16 << 20),
        cost_estimate=cost(1),
        name="hold",
    )(value, *others)


def relay(place, rates, received, token):
    return pl.pallas_call(
        relay_kernel,
        out_shape=[
            jax.ShapeDtypeStruct((XS * CHANS, WINDOW // 2 + 1, WIDE, LANES), BF16),
            jax.ShapeDtypeStruct((8, LANES), F32),
        ],
        in_specs=[in_smem(), in_vmem(), in_vmem(), anywhere()],
        out_specs=[in_vmem()] * 2,
        compiler_params=pltpu.CompilerParams(vmem_limit_bytes=16 << 20),
        cost_estimate=cost(1),
        name="relay",
    )(place, rates, received, token)


def read_out(place, intervals, skip_gain, received, early, late, kernels, frames):
    return pl.pallas_call(
        readout_kernel,
        out_shape=jax.ShapeDtypeStruct((FRAMES, CHANS, WIDE, CH), BF16),
        in_specs=[in_smem(), anywhere(), in_vmem(), in_vmem(), anywhere(), anywhere()]
        + [in_vmem()] * CHANS
        + [anywhere()],
        out_specs=anywhere(),
        scratch_shapes=[
            pltpu.SMEM((FRAMES,), F32),
            pltpu.VMEM((9, CHANS * OWN, CH), BF16),
            pltpu.VMEM((FRAMES, CHANS, WIDE, CH), BF16),
            pltpu.VMEM((FRAMES, WINDOW, WIDE, CH), BF16),
            pltpu.VMEM((FRAMES, WINDOW, WIDE, CH), BF16),
            pltpu.VMEM((FRAMES, CHANS, WIDE, CH), BF16),
            pltpu.VMEM((2, FRAMES, WIDE, CH), F32),
            pltpu.VMEM((WINDOW, WIDE, CH), F32),
            pltpu.SemaphoreType.DMA((OUT_CHUNKS,)),
            pltpu.SemaphoreType.DMA((OUT_CHUNKS,)),
            pltpu.SemaphoreType.DMA((OUT_CHUNKS,)),
            pltpu.SemaphoreType.DMA,
        ],
        compiler_params=pltpu.CompilerParams(vmem_limit_bytes=52 << 20),
        cost_estimate=cost(6),
        name="read_out",
    )(place, intervals, skip_gain, received, early, late, *kernels, frames)


def around(value):
    near = [
        (2 * c + core, 2 * ((c + step) % CHANS) + core)
        for c in range(CHANS)
        for core, step in ((0, 1), (1, CHANS - 1))
    ]
    far = [(c, (c + 2) % CHANS) for c in range(CHANS)]
    return lax.ppermute(value, ("chan", "clip"), near), lax.ppermute(value, "chan", far)


def after_kernel(*refs):
    del refs


def after(value, other, length=0):
    return pl.pallas_call(
        after_kernel,
        out_shape=jax.ShapeDtypeStruct(value.shape, value.dtype),
        in_specs=[anywhere()] * 2,
        out_specs=anywhere(),
        input_output_aliases={0: 0},
        compiler_params=pltpu.CompilerParams(vmem_limit_bytes=16 << 20),
        cost_estimate=cost(length),
        name="after",
    )(value, other)


def swap(value):
    return lax.ppermute(value, "clip", [(0, 1), (1, 0)])


def local(frames, intervals, decay_rates, in_kernel, out_kernel, skip_gain):
    axes = ("chan", "x", "z", "clip")
    place = jnp.stack([lax.axis_index(name) for name in axes]).astype(jnp.int32)
    rates = decay_rates.reshape(1, OWN)
    kernel_t = jnp.transpose(in_kernel.reshape(9, CH, OWN), (0, 2, 1))
    out_own = out_kernel.reshape(9, OWN, CH)
    in_near, in_far = around(kernel_t)
    in_far = after(in_far, in_near, 2)
    message = drive(intervals, rates, kernel_t, frames)
    arrived = lax.all_to_all(message, "z", 0, 0)
    out_near, out_far = around(hold(out_own, (in_near, in_far)))
    pieces = (kernel_t, in_near, swap(in_near), in_far)
    early, done = window(0, EARLY, place, *pieces, frames, place)
    onward, done = relay(place, rates, arrived, done)
    late, _ = window(EARLY, FRAMES - EARLY, place, *pieces, frames, done)
    out_near = after(out_near, done)
    received = lax.all_to_all(onward, ("x", "chan"), 0, 0)
    received = after(received, place, 2)
    out_far = after(out_far, done, 2)
    kernels = (out_own, out_near, swap(out_near), out_far)
    skip = skip_gain.reshape(1, CH)
    return read_out(place, intervals, skip, received, early, late, kernels, frames)


def solution(mesh):
    whole = jax.sharding.Mesh(
        mesh.devices.reshape(XS, ZS, CHANS, 2), ("x", "z", "chan", "clip")
    )
    time = ("clip", "x", "z")
    placed = (
        P(time, None, None, None),
        P(time),
        P("chan"),
        P(None, None, None, "chan"),
        P(None, None, "chan", None),
        P(),
    )
    return jax.shard_map(
        local,
        mesh=whole,
        in_specs=placed,
        out_specs=P(time, "chan", None, None),
        check_vma=False,
    )
```

```python
import functools

import jax
import jax.numpy as jnp
from jax import lax
from jax.experimental import pallas as pl
from jax.experimental.pallas import tpu as pltpu
from jax.sharding import PartitionSpec as P

F32 = jnp.float32
BF16 = jnp.bfloat16
FRAMES = 32
HALF = 16
ROWS = 16
WIDE = 16
CH = 256
OWN = 64
LANES = 128
CHANS = 4
ZS = 8
XS = 4
WINDOW = 6
STEP = 4
PIECES = ((0, 4), (4, 4), (8, 4), (12, 4))
CHUNKS = len(PIECES)


def split3(value):
    high = value.astype(BF16)
    rest = value - high.astype(F32)
    middle = rest.astype(BF16)
    low = (rest - middle.astype(F32)).astype(BF16)
    return high, middle, low


def join3(block, start):
    parts = block.astype(F32)
    return parts[start : start + 1] + parts[start + 1 : start + 2] + parts[start + 2 : start + 3]


def low_half(shape):
    return lax.broadcasted_iota(jnp.int32, shape, len(shape) - 1) < OWN


def swap_halves(value):
    return pltpu.roll(value, OWN, value.ndim - 1)


def doubled(rates):
    row = jnp.concatenate([rates, rates], axis=1)
    return row


def table(low_values, high_values):
    row = lax.broadcasted_iota(jnp.int32, (HALF, LANES), 0)
    low = low_half((HALF, LANES))
    result = jnp.zeros((HALF, LANES), F32)
    for t in range(HALF):
        result = jnp.where(row == t, jnp.where(low, low_values[t], high_values[t]), result)
    return result


def spread(target, index, lanes, rows):
    for t in range(HALF):
        target[index, t, :, lanes] = jnp.broadcast_to(rows[t : t + 1], (WIDE, LANES))


def one_minus_exp(value):
    series = value * (
        1.0 - value * (0.5 - value * (1.0 / 6 - value * (1.0 / 24 - value * (1.0 / 120))))
    )
    return jnp.where(value < 0.125, series, 1.0 - jnp.exp(-value))


def beside(left, centre, right):
    column = lax.broadcasted_iota(jnp.int32, centre.shape, 1)
    total = centre + jnp.where(column == 0, 0.0, pltpu.roll(left, 1, 1))
    return total + jnp.where(column == WIDE - 1, 0.0, pltpu.roll(right, WIDE - 1, 1))


def running(values):
    sums = [values[0]]
    for value in values[1:]:
        sums.append(sums[-1] + value)
    return sums


def drive_kernel(
    intervals_far, rates_far, kernel_far, frames,
    message,
    intervals, rates, kernel_t, padded, weights, factors, state, load_sem, small_sem,
):
    small = [
        pltpu.make_async_copy(source, target, small_sem.at[index])
        for index, (source, target) in enumerate(
            ((kernel_far, kernel_t), (intervals_far, intervals), (rates_far, rates))
        )
    ]
    for copy in small:
        copy.start()

    def load(chunk, half):
        first, size = PIECES[chunk]
        part = pl.ds(half * HALF + first, size)
        return pltpu.make_async_copy(
            frames.at[part],
            padded.at[part, pl.ds(1, ROWS)],
            load_sem.at[chunk, half],
        )

    load(0, 0).start()
    load(0, 1).start()

    empty = jnp.zeros((FRAMES, 1, WIDE, CH), BF16)
    padded[:, 0:1] = empty
    padded[:, ROWS + 1 : ROWS + 2] = empty
    nothing = jnp.zeros((CH, OWN), BF16)
    for copy in small:
        copy.wait()
    for chunk in range(1, CHUNKS):
        load(chunk, 0).start()
        load(chunk, 1).start()
    for i in range(3):
        tap = [kernel_t[3 * i + j].astype(F32).T.astype(BF16) for j in range(3)]
        weights[0, CH * i : CH * (i + 1), :] = jnp.concatenate([tap[0], tap[1], tap[2], nothing], 1)
        weights[1, CH * i : CH * (i + 1), :] = jnp.concatenate([tap[1], tap[0], nothing, tap[2]], 1)

    values = [intervals[t] for t in range(FRAMES)]
    rate = doubled(rates[...])
    scaled = table(values[:HALF], values[HALF:]) * rate
    spread(factors, 0, slice(None), jnp.exp(-scaled))
    spread(factors, 1, slice(None), jnp.sqrt(one_minus_exp(2.0 * scaled)))
    state[...] = jnp.zeros_like(state)

    def products(chunk):
        load(chunk, 0).wait()
        load(chunk, 1).wait()
        begin, size = PIECES[chunk]
        both = []
        for half in range(2):
            block = padded[pl.ds(half * HALF + begin, size)]
            taps = [block[:, i : i + ROWS].reshape(size * ROWS * WIDE, CH) for i in range(3)]
            both.append(
                jnp.dot(jnp.concatenate(taps, axis=1), weights[half], preferred_element_type=F32)
            )
        return both

    def advance(chunk, first, second):
        begin, size = PIECES[chunk]
        low = low_half((size * ROWS * WIDE, LANES))
        left = jnp.where(low, first[:, :LANES], second[:, :LANES])
        centre = swap_halves(jnp.where(low, second[:, :LANES], first[:, :LANES]))
        right = first[:, LANES:] + second[:, LANES:]
        shape = (size * ROWS, WIDE, LANES)
        drives = beside(left.reshape(shape), centre.reshape(shape), right.reshape(shape))
        drives = drives.reshape(size, ROWS, WIDE, LANES)
        carried = state[...]
        for step in range(size):
            now = begin + step
            carried = factors[0, now] * carried + factors[1, now] * drives[step]
        state[...] = carried

    waiting = products(0)
    for chunk in range(CHUNKS):
        ready = waiting
        if chunk + 1 < CHUNKS:
            waiting = products(chunk + 1)
        advance(chunk, *ready)

    late = functools.reduce(lambda a, b: a + b, values[HALF:])
    total = functools.reduce(lambda a, b: a + b, values[:HALF]) + late
    carried = state[...]
    end = carried + jnp.exp(-late * rate).reshape(1, 1, LANES) * swap_halves(carried)
    other = swap_halves(end)
    low = low_half((ROWS // 2, WIDE, LANES))
    packed = jnp.where(low, other[: ROWS // 2], end[ROWS // 2 :]).astype(BF16)
    row = lax.broadcasted_iota(jnp.int32, (WIDE, LANES), 0)
    pieces = split3(jnp.full((WIDE, LANES), total, F32))
    extra = jnp.zeros((WIDE, LANES), F32)
    for index, piece in enumerate(pieces):
        extra = jnp.where(row == index, piece.astype(F32), extra)
    extra = extra.astype(BF16)
    for z in range(ZS):
        message[z, : ROWS // 2] = packed
        message[z, ROWS // 2] = extra


WINDOW_STEP = 8
WINDOW_CHUNKS = FRAMES // WINDOW_STEP
TALL = 12


def assemble(target, own, near, swapped, far, first):
    def tap(index, carry):
        left = jnp.where(first, near[index], swapped[index])
        right = jnp.where(first, swapped[index], near[index])
        target[index] = jnp.concatenate([own[index], left, far[index], right], axis=0)
        return carry

    lax.fori_loop(0, 9, tap, 0)


def window_kernel(
    place, own, near, swapped, far, frames, later,
    drives, token,
    weights, rows, written, load_sem, store_sem,
):
    chan, first = place[0], place[3] == 0
    source = jnp.clip(CHANS * chan - 2, 0, 8)
    target = source - CHANS * chan + 4

    def load(chunk):
        part = pl.ds(chunk * WINDOW_STEP, WINDOW_STEP)
        return pltpu.make_async_copy(
            frames.at[part, pl.ds(source, 8)], rows.at[part, pl.ds(target, 8)], load_sem.at[chunk]
        )

    def store(chunk):
        part = pl.ds(chunk * WINDOW_STEP, WINDOW_STEP)
        return pltpu.make_async_copy(written.at[part], drives.at[part], store_sem.at[chunk])

    for chunk in range(WINDOW_CHUNKS):
        load(chunk).start()
    empty = jnp.zeros((FRAMES, 2, WIDE, CH), BF16)

    @pl.when(chan == 0)
    def _():
        rows[:, 2:4] = empty

    @pl.when(chan == CHANS - 1)
    def _():
        rows[:, 8:10] = empty

    token[...] = jnp.zeros_like(token)
    assemble(weights, own, near, swapped, far, first)

    def convolve(chunk, carry):
        load(chunk).wait()
        start = pl.multiple_of(chunk * WINDOW_STEP, WINDOW_STEP)
        block = rows[pl.ds(start, WINDOW_STEP)]
        size = WINDOW_STEP * WINDOW * WIDE
        taps = [block[:, 2 + i : 2 + i + WINDOW].reshape(size, CH) for i in range(3)]
        operand = jnp.concatenate(taps, axis=1)
        shape = (WINDOW_STEP * WINDOW, WIDE, CH)
        dims = (((1,), (1,)), ((), ()))
        parts = []
        for j in range(3):
            weight = jnp.concatenate([weights[3 * i + j] for i in range(3)], axis=1)
            parts.append(
                lax.dot_general(operand, weight, dims, preferred_element_type=F32).reshape(shape)
            )
        total = beside(*parts).reshape(WINDOW_STEP, WINDOW, WIDE, CH)
        for r in range(WINDOW):
            kept = total[:, r]
            if r == 0:
                kept = jnp.where(chan == 0, 0.0, kept)
            if r == WINDOW - 1:
                kept = jnp.where(chan == CHANS - 1, 0.0, kept)
            written[pl.ds(start, WINDOW_STEP), r] = kept.astype(BF16)
        store(chunk).start()
        return carry

    lax.fori_loop(0, WINDOW_CHUNKS, convolve, 0)
    for chunk in range(WINDOW_CHUNKS):
        store(chunk).wait()


def relay_kernel(place, rates, received, token, later, message):
    x, z = place[1], place[2]
    rate = doubled(rates[...])
    total = jnp.zeros((ROWS // 2, WIDE, LANES), F32)
    before = total
    elapsed = jnp.zeros((1, LANES), F32)
    elapsed_before = elapsed
    for other in range(ZS):
        mine = z == other
        before = jnp.where(mine, total, before)
        elapsed_before = jnp.where(mine, elapsed, elapsed_before)
        spent = join3(received[other, ROWS // 2], 0)
        decay = jnp.exp(-spent * rate).reshape(1, 1, LANES)
        total = decay * total + received[other, : ROWS // 2].astype(F32)
        elapsed = elapsed + spent

    low = low_half((WIDE, LANES))
    blank = jnp.zeros((WIDE, LANES), F32)

    def rows_of(value):
        swapped = swap_halves(value)
        top = [jnp.where(low, value[r], swapped[r]) for r in range(ROWS // 2)]
        bottom = [jnp.where(low, swapped[r], value[r]) for r in range(ROWS // 2)]
        return [blank] + top + bottom + [blank]

    totals, befores = rows_of(total), rows_of(before)
    row = lax.broadcasted_iota(jnp.int32, (WIDE, LANES), 0)
    extra = blank
    pieces = split3(elapsed) + split3(elapsed_before) + split3(rate)
    for index, piece in enumerate(pieces):
        extra = jnp.where(row == index, piece.astype(F32), extra)
    extra = extra.astype(BF16)
    for chan in range(CHANS):
        for q in range(WINDOW // 2):
            here = CHANS * chan + q
            there = here + WINDOW // 2
            later = jnp.where(low, totals[here], totals[there]).astype(BF16)
            level = jnp.where(low, befores[here], befores[there]).astype(BF16)
            for to in range(XS):
                message[to * CHANS + chan, q] = jnp.where(x == to, level, later)
        for to in range(XS):
            message[to * CHANS + chan, WINDOW // 2] = extra


OUT_STEP = 8
OUT_CHUNKS = FRAMES // OUT_STEP


def readout_kernel(
    place, intervals_far, skip_gain, received, drives_far,
    own, near, swapped, far, frames,
    result,
    intervals, weights, direct, drives, states, written, factors, state,
    load_sem, drive_sem, store_sem, small_sem,
):
    small = [pltpu.make_async_copy(intervals_far, intervals, small_sem)]
    for copy in small:
        copy.start()
    chan, x, first = place[0], place[1], place[3] == 0

    def load(chunk):
        part = pl.ds(chunk * OUT_STEP, OUT_STEP)
        return pltpu.make_async_copy(
            frames.at[part, pl.ds(CHANS * chan, CHANS)], direct.at[part], load_sem.at[chunk]
        )

    def arrive(chunk):
        part = pl.ds(chunk * OUT_STEP, OUT_STEP)
        return pltpu.make_async_copy(drives_far.at[part], drives.at[part], drive_sem.at[chunk])

    def store(chunk):
        part = pl.ds(chunk * OUT_STEP, OUT_STEP)
        return pltpu.make_async_copy(written.at[part], result.at[part], store_sem.at[chunk])

    for chunk in range(OUT_CHUNKS):
        arrive(chunk).start()
        load(chunk).start()

    assemble(weights, own, near, swapped, far, first)
    low = low_half((WIDE, LANES))
    rates, entering = [], []
    for step in range(CHANS):
        source = lax.rem(chan + CHANS - step, CHANS)
        level = received[x * CHANS + source]
        rate = join3(level[WINDOW // 2], 6)
        spent = join3(level[WINDOW // 2], 3)
        total = jnp.zeros((WINDOW // 2, WIDE, LANES), F32)
        for other in range(XS - 1):
            earlier = received[other * CHANS + source]
            decay = jnp.exp(-join3(earlier[WINDOW // 2], 0) * rate).reshape(1, 1, LANES)
            added = decay * total + earlier[: WINDOW // 2].astype(F32)
            total = jnp.where(other < x, added, total)
        decay = jnp.exp(-spent * rate).reshape(1, 1, LANES)
        total = level[: WINDOW // 2].astype(F32) + decay * total
        swapped = swap_halves(total)
        rates.append(rate)
        entering.append(
            [jnp.where(low, total[r], swapped[r]) for r in range(WINDOW // 2)]
            + [jnp.where(low, swapped[r], total[r]) for r in range(WINDOW // 2)]
        )

    for copy in small:
        copy.wait()
    values = [intervals[t] for t in range(FRAMES)]
    low_row = low_half((1, LANES))
    for pair in range(2):
        rate = jnp.where(low_row, rates[2 * pair], rates[2 * pair + 1])
        part = slice(LANES * pair, LANES * (pair + 1))
        for half in range(2):
            some = values[HALF * half : HALF * (half + 1)]
            scaled = table(some, some) * rate
            rest = pl.ds(HALF * half, HALF)
            spread(factors.at[:, rest], 0, part, jnp.exp(-scaled))
            spread(factors.at[:, rest], 1, part, jnp.sqrt(one_minus_exp(2.0 * scaled)))
        for r in range(WINDOW):
            state[r, :, part] = jnp.where(low, entering[2 * pair][r], entering[2 * pair + 1][r])

    def convolve(chunk, carry):
        start = pl.multiple_of(chunk * OUT_STEP, OUT_STEP)
        arrive(chunk).wait()
        carried = state[...]
        for step in range(OUT_STEP):
            decay, gain = factors[0, start + step], factors[1, start + step]
            carried = decay * carried + gain * drives[start + step].astype(F32)
            states[start + step] = carried.astype(BF16)
        state[...] = carried
        size = OUT_STEP * CHANS * WIDE
        block = states[pl.ds(start, OUT_STEP)]
        taps = [block[:, i : i + CHANS].reshape(size, CH) for i in range(3)]
        operand = jnp.concatenate(taps, axis=1)
        shape = (OUT_STEP * CHANS, WIDE, CH)
        parts = []
        for j in range(3):
            weight = jnp.concatenate([weights[3 * i + j] for i in range(3)], axis=0)
            parts.append(jnp.dot(operand, weight, preferred_element_type=F32).reshape(shape))
        load(chunk).wait()
        passed = direct[pl.ds(start, OUT_STEP)].astype(F32).reshape(shape)
        total = beside(*parts) + skip_gain[...].reshape(1, 1, CH) * passed
        written[pl.ds(start, OUT_STEP)] = total.astype(BF16).reshape(OUT_STEP, CHANS, WIDE, CH)
        store(chunk).start()
        return carry

    lax.fori_loop(0, OUT_CHUNKS, convolve, 0)
    for chunk in range(OUT_CHUNKS):
        store(chunk).wait()


def in_vmem():
    return pl.BlockSpec(memory_space=pltpu.VMEM)


def in_smem():
    return pl.BlockSpec(memory_space=pltpu.SMEM)


def anywhere():
    return pl.BlockSpec(memory_space=pl.ANY)


def cost(microseconds):
    return pl.CostEstimate(
        flops=int(microseconds * 1.1e9), bytes_accessed=1 << 20, transcendentals=0
    )


def drive(intervals, rates, kernel_t, frames):
    return pl.pallas_call(
        drive_kernel,
        out_shape=jax.ShapeDtypeStruct((ZS, ROWS // 2 + 1, WIDE, LANES), BF16),
        in_specs=[anywhere()] * 4,
        out_specs=in_vmem(),
        scratch_shapes=[
            pltpu.SMEM((FRAMES,), F32),
            pltpu.VMEM((1, OWN), F32),
            pltpu.VMEM((9, OWN, CH), BF16),
            pltpu.VMEM((FRAMES, ROWS + 2, WIDE, CH), BF16),
            pltpu.VMEM((2, 3 * CH, CH), BF16),
            pltpu.VMEM((2, HALF, WIDE, LANES), F32),
            pltpu.VMEM((ROWS, WIDE, LANES), F32),
            pltpu.SemaphoreType.DMA((CHUNKS, 2)),
            pltpu.SemaphoreType.DMA((3,)),
        ],
        compiler_params=pltpu.CompilerParams(vmem_limit_bytes=60 << 20),
        cost_estimate=cost(8),
        name="drive",
    )(intervals, rates, kernel_t, frames)


def window(place, own, near, swapped, far, frames, later):
    return pl.pallas_call(
        window_kernel,
        out_shape=[
            jax.ShapeDtypeStruct((FRAMES, WINDOW, WIDE, CH), BF16),
            jax.ShapeDtypeStruct((8, LANES), F32),
        ],
        in_specs=[in_smem()] + [in_vmem()] * CHANS + [anywhere()] * 2,
        out_specs=[anywhere(), in_vmem()],
        scratch_shapes=[
            pltpu.VMEM((9, CHANS * OWN, CH), BF16),
            pltpu.VMEM((FRAMES, TALL, WIDE, CH), BF16),
            pltpu.VMEM((FRAMES, WINDOW, WIDE, CH), BF16),
            pltpu.SemaphoreType.DMA((WINDOW_CHUNKS,)),
            pltpu.SemaphoreType.DMA((WINDOW_CHUNKS,)),
        ],
        compiler_params=pltpu.CompilerParams(vmem_limit_bytes=52 << 20),
        cost_estimate=cost(1),
        name="window",
    )(place, own, near, swapped, far, frames, later)


def relay(place, rates, received, token, later):
    return pl.pallas_call(
        relay_kernel,
        out_shape=jax.ShapeDtypeStruct((XS * CHANS, WINDOW // 2 + 1, WIDE, LANES), BF16),
        in_specs=[in_smem(), in_vmem(), in_vmem(), anywhere(), anywhere()],
        out_specs=in_vmem(),
        compiler_params=pltpu.CompilerParams(vmem_limit_bytes=16 << 20),
        cost_estimate=cost(1),
        name="relay",
    )(place, rates, received, token, later)


def read_out(place, intervals, skip_gain, received, drives, kernels, frames):
    return pl.pallas_call(
        readout_kernel,
        out_shape=jax.ShapeDtypeStruct((FRAMES, CHANS, WIDE, CH), BF16),
        in_specs=[in_smem(), anywhere(), in_vmem(), in_vmem(), anywhere()]
        + [in_vmem()] * CHANS
        + [anywhere()],
        out_specs=anywhere(),
        scratch_shapes=[
            pltpu.SMEM((FRAMES,), F32),
            pltpu.VMEM((9, CHANS * OWN, CH), BF16),
            pltpu.VMEM((FRAMES, CHANS, WIDE, CH), BF16),
            pltpu.VMEM((FRAMES, WINDOW, WIDE, CH), BF16),
            pltpu.VMEM((FRAMES, WINDOW, WIDE, CH), BF16),
            pltpu.VMEM((FRAMES, CHANS, WIDE, CH), BF16),
            pltpu.VMEM((2, FRAMES, WIDE, CH), F32),
            pltpu.VMEM((WINDOW, WIDE, CH), F32),
            pltpu.SemaphoreType.DMA((OUT_CHUNKS,)),
            pltpu.SemaphoreType.DMA((OUT_CHUNKS,)),
            pltpu.SemaphoreType.DMA((OUT_CHUNKS,)),
            pltpu.SemaphoreType.DMA,
        ],
        compiler_params=pltpu.CompilerParams(vmem_limit_bytes=52 << 20),
        cost_estimate=cost(6),
        name="read_out",
    )(place, intervals, skip_gain, received, drives, *kernels, frames)


def neighbour(value):
    route = [
        (2 * c + core, 2 * ((c + step) % CHANS) + core)
        for c in range(CHANS)
        for core, step in ((0, 1), (1, CHANS - 1))
    ]
    return lax.ppermute(value, ("chan", "clip"), route)


def opposite(value):
    return lax.ppermute(value, "chan", [(c, (c + 2) % CHANS) for c in range(CHANS)])


def after_kernel(*refs):
    del refs


def after(value, other, length=0):
    return pl.pallas_call(
        after_kernel,
        out_shape=jax.ShapeDtypeStruct(value.shape, value.dtype),
        in_specs=[anywhere()] * 2,
        out_specs=anywhere(),
        input_output_aliases={0: 0},
        compiler_params=pltpu.CompilerParams(vmem_limit_bytes=16 << 20),
        cost_estimate=cost(length),
        name="after",
    )(value, other)


def swap(value):
    return lax.ppermute(value, "clip", [(0, 1), (1, 0)])


def local(frames, intervals, decay_rates, in_kernel, out_kernel, skip_gain):
    axes = ("chan", "x", "z", "clip")
    place = jnp.stack([lax.axis_index(name) for name in axes]).astype(jnp.int32)
    rates = decay_rates.reshape(1, OWN)
    kernel_t = jnp.transpose(in_kernel.reshape(9, CH, OWN), (0, 2, 1))
    out_own = out_kernel.reshape(9, OWN, CH)
    near, out_near = neighbour(kernel_t), neighbour(out_own)
    far = opposite(kernel_t)
    message = drive(intervals, rates, kernel_t, frames)
    arrived = lax.all_to_all(message, "z", 0, 0)
    pieces = (kernel_t, near, swap(near), after(far, near, 2))
    out_pieces = (out_own, out_near, swap(out_near), neighbour(out_near))
    drives, done = window(place, *pieces, frames, out_pieces[2])
    onward = relay(place, rates, arrived, done, out_pieces[3])
    received = lax.all_to_all(onward, ("x", "chan"), 0, 0)
    skip = skip_gain.reshape(1, CH)
    return read_out(place, intervals, skip, received, drives, out_pieces, frames)


def solution(mesh):
    whole = jax.sharding.Mesh(
        mesh.devices.reshape(XS, ZS, CHANS, 2), ("x", "z", "chan", "clip")
    )
    time = ("clip", "x", "z")
    placed = (
        P(time, None, None, None),
        P(time),
        P("chan"),
        P(None, None, None, "chan"),
        P(None, None, "chan", None),
        P(),
    )
    return jax.shard_map(
        local,
        mesh=whole,
        in_specs=placed,
        out_specs=P(time, "chan", None, None),
        check_vma=False,
    )
```

```python
import functools

import jax
import jax.numpy as jnp
from jax import lax
from jax.experimental import pallas as pl
from jax.experimental.pallas import tpu as pltpu
from jax.sharding import PartitionSpec as P

F32 = jnp.float32
BF16 = jnp.bfloat16
FRAMES = 32
HALF = 16
ROWS = 16
WIDE = 16
CH = 256
OWN = 64
LANES = 128
CHANS = 4
ZS = 8
XS = 4
WINDOW = 6
STEP = 4
PIECES = ((0, 4), (4, 4), (8, 4), (12, 4))
CHUNKS = len(PIECES)


def split3(value):
    high = value.astype(BF16)
    rest = value - high.astype(F32)
    middle = rest.astype(BF16)
    low = (rest - middle.astype(F32)).astype(BF16)
    return high, middle, low


def join3(block, start):
    parts = block.astype(F32)
    return parts[start : start + 1] + parts[start + 1 : start + 2] + parts[start + 2 : start + 3]


def low_half(shape):
    return lax.broadcasted_iota(jnp.int32, shape, len(shape) - 1) < OWN


def swap_halves(value):
    return pltpu.roll(value, OWN, value.ndim - 1)


def doubled(rates):
    row = jnp.concatenate([rates, rates], axis=1)
    return row


def table(low_values, high_values):
    row = lax.broadcasted_iota(jnp.int32, (HALF, LANES), 0)
    low = low_half((HALF, LANES))
    result = jnp.zeros((HALF, LANES), F32)
    for t in range(HALF):
        result = jnp.where(row == t, jnp.where(low, low_values[t], high_values[t]), result)
    return result


def spread(target, index, lanes, rows):
    for t in range(HALF):
        target[index, t, :, lanes] = jnp.broadcast_to(rows[t : t + 1], (WIDE, LANES))


def one_minus_exp(value):
    series = value * (
        1.0 - value * (0.5 - value * (1.0 / 6 - value * (1.0 / 24 - value * (1.0 / 120))))
    )
    return jnp.where(value < 0.125, series, 1.0 - jnp.exp(-value))


def beside(left, centre, right):
    column = lax.broadcasted_iota(jnp.int32, centre.shape, 1)
    total = centre + jnp.where(column == 0, 0.0, pltpu.roll(left, 1, 1))
    return total + jnp.where(column == WIDE - 1, 0.0, pltpu.roll(right, WIDE - 1, 1))


def running(values):
    sums = [values[0]]
    for value in values[1:]:
        sums.append(sums[-1] + value)
    return sums


def drive_kernel(
    intervals_far, rates_far, kernel_far, frames,
    message,
    intervals, rates, kernel_t, padded, weights, factors, state, load_sem, small_sem,
):
    small = [
        pltpu.make_async_copy(source, target, small_sem.at[index])
        for index, (source, target) in enumerate(
            ((kernel_far, kernel_t), (intervals_far, intervals), (rates_far, rates))
        )
    ]
    for copy in small:
        copy.start()

    def load(chunk, half):
        first, size = PIECES[chunk]
        part = pl.ds(half * HALF + first, size)
        return pltpu.make_async_copy(
            frames.at[part],
            padded.at[part, pl.ds(1, ROWS)],
            load_sem.at[chunk, half],
        )

    load(0, 0).start()
    load(0, 1).start()

    empty = jnp.zeros((FRAMES, 1, WIDE, CH), BF16)
    padded[:, 0:1] = empty
    padded[:, ROWS + 1 : ROWS + 2] = empty
    nothing = jnp.zeros((CH, OWN), BF16)
    for copy in small:
        copy.wait()
    for chunk in range(1, CHUNKS):
        load(chunk, 0).start()
        load(chunk, 1).start()
    for i in range(3):
        tap = [kernel_t[3 * i + j].astype(F32).T.astype(BF16) for j in range(3)]
        weights[0, CH * i : CH * (i + 1), :] = jnp.concatenate([tap[0], tap[1], tap[2], nothing], 1)
        weights[1, CH * i : CH * (i + 1), :] = jnp.concatenate([tap[1], tap[0], nothing, tap[2]], 1)

    values = [intervals[t] for t in range(FRAMES)]
    rate = doubled(rates[...])
    scaled = table(values[:HALF], values[HALF:]) * rate
    spread(factors, 0, slice(None), jnp.exp(-scaled))
    spread(factors, 1, slice(None), jnp.sqrt(one_minus_exp(2.0 * scaled)))
    state[...] = jnp.zeros_like(state)

    def products(chunk):
        load(chunk, 0).wait()
        load(chunk, 1).wait()
        begin, size = PIECES[chunk]
        both = []
        for half in range(2):
            block = padded[pl.ds(half * HALF + begin, size)]
            taps = [block[:, i : i + ROWS].reshape(size * ROWS * WIDE, CH) for i in range(3)]
            both.append(
                jnp.dot(jnp.concatenate(taps, axis=1), weights[half], preferred_element_type=F32)
            )
        return both

    def advance(chunk, first, second):
        begin, size = PIECES[chunk]
        low = low_half((size * ROWS * WIDE, LANES))
        left = jnp.where(low, first[:, :LANES], second[:, :LANES])
        centre = swap_halves(jnp.where(low, second[:, :LANES], first[:, :LANES]))
        right = first[:, LANES:] + second[:, LANES:]
        shape = (size * ROWS, WIDE, LANES)
        drives = beside(left.reshape(shape), centre.reshape(shape), right.reshape(shape))
        drives = drives.reshape(size, ROWS, WIDE, LANES)
        carried = state[...]
        for step in range(size):
            now = begin + step
            carried = factors[0, now] * carried + factors[1, now] * drives[step]
        state[...] = carried

    waiting = products(0)
    for chunk in range(CHUNKS):
        ready = waiting
        if chunk + 1 < CHUNKS:
            waiting = products(chunk + 1)
        advance(chunk, *ready)

    late = functools.reduce(lambda a, b: a + b, values[HALF:])
    total = functools.reduce(lambda a, b: a + b, values[:HALF]) + late
    carried = state[...]
    end = carried + jnp.exp(-late * rate).reshape(1, 1, LANES) * swap_halves(carried)
    other = swap_halves(end)
    low = low_half((ROWS // 2, WIDE, LANES))
    packed = jnp.where(low, other[: ROWS // 2], end[ROWS // 2 :]).astype(BF16)
    row = lax.broadcasted_iota(jnp.int32, (WIDE, LANES), 0)
    pieces = split3(jnp.full((WIDE, LANES), total, F32))
    extra = jnp.zeros((WIDE, LANES), F32)
    for index, piece in enumerate(pieces):
        extra = jnp.where(row == index, piece.astype(F32), extra)
    extra = extra.astype(BF16)
    for z in range(ZS):
        message[z, : ROWS // 2] = packed
        message[z, ROWS // 2] = extra


WINDOW_STEP = 8
WINDOW_CHUNKS = FRAMES // WINDOW_STEP
TALL = 12


def assemble(target, own, near, swapped, far, first):
    def tap(index, carry):
        left = jnp.where(first, near[index], swapped[index])
        right = jnp.where(first, swapped[index], near[index])
        target[index] = jnp.concatenate([own[index], left, far[index], right], axis=0)
        return carry

    lax.fori_loop(0, 9, tap, 0)


def window_kernel(
    place, own, near, swapped, far, frames, later,
    drives, token,
    weights, rows, written, load_sem, store_sem,
):
    chan, first = place[0], place[3] == 0
    source = jnp.clip(CHANS * chan - 2, 0, 8)
    target = source - CHANS * chan + 4

    def load(chunk):
        part = pl.ds(chunk * WINDOW_STEP, WINDOW_STEP)
        return pltpu.make_async_copy(
            frames.at[part, pl.ds(source, 8)], rows.at[part, pl.ds(target, 8)], load_sem.at[chunk]
        )

    def store(chunk):
        part = pl.ds(chunk * WINDOW_STEP, WINDOW_STEP)
        return pltpu.make_async_copy(written.at[part], drives.at[part], store_sem.at[chunk])

    for chunk in range(WINDOW_CHUNKS):
        load(chunk).start()
    empty = jnp.zeros((FRAMES, 2, WIDE, CH), BF16)

    @pl.when(chan == 0)
    def _():
        rows[:, 2:4] = empty

    @pl.when(chan == CHANS - 1)
    def _():
        rows[:, 8:10] = empty

    token[...] = jnp.zeros_like(token)
    assemble(weights, own, near, swapped, far, first)

    def convolve(chunk, carry):
        load(chunk).wait()
        start = pl.multiple_of(chunk * WINDOW_STEP, WINDOW_STEP)
        block = rows[pl.ds(start, WINDOW_STEP)]
        size = WINDOW_STEP * WINDOW * WIDE
        taps = [block[:, 2 + i : 2 + i + WINDOW].reshape(size, CH) for i in range(3)]
        operand = jnp.concatenate(taps, axis=1)
        shape = (WINDOW_STEP * WINDOW, WIDE, CH)
        dims = (((1,), (1,)), ((), ()))
        parts = []
        for j in range(3):
            weight = jnp.concatenate([weights[3 * i + j] for i in range(3)], axis=1)
            parts.append(
                lax.dot_general(operand, weight, dims, preferred_element_type=F32).reshape(shape)
            )
        total = beside(*parts).reshape(WINDOW_STEP, WINDOW, WIDE, CH)
        for r in range(WINDOW):
            kept = total[:, r]
            if r == 0:
                kept = jnp.where(chan == 0, 0.0, kept)
            if r == WINDOW - 1:
                kept = jnp.where(chan == CHANS - 1, 0.0, kept)
            written[pl.ds(start, WINDOW_STEP), r] = kept.astype(BF16)
        store(chunk).start()
        return carry

    lax.fori_loop(0, WINDOW_CHUNKS, convolve, 0)
    for chunk in range(WINDOW_CHUNKS):
        store(chunk).wait()


def relay_kernel(place, rates, received, token, later, message):
    x, z = place[1], place[2]
    rate = doubled(rates[...])
    total = jnp.zeros((ROWS // 2, WIDE, LANES), F32)
    before = total
    elapsed = jnp.zeros((1, LANES), F32)
    elapsed_before = elapsed
    for other in range(ZS):
        mine = z == other
        before = jnp.where(mine, total, before)
        elapsed_before = jnp.where(mine, elapsed, elapsed_before)
        spent = join3(received[ZS - 1 - other, ROWS // 2], 0)
        decay = jnp.exp(-spent * rate).reshape(1, 1, LANES)
        total = decay * total + received[ZS - 1 - other, : ROWS // 2].astype(F32)
        elapsed = elapsed + spent

    low = low_half((WIDE, LANES))
    blank = jnp.zeros((WIDE, LANES), F32)

    def rows_of(value):
        swapped = swap_halves(value)
        top = [jnp.where(low, value[r], swapped[r]) for r in range(ROWS // 2)]
        bottom = [jnp.where(low, swapped[r], value[r]) for r in range(ROWS // 2)]
        return [blank] + top + bottom + [blank]

    totals, befores = rows_of(total), rows_of(before)
    row = lax.broadcasted_iota(jnp.int32, (WIDE, LANES), 0)
    extra = blank
    pieces = split3(elapsed) + split3(elapsed_before) + split3(rate)
    for index, piece in enumerate(pieces):
        extra = jnp.where(row == index, piece.astype(F32), extra)
    extra = extra.astype(BF16)
    for chan in range(CHANS):
        for q in range(WINDOW // 2):
            here = CHANS * chan + q
            there = here + WINDOW // 2
            later = jnp.where(low, totals[here], totals[there]).astype(BF16)
            level = jnp.where(low, befores[here], befores[there]).astype(BF16)
            for to in range(XS):
                message[to * CHANS + chan, q] = jnp.where(x == to, level, later)
        for to in range(XS):
            message[to * CHANS + chan, WINDOW // 2] = extra


OUT_STEP = 8
OUT_CHUNKS = FRAMES // OUT_STEP


def readout_kernel(
    place, intervals_far, skip_gain, received, drives_far,
    own, near, swapped, far, frames,
    result,
    intervals, weights, direct, drives, states, written, factors, state,
    load_sem, drive_sem, store_sem, small_sem,
):
    small = [pltpu.make_async_copy(intervals_far, intervals, small_sem)]
    for copy in small:
        copy.start()
    chan, x, first = place[0], place[1], place[3] == 0

    def load(chunk):
        part = pl.ds(chunk * OUT_STEP, OUT_STEP)
        return pltpu.make_async_copy(
            frames.at[part, pl.ds(CHANS * chan, CHANS)], direct.at[part], load_sem.at[chunk]
        )

    def arrive(chunk):
        part = pl.ds(chunk * OUT_STEP, OUT_STEP)
        return pltpu.make_async_copy(drives_far.at[part], drives.at[part], drive_sem.at[chunk])

    def store(chunk):
        part = pl.ds(chunk * OUT_STEP, OUT_STEP)
        return pltpu.make_async_copy(written.at[part], result.at[part], store_sem.at[chunk])

    for chunk in range(OUT_CHUNKS):
        arrive(chunk).start()
        load(chunk).start()

    assemble(weights, own, near, swapped, far, first)
    low = low_half((WIDE, LANES))
    rates, entering = [], []
    for step in range(CHANS):
        source = lax.rem(chan + CHANS - step, CHANS)
        level = received[x * CHANS + source]
        rate = join3(level[WINDOW // 2], 6)
        spent = join3(level[WINDOW // 2], 3)
        total = jnp.zeros((WINDOW // 2, WIDE, LANES), F32)
        for other in range(XS - 1):
            earlier = received[other * CHANS + source]
            decay = jnp.exp(-join3(earlier[WINDOW // 2], 0) * rate).reshape(1, 1, LANES)
            added = decay * total + earlier[: WINDOW // 2].astype(F32)
            total = jnp.where(other < x, added, total)
        decay = jnp.exp(-spent * rate).reshape(1, 1, LANES)
        total = level[: WINDOW // 2].astype(F32) + decay * total
        swapped = swap_halves(total)
        rates.append(rate)
        entering.append(
            [jnp.where(low, total[r], swapped[r]) for r in range(WINDOW // 2)]
            + [jnp.where(low, swapped[r], total[r]) for r in range(WINDOW // 2)]
        )

    for copy in small:
        copy.wait()
    values = [intervals[t] for t in range(FRAMES)]
    low_row = low_half((1, LANES))
    for pair in range(2):
        rate = jnp.where(low_row, rates[2 * pair], rates[2 * pair + 1])
        part = slice(LANES * pair, LANES * (pair + 1))
        for half in range(2):
            some = values[HALF * half : HALF * (half + 1)]
            scaled = table(some, some) * rate
            rest = pl.ds(HALF * half, HALF)
            spread(factors.at[:, rest], 0, part, jnp.exp(-scaled))
            spread(factors.at[:, rest], 1, part, jnp.sqrt(one_minus_exp(2.0 * scaled)))
        for r in range(WINDOW):
            state[r, :, part] = jnp.where(low, entering[2 * pair][r], entering[2 * pair + 1][r])

    def convolve(chunk, carry):
        start = pl.multiple_of(chunk * OUT_STEP, OUT_STEP)
        arrive(chunk).wait()
        carried = state[...]
        for step in range(OUT_STEP):
            decay, gain = factors[0, start + step], factors[1, start + step]
            carried = decay * carried + gain * drives[start + step].astype(F32)
            states[start + step] = carried.astype(BF16)
        state[...] = carried
        size = OUT_STEP * CHANS * WIDE
        block = states[pl.ds(start, OUT_STEP)]
        taps = [block[:, i : i + CHANS].reshape(size, CH) for i in range(3)]
        operand = jnp.concatenate(taps, axis=1)
        shape = (OUT_STEP * CHANS, WIDE, CH)
        parts = []
        for j in range(3):
            weight = jnp.concatenate([weights[3 * i + j] for i in range(3)], axis=0)
            parts.append(jnp.dot(operand, weight, preferred_element_type=F32).reshape(shape))
        load(chunk).wait()
        passed = direct[pl.ds(start, OUT_STEP)].astype(F32).reshape(shape)
        total = beside(*parts) + skip_gain[...].reshape(1, 1, CH) * passed
        written[pl.ds(start, OUT_STEP)] = total.astype(BF16).reshape(OUT_STEP, CHANS, WIDE, CH)
        store(chunk).start()
        return carry

    lax.fori_loop(0, OUT_CHUNKS, convolve, 0)
    for chunk in range(OUT_CHUNKS):
        store(chunk).wait()


def in_vmem():
    return pl.BlockSpec(memory_space=pltpu.VMEM)


def in_smem():
    return pl.BlockSpec(memory_space=pltpu.SMEM)


def anywhere():
    return pl.BlockSpec(memory_space=pl.ANY)


def cost(microseconds):
    return pl.CostEstimate(
        flops=int(microseconds * 1.1e9), bytes_accessed=1 << 20, transcendentals=0
    )


def drive(intervals, rates, kernel_t, frames):
    return pl.pallas_call(
        drive_kernel,
        out_shape=jax.ShapeDtypeStruct((ZS, ROWS // 2 + 1, WIDE, LANES), BF16),
        in_specs=[anywhere()] * 4,
        out_specs=in_vmem(),
        scratch_shapes=[
            pltpu.SMEM((FRAMES,), F32),
            pltpu.VMEM((1, OWN), F32),
            pltpu.VMEM((9, OWN, CH), BF16),
            pltpu.VMEM((FRAMES, ROWS + 2, WIDE, CH), BF16),
            pltpu.VMEM((2, 3 * CH, CH), BF16),
            pltpu.VMEM((2, HALF, WIDE, LANES), F32),
            pltpu.VMEM((ROWS, WIDE, LANES), F32),
            pltpu.SemaphoreType.DMA((CHUNKS, 2)),
            pltpu.SemaphoreType.DMA((3,)),
        ],
        compiler_params=pltpu.CompilerParams(vmem_limit_bytes=60 << 20),
        cost_estimate=cost(8),
        name="drive",
    )(intervals, rates, kernel_t, frames)


def window(place, own, near, swapped, far, frames, later):
    return pl.pallas_call(
        window_kernel,
        out_shape=[
            jax.ShapeDtypeStruct((FRAMES, WINDOW, WIDE, CH), BF16),
            jax.ShapeDtypeStruct((8, LANES), F32),
        ],
        in_specs=[in_smem()] + [in_vmem()] * CHANS + [anywhere()] * 2,
        out_specs=[anywhere(), in_vmem()],
        scratch_shapes=[
            pltpu.VMEM((9, CHANS * OWN, CH), BF16),
            pltpu.VMEM((FRAMES, TALL, WIDE, CH), BF16),
            pltpu.VMEM((FRAMES, WINDOW, WIDE, CH), BF16),
            pltpu.SemaphoreType.DMA((WINDOW_CHUNKS,)),
            pltpu.SemaphoreType.DMA((WINDOW_CHUNKS,)),
        ],
        compiler_params=pltpu.CompilerParams(vmem_limit_bytes=52 << 20),
        cost_estimate=cost(1),
        name="window",
    )(place, own, near, swapped, far, frames, later)


def relay(place, rates, received, token, later):
    return pl.pallas_call(
        relay_kernel,
        out_shape=jax.ShapeDtypeStruct((XS * CHANS, WINDOW // 2 + 1, WIDE, LANES), BF16),
        in_specs=[in_smem(), in_vmem(), in_vmem(), anywhere(), anywhere()],
        out_specs=in_vmem(),
        compiler_params=pltpu.CompilerParams(vmem_limit_bytes=16 << 20),
        cost_estimate=cost(1),
        name="relay",
    )(place, rates, received, token, later)


def read_out(place, intervals, skip_gain, received, drives, kernels, frames):
    return pl.pallas_call(
        readout_kernel,
        out_shape=jax.ShapeDtypeStruct((FRAMES, CHANS, WIDE, CH), BF16),
        in_specs=[in_smem(), anywhere(), in_vmem(), in_vmem(), anywhere()]
        + [in_vmem()] * CHANS
        + [anywhere()],
        out_specs=anywhere(),
        scratch_shapes=[
            pltpu.SMEM((FRAMES,), F32),
            pltpu.VMEM((9, CHANS * OWN, CH), BF16),
            pltpu.VMEM((FRAMES, CHANS, WIDE, CH), BF16),
            pltpu.VMEM((FRAMES, WINDOW, WIDE, CH), BF16),
            pltpu.VMEM((FRAMES, WINDOW, WIDE, CH), BF16),
            pltpu.VMEM((FRAMES, CHANS, WIDE, CH), BF16),
            pltpu.VMEM((2, FRAMES, WIDE, CH), F32),
            pltpu.VMEM((WINDOW, WIDE, CH), F32),
            pltpu.SemaphoreType.DMA((OUT_CHUNKS,)),
            pltpu.SemaphoreType.DMA((OUT_CHUNKS,)),
            pltpu.SemaphoreType.DMA((OUT_CHUNKS,)),
            pltpu.SemaphoreType.DMA,
        ],
        compiler_params=pltpu.CompilerParams(vmem_limit_bytes=52 << 20),
        cost_estimate=cost(6),
        name="read_out",
    )(place, intervals, skip_gain, received, drives, *kernels, frames)


def neighbour(value):
    route = [
        (2 * c + core, 2 * ((c + step) % CHANS) + core)
        for c in range(CHANS)
        for core, step in ((0, 1), (1, CHANS - 1))
    ]
    return lax.ppermute(value, ("chan", "clip"), route)


def opposite(value):
    return lax.ppermute(value, "chan", [(c, (c + 2) % CHANS) for c in range(CHANS)])


def after_kernel(*refs):
    del refs


def after(value, other, length=0):
    return pl.pallas_call(
        after_kernel,
        out_shape=jax.ShapeDtypeStruct(value.shape, value.dtype),
        in_specs=[anywhere()] * 2,
        out_specs=anywhere(),
        input_output_aliases={0: 0},
        compiler_params=pltpu.CompilerParams(vmem_limit_bytes=16 << 20),
        cost_estimate=cost(length),
        name="after",
    )(value, other)


def swap(value):
    return lax.ppermute(value, "clip", [(0, 1), (1, 0)])


def local(frames, intervals, decay_rates, in_kernel, out_kernel, skip_gain):
    axes = ("chan", "x", "z", "clip")
    place = jnp.stack([lax.axis_index(name) for name in axes]).astype(jnp.int32)
    rates = decay_rates.reshape(1, OWN)
    kernel_t = jnp.transpose(in_kernel.reshape(9, CH, OWN), (0, 2, 1))
    out_own = out_kernel.reshape(9, OWN, CH)
    near, out_near = neighbour(kernel_t), neighbour(out_own)
    far = opposite(kernel_t)
    message = drive(intervals, rates, kernel_t, frames)
    backwards = [list(reversed(range(ZS)))]
    arrived = lax.all_to_all(message, "z", 0, 0, axis_index_groups=backwards)
    pieces = (kernel_t, near, swap(near), after(far, near, 2))
    out_pieces = (out_own, out_near, swap(out_near), neighbour(out_near))
    drives, done = window(place, *pieces, frames, out_pieces[2])
    onward = relay(place, rates, arrived, done, out_pieces[3])
    received = lax.all_to_all(onward, ("x", "chan"), 0, 0)
    skip = skip_gain.reshape(1, CH)
    return read_out(place, intervals, skip, received, drives, out_pieces, frames)


def solution(mesh):
    whole = jax.sharding.Mesh(
        mesh.devices.reshape(XS, ZS, CHANS, 2), ("x", "z", "chan", "clip")
    )
    time = ("clip", "x", "z")
    placed = (
        P(time, None, None, None),
        P(time),
        P("chan"),
        P(None, None, None, "chan"),
        P(None, None, "chan", None),
        P(),
    )
    return jax.shard_map(
        local,
        mesh=whole,
        in_specs=placed,
        out_specs=P(time, "chan", None, None),
        check_vma=False,
    )
```

```python
import functools

import jax
import jax.numpy as jnp
from jax import lax
from jax.experimental import pallas as pl
from jax.experimental.pallas import tpu as pltpu
from jax.sharding import PartitionSpec as P

F32 = jnp.float32
BF16 = jnp.bfloat16
FRAMES = 32
HALF = 16
ROWS = 16
WIDE = 16
CH = 256
OWN = 64
LANES = 128
CHANS = 4
ZS = 8
XS = 4
WINDOW = 6
LAST = XS * CHANS - 1
STEP = 4
PIECES = ((0, 4), (4, 4), (8, 4), (12, 4))
CHUNKS = len(PIECES)


def split3(value):
    high = value.astype(BF16)
    rest = value - high.astype(F32)
    middle = rest.astype(BF16)
    low = (rest - middle.astype(F32)).astype(BF16)
    return high, middle, low


def join3(block, start):
    parts = block.astype(F32)
    return parts[start : start + 1] + parts[start + 1 : start + 2] + parts[start + 2 : start + 3]


def low_half(shape):
    return lax.broadcasted_iota(jnp.int32, shape, len(shape) - 1) < OWN


def swap_halves(value):
    return pltpu.roll(value, OWN, value.ndim - 1)


def doubled(rates):
    row = jnp.concatenate([rates, rates], axis=1)
    return row


def table(low_values, high_values):
    row = lax.broadcasted_iota(jnp.int32, (HALF, LANES), 0)
    low = low_half((HALF, LANES))
    result = jnp.zeros((HALF, LANES), F32)
    for t in range(HALF):
        result = jnp.where(row == t, jnp.where(low, low_values[t], high_values[t]), result)
    return result


def spread(target, index, lanes, rows):
    for t in range(HALF):
        target[index, t, :, lanes] = jnp.broadcast_to(rows[t : t + 1], (WIDE, LANES))


def one_minus_exp(value):
    series = value * (
        1.0 - value * (0.5 - value * (1.0 / 6 - value * (1.0 / 24 - value * (1.0 / 120))))
    )
    return jnp.where(value < 0.125, series, 1.0 - jnp.exp(-value))


def beside(left, centre, right):
    column = lax.broadcasted_iota(jnp.int32, centre.shape, 1)
    total = centre + jnp.where(column == 0, 0.0, pltpu.roll(left, 1, 1))
    return total + jnp.where(column == WIDE - 1, 0.0, pltpu.roll(right, WIDE - 1, 1))


def running(values):
    sums = [values[0]]
    for value in values[1:]:
        sums.append(sums[-1] + value)
    return sums


def drive_kernel(
    intervals_far, rates_far, kernel_far, frames,
    message,
    intervals, rates, kernel_t, padded, weights, factors, state, load_sem, small_sem,
):
    small = [
        pltpu.make_async_copy(source, target, small_sem.at[index])
        for index, (source, target) in enumerate(
            ((kernel_far, kernel_t), (intervals_far, intervals), (rates_far, rates))
        )
    ]
    for copy in small:
        copy.start()

    def load(chunk, half):
        first, size = PIECES[chunk]
        part = pl.ds(half * HALF + first, size)
        return pltpu.make_async_copy(
            frames.at[part],
            padded.at[part, pl.ds(1, ROWS)],
            load_sem.at[chunk, half],
        )

    load(0, 0).start()
    load(0, 1).start()

    empty = jnp.zeros((FRAMES, 1, WIDE, CH), BF16)
    padded[:, 0:1] = empty
    padded[:, ROWS + 1 : ROWS + 2] = empty
    nothing = jnp.zeros((CH, OWN), BF16)
    for copy in small:
        copy.wait()
    for chunk in range(1, CHUNKS):
        load(chunk, 0).start()
        load(chunk, 1).start()
    for i in range(3):
        tap = [kernel_t[3 * i + j].astype(F32).T.astype(BF16) for j in range(3)]
        weights[0, CH * i : CH * (i + 1), :] = jnp.concatenate([tap[0], tap[1], tap[2], nothing], 1)
        weights[1, CH * i : CH * (i + 1), :] = jnp.concatenate([tap[1], tap[0], nothing, tap[2]], 1)

    values = [intervals[t] for t in range(FRAMES)]
    rate = doubled(rates[...])
    scaled = table(values[:HALF], values[HALF:]) * rate
    spread(factors, 0, slice(None), jnp.exp(-scaled))
    spread(factors, 1, slice(None), jnp.sqrt(one_minus_exp(2.0 * scaled)))
    state[...] = jnp.zeros_like(state)

    def products(chunk):
        load(chunk, 0).wait()
        load(chunk, 1).wait()
        begin, size = PIECES[chunk]
        both = []
        for half in range(2):
            block = padded[pl.ds(half * HALF + begin, size)]
            taps = [block[:, i : i + ROWS].reshape(size * ROWS * WIDE, CH) for i in range(3)]
            both.append(
                jnp.dot(jnp.concatenate(taps, axis=1), weights[half], preferred_element_type=F32)
            )
        return both

    def advance(chunk, first, second):
        begin, size = PIECES[chunk]
        low = low_half((size * ROWS * WIDE, LANES))
        left = jnp.where(low, first[:, :LANES], second[:, :LANES])
        centre = swap_halves(jnp.where(low, second[:, :LANES], first[:, :LANES]))
        right = first[:, LANES:] + second[:, LANES:]
        shape = (size * ROWS, WIDE, LANES)
        drives = beside(left.reshape(shape), centre.reshape(shape), right.reshape(shape))
        drives = drives.reshape(size, ROWS, WIDE, LANES)
        carried = state[...]
        for step in range(size):
            now = begin + step
            carried = factors[0, now] * carried + factors[1, now] * drives[step]
        state[...] = carried

    waiting = products(0)
    for chunk in range(CHUNKS):
        ready = waiting
        if chunk + 1 < CHUNKS:
            waiting = products(chunk + 1)
        advance(chunk, *ready)

    late = functools.reduce(lambda a, b: a + b, values[HALF:])
    total = functools.reduce(lambda a, b: a + b, values[:HALF]) + late
    carried = state[...]
    end = carried + jnp.exp(-late * rate).reshape(1, 1, LANES) * swap_halves(carried)
    other = swap_halves(end)
    low = low_half((ROWS // 2, WIDE, LANES))
    packed = jnp.where(low, other[: ROWS // 2], end[ROWS // 2 :]).astype(BF16)
    row = lax.broadcasted_iota(jnp.int32, (WIDE, LANES), 0)
    pieces = split3(jnp.full((WIDE, LANES), total, F32))
    extra = jnp.zeros((WIDE, LANES), F32)
    for index, piece in enumerate(pieces):
        extra = jnp.where(row == index, piece.astype(F32), extra)
    extra = extra.astype(BF16)
    for z in range(ZS):
        message[z, : ROWS // 2] = packed
        message[z, ROWS // 2] = extra


WINDOW_STEP = 8
WINDOW_CHUNKS = FRAMES // WINDOW_STEP
TALL = 12


def assemble(target, own, near, swapped, far, first):
    def tap(index, carry):
        left = jnp.where(first, near[index], swapped[index])
        right = jnp.where(first, swapped[index], near[index])
        target[index] = jnp.concatenate([own[index], left, far[index], right], axis=0)
        return carry

    lax.fori_loop(0, 9, tap, 0)


def window_kernel(
    place, own, near, swapped, far, frames, later,
    drives, token,
    weights, rows, written, load_sem, store_sem,
):
    chan, first = place[0], place[3] == 0
    source = jnp.clip(CHANS * chan - 2, 0, 8)
    target = source - CHANS * chan + 4

    def load(chunk):
        part = pl.ds(chunk * WINDOW_STEP, WINDOW_STEP)
        return pltpu.make_async_copy(
            frames.at[part, pl.ds(source, 8)], rows.at[part, pl.ds(target, 8)], load_sem.at[chunk]
        )

    def store(chunk):
        part = pl.ds(chunk * WINDOW_STEP, WINDOW_STEP)
        return pltpu.make_async_copy(written.at[part], drives.at[part], store_sem.at[chunk])

    for chunk in range(WINDOW_CHUNKS):
        load(chunk).start()
    empty = jnp.zeros((FRAMES, 2, WIDE, CH), BF16)

    @pl.when(chan == 0)
    def _():
        rows[:, 2:4] = empty

    @pl.when(chan == CHANS - 1)
    def _():
        rows[:, 8:10] = empty

    token[...] = jnp.zeros_like(token)
    assemble(weights, own, near, swapped, far, first)

    def convolve(chunk, carry):
        load(chunk).wait()
        start = pl.multiple_of(chunk * WINDOW_STEP, WINDOW_STEP)
        block = rows[pl.ds(start, WINDOW_STEP)]
        size = WINDOW_STEP * WINDOW * WIDE
        taps = [block[:, 2 + i : 2 + i + WINDOW].reshape(size, CH) for i in range(3)]
        operand = jnp.concatenate(taps, axis=1)
        shape = (WINDOW_STEP * WINDOW, WIDE, CH)
        dims = (((1,), (1,)), ((), ()))
        parts = []
        for j in range(3):
            weight = jnp.concatenate([weights[3 * i + j] for i in range(3)], axis=1)
            parts.append(
                lax.dot_general(operand, weight, dims, preferred_element_type=F32).reshape(shape)
            )
        total = beside(*parts).reshape(WINDOW_STEP, WINDOW, WIDE, CH)
        for r in range(WINDOW):
            kept = total[:, r]
            if r == 0:
                kept = jnp.where(chan == 0, 0.0, kept)
            if r == WINDOW - 1:
                kept = jnp.where(chan == CHANS - 1, 0.0, kept)
            written[pl.ds(start, WINDOW_STEP), r] = kept.astype(BF16)
        store(chunk).start()
        return carry

    lax.fori_loop(0, WINDOW_CHUNKS, convolve, 0)
    for chunk in range(WINDOW_CHUNKS):
        store(chunk).wait()


def relay_kernel(place, rates, received, token, later, message):
    x, z = place[1], place[2]
    rate = doubled(rates[...])
    total = jnp.zeros((ROWS // 2, WIDE, LANES), F32)
    before = total
    elapsed = jnp.zeros((1, LANES), F32)
    elapsed_before = elapsed
    for other in range(ZS):
        mine = z == other
        before = jnp.where(mine, total, before)
        elapsed_before = jnp.where(mine, elapsed, elapsed_before)
        spent = join3(received[ZS - 1 - other, ROWS // 2], 0)
        decay = jnp.exp(-spent * rate).reshape(1, 1, LANES)
        total = decay * total + received[ZS - 1 - other, : ROWS // 2].astype(F32)
        elapsed = elapsed + spent

    low = low_half((WIDE, LANES))
    blank = jnp.zeros((WIDE, LANES), F32)

    def rows_of(value):
        swapped = swap_halves(value)
        top = [jnp.where(low, value[r], swapped[r]) for r in range(ROWS // 2)]
        bottom = [jnp.where(low, swapped[r], value[r]) for r in range(ROWS // 2)]
        return [blank] + top + bottom + [blank]

    totals, befores = rows_of(total), rows_of(before)
    row = lax.broadcasted_iota(jnp.int32, (WIDE, LANES), 0)
    extra = blank
    pieces = split3(elapsed) + split3(elapsed_before) + split3(rate)
    for index, piece in enumerate(pieces):
        extra = jnp.where(row == index, piece.astype(F32), extra)
    extra = extra.astype(BF16)
    for chan in range(CHANS):
        for q in range(WINDOW // 2):
            here = CHANS * chan + q
            there = here + WINDOW // 2
            later = jnp.where(low, totals[here], totals[there]).astype(BF16)
            level = jnp.where(low, befores[here], befores[there]).astype(BF16)
            for to in range(XS):
                message[LAST - to * CHANS - chan, q] = jnp.where(x == to, level, later)
        for to in range(XS):
            message[LAST - to * CHANS - chan, WINDOW // 2] = extra


OUT_STEP = 8
OUT_CHUNKS = FRAMES // OUT_STEP


def readout_kernel(
    place, intervals_far, skip_gain, received, drives_far,
    own, near, swapped, far, frames,
    result,
    intervals, weights, direct, drives, states, written, factors, state,
    load_sem, drive_sem, store_sem, small_sem,
):
    small = [pltpu.make_async_copy(intervals_far, intervals, small_sem)]
    for copy in small:
        copy.start()
    chan, x, first = place[0], place[1], place[3] == 0

    def load(chunk):
        part = pl.ds(chunk * OUT_STEP, OUT_STEP)
        return pltpu.make_async_copy(
            frames.at[part, pl.ds(CHANS * chan, CHANS)], direct.at[part], load_sem.at[chunk]
        )

    def arrive(chunk):
        part = pl.ds(chunk * OUT_STEP, OUT_STEP)
        return pltpu.make_async_copy(drives_far.at[part], drives.at[part], drive_sem.at[chunk])

    def store(chunk):
        part = pl.ds(chunk * OUT_STEP, OUT_STEP)
        return pltpu.make_async_copy(written.at[part], result.at[part], store_sem.at[chunk])

    for chunk in range(OUT_CHUNKS):
        arrive(chunk).start()
        load(chunk).start()

    assemble(weights, own, near, swapped, far, first)
    low = low_half((WIDE, LANES))
    rates, entering = [], []
    for step in range(CHANS):
        source = lax.rem(chan + CHANS - step, CHANS)
        level = received[LAST - x * CHANS - source]
        rate = join3(level[WINDOW // 2], 6)
        spent = join3(level[WINDOW // 2], 3)
        total = jnp.zeros((WINDOW // 2, WIDE, LANES), F32)
        for other in range(XS - 1):
            earlier = received[LAST - other * CHANS - source]
            decay = jnp.exp(-join3(earlier[WINDOW // 2], 0) * rate).reshape(1, 1, LANES)
            added = decay * total + earlier[: WINDOW // 2].astype(F32)
            total = jnp.where(other < x, added, total)
        decay = jnp.exp(-spent * rate).reshape(1, 1, LANES)
        total = level[: WINDOW // 2].astype(F32) + decay * total
        swapped = swap_halves(total)
        rates.append(rate)
        entering.append(
            [jnp.where(low, total[r], swapped[r]) for r in range(WINDOW // 2)]
            + [jnp.where(low, swapped[r], total[r]) for r in range(WINDOW // 2)]
        )

    for copy in small:
        copy.wait()
    values = [intervals[t] for t in range(FRAMES)]
    low_row = low_half((1, LANES))
    for pair in range(2):
        rate = jnp.where(low_row, rates[2 * pair], rates[2 * pair + 1])
        part = slice(LANES * pair, LANES * (pair + 1))
        for half in range(2):
            some = values[HALF * half : HALF * (half + 1)]
            scaled = table(some, some) * rate
            rest = pl.ds(HALF * half, HALF)
            spread(factors.at[:, rest], 0, part, jnp.exp(-scaled))
            spread(factors.at[:, rest], 1, part, jnp.sqrt(one_minus_exp(2.0 * scaled)))
        for r in range(WINDOW):
            state[r, :, part] = jnp.where(low, entering[2 * pair][r], entering[2 * pair + 1][r])

    def convolve(chunk, carry):
        start = pl.multiple_of(chunk * OUT_STEP, OUT_STEP)
        arrive(chunk).wait()
        carried = state[...]
        for step in range(OUT_STEP):
            decay, gain = factors[0, start + step], factors[1, start + step]
            carried = decay * carried + gain * drives[start + step].astype(F32)
            states[start + step] = carried.astype(BF16)
        state[...] = carried
        size = OUT_STEP * CHANS * WIDE
        block = states[pl.ds(start, OUT_STEP)]
        taps = [block[:, i : i + CHANS].reshape(size, CH) for i in range(3)]
        operand = jnp.concatenate(taps, axis=1)
        shape = (OUT_STEP * CHANS, WIDE, CH)
        parts = []
        for j in range(3):
            weight = jnp.concatenate([weights[3 * i + j] for i in range(3)], axis=0)
            parts.append(jnp.dot(operand, weight, preferred_element_type=F32).reshape(shape))
        load(chunk).wait()
        passed = direct[pl.ds(start, OUT_STEP)].astype(F32).reshape(shape)
        total = beside(*parts) + skip_gain[...].reshape(1, 1, CH) * passed
        written[pl.ds(start, OUT_STEP)] = total.astype(BF16).reshape(OUT_STEP, CHANS, WIDE, CH)
        store(chunk).start()
        return carry

    lax.fori_loop(0, OUT_CHUNKS, convolve, 0)
    for chunk in range(OUT_CHUNKS):
        store(chunk).wait()


def in_vmem():
    return pl.BlockSpec(memory_space=pltpu.VMEM)


def in_smem():
    return pl.BlockSpec(memory_space=pltpu.SMEM)


def anywhere():
    return pl.BlockSpec(memory_space=pl.ANY)


def cost(microseconds):
    return pl.CostEstimate(
        flops=int(microseconds * 1.1e9), bytes_accessed=1 << 20, transcendentals=0
    )


def drive(intervals, rates, kernel_t, frames):
    return pl.pallas_call(
        drive_kernel,
        out_shape=jax.ShapeDtypeStruct((ZS, ROWS // 2 + 1, WIDE, LANES), BF16),
        in_specs=[anywhere()] * 4,
        out_specs=in_vmem(),
        scratch_shapes=[
            pltpu.SMEM((FRAMES,), F32),
            pltpu.VMEM((1, OWN), F32),
            pltpu.VMEM((9, OWN, CH), BF16),
            pltpu.VMEM((FRAMES, ROWS + 2, WIDE, CH), BF16),
            pltpu.VMEM((2, 3 * CH, CH), BF16),
            pltpu.VMEM((2, HALF, WIDE, LANES), F32),
            pltpu.VMEM((ROWS, WIDE, LANES), F32),
            pltpu.SemaphoreType.DMA((CHUNKS, 2)),
            pltpu.SemaphoreType.DMA((3,)),
        ],
        compiler_params=pltpu.CompilerParams(vmem_limit_bytes=60 << 20),
        cost_estimate=cost(8),
        name="drive",
    )(intervals, rates, kernel_t, frames)


def window(place, own, near, swapped, far, frames, later):
    return pl.pallas_call(
        window_kernel,
        out_shape=[
            jax.ShapeDtypeStruct((FRAMES, WINDOW, WIDE, CH), BF16),
            jax.ShapeDtypeStruct((8, LANES), F32),
        ],
        in_specs=[in_smem()] + [in_vmem()] * CHANS + [anywhere()] * 2,
        out_specs=[anywhere(), in_vmem()],
        scratch_shapes=[
            pltpu.VMEM((9, CHANS * OWN, CH), BF16),
            pltpu.VMEM((FRAMES, TALL, WIDE, CH), BF16),
            pltpu.VMEM((FRAMES, WINDOW, WIDE, CH), BF16),
            pltpu.SemaphoreType.DMA((WINDOW_CHUNKS,)),
            pltpu.SemaphoreType.DMA((WINDOW_CHUNKS,)),
        ],
        compiler_params=pltpu.CompilerParams(vmem_limit_bytes=52 << 20),
        cost_estimate=cost(1),
        name="window",
    )(place, own, near, swapped, far, frames, later)


def relay(place, rates, received, token, later):
    return pl.pallas_call(
        relay_kernel,
        out_shape=jax.ShapeDtypeStruct((XS * CHANS, WINDOW // 2 + 1, WIDE, LANES), BF16),
        in_specs=[in_smem(), in_vmem(), in_vmem(), anywhere(), anywhere()],
        out_specs=in_vmem(),
        compiler_params=pltpu.CompilerParams(vmem_limit_bytes=16 << 20),
        cost_estimate=cost(1),
        name="relay",
    )(place, rates, received, token, later)


def read_out(place, intervals, skip_gain, received, drives, kernels, frames):
    return pl.pallas_call(
        readout_kernel,
        out_shape=jax.ShapeDtypeStruct((FRAMES, CHANS, WIDE, CH), BF16),
        in_specs=[in_smem(), anywhere(), in_vmem(), in_vmem(), anywhere()]
        + [in_vmem()] * CHANS
        + [anywhere()],
        out_specs=anywhere(),
        scratch_shapes=[
            pltpu.SMEM((FRAMES,), F32),
            pltpu.VMEM((9, CHANS * OWN, CH), BF16),
            pltpu.VMEM((FRAMES, CHANS, WIDE, CH), BF16),
            pltpu.VMEM((FRAMES, WINDOW, WIDE, CH), BF16),
            pltpu.VMEM((FRAMES, WINDOW, WIDE, CH), BF16),
            pltpu.VMEM((FRAMES, CHANS, WIDE, CH), BF16),
            pltpu.VMEM((2, FRAMES, WIDE, CH), F32),
            pltpu.VMEM((WINDOW, WIDE, CH), F32),
            pltpu.SemaphoreType.DMA((OUT_CHUNKS,)),
            pltpu.SemaphoreType.DMA((OUT_CHUNKS,)),
            pltpu.SemaphoreType.DMA((OUT_CHUNKS,)),
            pltpu.SemaphoreType.DMA,
        ],
        compiler_params=pltpu.CompilerParams(vmem_limit_bytes=52 << 20),
        cost_estimate=cost(6),
        name="read_out",
    )(place, intervals, skip_gain, received, drives, *kernels, frames)


def neighbour(value):
    route = [
        (2 * c + core, 2 * ((c + step) % CHANS) + core)
        for c in range(CHANS)
        for core, step in ((0, 1), (1, CHANS - 1))
    ]
    return lax.ppermute(value, ("chan", "clip"), route)


def opposite(value):
    return lax.ppermute(value, "chan", [(c, (c + 2) % CHANS) for c in range(CHANS)])


def after_kernel(*refs):
    del refs


def after(value, other, length=0):
    return pl.pallas_call(
        after_kernel,
        out_shape=jax.ShapeDtypeStruct(value.shape, value.dtype),
        in_specs=[anywhere()] * 2,
        out_specs=anywhere(),
        input_output_aliases={0: 0},
        compiler_params=pltpu.CompilerParams(vmem_limit_bytes=16 << 20),
        cost_estimate=cost(length),
        name="after",
    )(value, other)


def swap(value):
    return lax.ppermute(value, "clip", [(0, 1), (1, 0)])


def local(frames, intervals, decay_rates, in_kernel, out_kernel, skip_gain):
    axes = ("chan", "x", "z", "clip")
    place = jnp.stack([lax.axis_index(name) for name in axes]).astype(jnp.int32)
    rates = decay_rates.reshape(1, OWN)
    kernel_t = jnp.transpose(in_kernel.reshape(9, CH, OWN), (0, 2, 1))
    out_own = out_kernel.reshape(9, OWN, CH)
    near, out_near = neighbour(kernel_t), neighbour(out_own)
    far = opposite(kernel_t)
    message = drive(intervals, rates, kernel_t, frames)
    backwards = [list(reversed(range(ZS)))]
    arrived = lax.all_to_all(message, "z", 0, 0, axis_index_groups=backwards)
    pieces = (kernel_t, near, swap(near), after(far, near, 2))
    out_pieces = (out_own, out_near, swap(out_near), neighbour(out_near))
    drives, done = window(place, *pieces, frames, out_pieces[2])
    onward = relay(place, rates, arrived, done, out_pieces[3])
    backwards = [list(reversed(range(XS * CHANS)))]
    received = lax.all_to_all(onward, ("x", "chan"), 0, 0, axis_index_groups=backwards)
    skip = skip_gain.reshape(1, CH)
    return read_out(place, intervals, skip, received, drives, out_pieces, frames)


def solution(mesh):
    whole = jax.sharding.Mesh(
        mesh.devices.reshape(XS, ZS, CHANS, 2), ("x", "z", "chan", "clip")
    )
    time = ("clip", "x", "z")
    placed = (
        P(time, None, None, None),
        P(time),
        P("chan"),
        P(None, None, None, "chan"),
        P(None, None, "chan", None),
        P(),
    )
    return jax.shard_map(
        local,
        mesh=whole,
        in_specs=placed,
        out_specs=P(time, "chan", None, None),
        check_vma=False,
    )
```

```python
import functools

import jax
import jax.numpy as jnp
from jax import lax
from jax.experimental import pallas as pl
from jax.experimental.pallas import tpu as pltpu
from jax.sharding import PartitionSpec as P

F32 = jnp.float32
BF16 = jnp.bfloat16
FRAMES = 32
HALF = 16
ROWS = 16
WIDE = 16
CH = 256
OWN = 64
LANES = 128
CHANS = 4
ZS = 8
XS = 4
WINDOW = 6
LAST = XS * CHANS - 1
STEP = 4
PIECES = ((0, 4), (4, 4), (8, 4), (12, 4))
CHUNKS = len(PIECES)


def split3(value):
    high = value.astype(BF16)
    rest = value - high.astype(F32)
    middle = rest.astype(BF16)
    low = (rest - middle.astype(F32)).astype(BF16)
    return high, middle, low


def join3(block, start):
    parts = block.astype(F32)
    return parts[start : start + 1] + parts[start + 1 : start + 2] + parts[start + 2 : start + 3]


def low_half(shape):
    return lax.broadcasted_iota(jnp.int32, shape, len(shape) - 1) < OWN


def swap_halves(value):
    return pltpu.roll(value, OWN, value.ndim - 1)


def doubled(rates):
    row = jnp.concatenate([rates, rates], axis=1)
    return row


def table(low_values, high_values):
    row = lax.broadcasted_iota(jnp.int32, (HALF, LANES), 0)
    low = low_half((HALF, LANES))
    result = jnp.zeros((HALF, LANES), F32)
    for t in range(HALF):
        result = jnp.where(row == t, jnp.where(low, low_values[t], high_values[t]), result)
    return result


def spread(target, index, lanes, rows):
    for t in range(HALF):
        target[index, t, :, lanes] = jnp.broadcast_to(rows[t : t + 1], (WIDE, LANES))


def one_minus_exp(value):
    series = value * (
        1.0 - value * (0.5 - value * (1.0 / 6 - value * (1.0 / 24 - value * (1.0 / 120))))
    )
    return jnp.where(value < 0.125, series, 1.0 - jnp.exp(-value))


def beside(left, centre, right):
    column = lax.broadcasted_iota(jnp.int32, centre.shape, 1)
    total = centre + jnp.where(column == 0, 0.0, pltpu.roll(left, 1, 1))
    return total + jnp.where(column == WIDE - 1, 0.0, pltpu.roll(right, WIDE - 1, 1))


def running(values):
    sums = [values[0]]
    for value in values[1:]:
        sums.append(sums[-1] + value)
    return sums


def drive_kernel(
    intervals_far, rates_far, kernel_far, frames,
    message,
    intervals, rates, kernel_t, padded, weights, factors, state, load_sem, small_sem,
):
    small = [
        pltpu.make_async_copy(source, target, small_sem.at[index])
        for index, (source, target) in enumerate(
            ((kernel_far, kernel_t), (intervals_far, intervals), (rates_far, rates))
        )
    ]
    for copy in small:
        copy.start()

    def load(chunk, half):
        first, size = PIECES[chunk]
        part = pl.ds(half * HALF + first, size)
        return pltpu.make_async_copy(
            frames.at[part],
            padded.at[part, pl.ds(1, ROWS)],
            load_sem.at[chunk, half],
        )

    load(0, 0).start()
    load(0, 1).start()

    empty = jnp.zeros((FRAMES, 1, WIDE, CH), BF16)
    padded[:, 0:1] = empty
    padded[:, ROWS + 1 : ROWS + 2] = empty
    nothing = jnp.zeros((CH, OWN), BF16)
    for copy in small:
        copy.wait()
    for chunk in range(1, CHUNKS):
        load(chunk, 0).start()
        load(chunk, 1).start()
    for i in range(3):
        tap = [kernel_t[3 * i + j].astype(F32).T.astype(BF16) for j in range(3)]
        weights[0, CH * i : CH * (i + 1), :] = jnp.concatenate([tap[0], tap[1], tap[2], nothing], 1)
        weights[1, CH * i : CH * (i + 1), :] = jnp.concatenate([tap[1], tap[0], nothing, tap[2]], 1)

    values = [intervals[t] for t in range(FRAMES)]
    rate = doubled(rates[...])
    scaled = table(values[:HALF], values[HALF:]) * rate
    spread(factors, 0, slice(None), jnp.exp(-scaled))
    spread(factors, 1, slice(None), jnp.sqrt(one_minus_exp(2.0 * scaled)))
    state[...] = jnp.zeros_like(state)

    def products(chunk):
        load(chunk, 0).wait()
        load(chunk, 1).wait()
        begin, size = PIECES[chunk]
        both = []
        for half in range(2):
            block = padded[pl.ds(half * HALF + begin, size)]
            taps = [block[:, i : i + ROWS].reshape(size * ROWS * WIDE, CH) for i in range(3)]
            both.append(
                jnp.dot(jnp.concatenate(taps, axis=1), weights[half], preferred_element_type=F32)
            )
        return both

    def advance(chunk, first, second):
        begin, size = PIECES[chunk]
        low = low_half((size * ROWS * WIDE, LANES))
        left = jnp.where(low, first[:, :LANES], second[:, :LANES])
        centre = swap_halves(jnp.where(low, second[:, :LANES], first[:, :LANES]))
        right = first[:, LANES:] + second[:, LANES:]
        shape = (size * ROWS, WIDE, LANES)
        drives = beside(left.reshape(shape), centre.reshape(shape), right.reshape(shape))
        drives = drives.reshape(size, ROWS, WIDE, LANES)
        carried = state[...]
        for step in range(size):
            now = begin + step
            carried = factors[0, now] * carried + factors[1, now] * drives[step]
        state[...] = carried

    waiting = products(0)
    for chunk in range(CHUNKS):
        ready = waiting
        if chunk + 1 < CHUNKS:
            waiting = products(chunk + 1)
        advance(chunk, *ready)

    late = functools.reduce(lambda a, b: a + b, values[HALF:])
    total = functools.reduce(lambda a, b: a + b, values[:HALF]) + late
    carried = state[...]
    end = carried + jnp.exp(-late * rate).reshape(1, 1, LANES) * swap_halves(carried)
    other = swap_halves(end)
    low = low_half((ROWS // 2, WIDE, LANES))
    packed = jnp.where(low, other[: ROWS // 2], end[ROWS // 2 :]).astype(BF16)
    row = lax.broadcasted_iota(jnp.int32, (WIDE, LANES), 0)
    pieces = split3(jnp.full((WIDE, LANES), total, F32))
    extra = jnp.zeros((WIDE, LANES), F32)
    for index, piece in enumerate(pieces):
        extra = jnp.where(row == index, piece.astype(F32), extra)
    extra = extra.astype(BF16)
    for z in range(ZS):
        message[z, : ROWS // 2] = packed
        message[z, ROWS // 2] = extra


WINDOW_STEP = 8
EARLY = 24
TALL = 12


def assemble(target, own, near, swapped, far, first):
    def tap(index, carry):
        left = jnp.where(first, near[index], swapped[index])
        right = jnp.where(first, swapped[index], near[index])
        target[index] = jnp.concatenate([own[index], left, far[index], right], axis=0)
        return carry

    lax.fori_loop(0, 9, tap, 0)


def window_kernel(
    begin, size, place, own, near, swapped, far, frames, _,
    drives, token,
    weights, rows, written, load_sem, store_sem,
):
    chunks = size // WINDOW_STEP
    chan, first = place[0], place[3] == 0
    source = jnp.clip(CHANS * chan - 2, 0, 8)
    target = source - CHANS * chan + 4

    def load(chunk):
        part = pl.ds(chunk * WINDOW_STEP, WINDOW_STEP)
        where = pl.ds(begin + chunk * WINDOW_STEP, WINDOW_STEP)
        return pltpu.make_async_copy(
            frames.at[where, pl.ds(source, 8)], rows.at[part, pl.ds(target, 8)], load_sem.at[chunk]
        )

    def store(chunk):
        part = pl.ds(chunk * WINDOW_STEP, WINDOW_STEP)
        return pltpu.make_async_copy(written.at[part], drives.at[part], store_sem.at[chunk])

    for chunk in range(chunks):
        load(chunk).start()
    empty = jnp.zeros((size, 2, WIDE, CH), BF16)

    @pl.when(chan == 0)
    def _():
        rows[:, 2:4] = empty

    @pl.when(chan == CHANS - 1)
    def _():
        rows[:, 8:10] = empty

    token[...] = jnp.zeros_like(token)
    assemble(weights, own, near, swapped, far, first)

    def convolve(chunk, carry):
        load(chunk).wait()
        start = pl.multiple_of(chunk * WINDOW_STEP, WINDOW_STEP)
        block = rows[pl.ds(start, WINDOW_STEP)]
        pixels = WINDOW_STEP * WINDOW * WIDE
        taps = [block[:, 2 + i : 2 + i + WINDOW].reshape(pixels, CH) for i in range(3)]
        operand = jnp.concatenate(taps, axis=1)
        shape = (WINDOW_STEP * WINDOW, WIDE, CH)
        dims = (((1,), (1,)), ((), ()))
        parts = []
        for j in range(3):
            weight = jnp.concatenate([weights[3 * i + j] for i in range(3)], axis=1)
            parts.append(
                lax.dot_general(operand, weight, dims, preferred_element_type=F32).reshape(shape)
            )
        total = beside(*parts).reshape(WINDOW_STEP, WINDOW, WIDE, CH)
        for r in range(WINDOW):
            kept = total[:, r]
            if r == 0:
                kept = jnp.where(chan == 0, 0.0, kept)
            if r == WINDOW - 1:
                kept = jnp.where(chan == CHANS - 1, 0.0, kept)
            written[pl.ds(start, WINDOW_STEP), r] = kept.astype(BF16)
        store(chunk).start()
        return carry

    lax.fori_loop(0, chunks, convolve, 0)
    for chunk in range(chunks):
        store(chunk).wait()


def relay_kernel(place, rates, received, token, message, done):
    x, z = place[1], place[2]
    done[...] = jnp.zeros_like(done)
    rate = doubled(rates[...])
    total = jnp.zeros((ROWS // 2, WIDE, LANES), F32)
    before = total
    elapsed = jnp.zeros((1, LANES), F32)
    elapsed_before = elapsed
    for other in range(ZS):
        mine = z == other
        before = jnp.where(mine, total, before)
        elapsed_before = jnp.where(mine, elapsed, elapsed_before)
        spent = join3(received[ZS - 1 - other, ROWS // 2], 0)
        decay = jnp.exp(-spent * rate).reshape(1, 1, LANES)
        total = decay * total + received[ZS - 1 - other, : ROWS // 2].astype(F32)
        elapsed = elapsed + spent

    low = low_half((WIDE, LANES))
    blank = jnp.zeros((WIDE, LANES), F32)

    def rows_of(value):
        swapped = swap_halves(value)
        top = [jnp.where(low, value[r], swapped[r]) for r in range(ROWS // 2)]
        bottom = [jnp.where(low, swapped[r], value[r]) for r in range(ROWS // 2)]
        return [blank] + top + bottom + [blank]

    totals, befores = rows_of(total), rows_of(before)
    row = lax.broadcasted_iota(jnp.int32, (WIDE, LANES), 0)
    extra = blank
    pieces = split3(elapsed) + split3(elapsed_before) + split3(rate)
    for index, piece in enumerate(pieces):
        extra = jnp.where(row == index, piece.astype(F32), extra)
    extra = extra.astype(BF16)
    for chan in range(CHANS):
        for q in range(WINDOW // 2):
            here = CHANS * chan + q
            there = here + WINDOW // 2
            later = jnp.where(low, totals[here], totals[there]).astype(BF16)
            level = jnp.where(low, befores[here], befores[there]).astype(BF16)
            for to in range(XS):
                message[LAST - to * CHANS - chan, q] = jnp.where(x == to, level, later)
        for to in range(XS):
            message[LAST - to * CHANS - chan, WINDOW // 2] = extra


OUT_STEP = 8
OUT_CHUNKS = FRAMES // OUT_STEP


def readout_kernel(
    place, intervals_far, skip_gain, received, early, late,
    own, near, swapped, far, frames,
    result,
    intervals, weights, direct, drives, states, written, factors, state,
    load_sem, drive_sem, store_sem, small_sem,
):
    small = [pltpu.make_async_copy(intervals_far, intervals, small_sem)]
    for copy in small:
        copy.start()
    chan, x, first = place[0], place[1], place[3] == 0

    def load(chunk):
        part = pl.ds(chunk * OUT_STEP, OUT_STEP)
        return pltpu.make_async_copy(
            frames.at[part, pl.ds(CHANS * chan, CHANS)], direct.at[part], load_sem.at[chunk]
        )

    def arrive(chunk, source=early, skipped=0):
        part = pl.ds(chunk * OUT_STEP, OUT_STEP)
        where = pl.ds(chunk * OUT_STEP - skipped, OUT_STEP)
        return pltpu.make_async_copy(source.at[where], drives.at[part], drive_sem.at[chunk])

    def arrived(chunk):
        part = drives.at[pl.ds(chunk * OUT_STEP, OUT_STEP)]
        return pltpu.make_async_copy(part, part, drive_sem.at[chunk])

    def store(chunk):
        part = pl.ds(chunk * OUT_STEP, OUT_STEP)
        return pltpu.make_async_copy(written.at[part], result.at[part], store_sem.at[chunk])

    for chunk in range(OUT_CHUNKS):
        if chunk * OUT_STEP < EARLY:
            arrive(chunk).start()
        else:
            arrive(chunk, late, EARLY).start()
        load(chunk).start()

    assemble(weights, own, near, swapped, far, first)
    low = low_half((WIDE, LANES))
    rates, entering = [], []
    for step in range(CHANS):
        source = lax.rem(chan + CHANS - step, CHANS)
        level = received[LAST - x * CHANS - source]
        rate = join3(level[WINDOW // 2], 6)
        spent = join3(level[WINDOW // 2], 3)
        total = jnp.zeros((WINDOW // 2, WIDE, LANES), F32)
        for other in range(XS - 1):
            earlier = received[LAST - other * CHANS - source]
            decay = jnp.exp(-join3(earlier[WINDOW // 2], 0) * rate).reshape(1, 1, LANES)
            added = decay * total + earlier[: WINDOW // 2].astype(F32)
            total = jnp.where(other < x, added, total)
        decay = jnp.exp(-spent * rate).reshape(1, 1, LANES)
        total = level[: WINDOW // 2].astype(F32) + decay * total
        swapped = swap_halves(total)
        rates.append(rate)
        entering.append(
            [jnp.where(low, total[r], swapped[r]) for r in range(WINDOW // 2)]
            + [jnp.where(low, swapped[r], total[r]) for r in range(WINDOW // 2)]
        )

    for copy in small:
        copy.wait()
    values = [intervals[t] for t in range(FRAMES)]
    low_row = low_half((1, LANES))
    for pair in range(2):
        rate = jnp.where(low_row, rates[2 * pair], rates[2 * pair + 1])
        part = slice(LANES * pair, LANES * (pair + 1))
        for half in range(2):
            some = values[HALF * half : HALF * (half + 1)]
            scaled = table(some, some) * rate
            rest = pl.ds(HALF * half, HALF)
            spread(factors.at[:, rest], 0, part, jnp.exp(-scaled))
            spread(factors.at[:, rest], 1, part, jnp.sqrt(one_minus_exp(2.0 * scaled)))
        for r in range(WINDOW):
            state[r, :, part] = jnp.where(low, entering[2 * pair][r], entering[2 * pair + 1][r])

    def convolve(chunk, carry):
        start = pl.multiple_of(chunk * OUT_STEP, OUT_STEP)
        arrived(chunk).wait()
        carried = state[...]
        for step in range(OUT_STEP):
            decay, gain = factors[0, start + step], factors[1, start + step]
            carried = decay * carried + gain * drives[start + step].astype(F32)
            states[start + step] = carried.astype(BF16)
        state[...] = carried
        size = OUT_STEP * CHANS * WIDE
        block = states[pl.ds(start, OUT_STEP)]
        taps = [block[:, i : i + CHANS].reshape(size, CH) for i in range(3)]
        operand = jnp.concatenate(taps, axis=1)
        shape = (OUT_STEP * CHANS, WIDE, CH)
        parts = []
        for j in range(3):
            weight = jnp.concatenate([weights[3 * i + j] for i in range(3)], axis=0)
            parts.append(jnp.dot(operand, weight, preferred_element_type=F32).reshape(shape))
        load(chunk).wait()
        passed = direct[pl.ds(start, OUT_STEP)].astype(F32).reshape(shape)
        total = beside(*parts) + skip_gain[...].reshape(1, 1, CH) * passed
        written[pl.ds(start, OUT_STEP)] = total.astype(BF16).reshape(OUT_STEP, CHANS, WIDE, CH)
        store(chunk).start()
        return carry

    lax.fori_loop(0, OUT_CHUNKS, convolve, 0)
    for chunk in range(OUT_CHUNKS):
        store(chunk).wait()


def in_vmem():
    return pl.BlockSpec(memory_space=pltpu.VMEM)


def in_smem():
    return pl.BlockSpec(memory_space=pltpu.SMEM)


def anywhere():
    return pl.BlockSpec(memory_space=pl.ANY)


def cost(microseconds):
    return pl.CostEstimate(
        flops=int(microseconds * 1.1e9), bytes_accessed=1 << 20, transcendentals=0
    )


def drive(intervals, rates, kernel_t, frames):
    return pl.pallas_call(
        drive_kernel,
        out_shape=jax.ShapeDtypeStruct((ZS, ROWS // 2 + 1, WIDE, LANES), BF16),
        in_specs=[anywhere()] * 4,
        out_specs=in_vmem(),
        scratch_shapes=[
            pltpu.SMEM((FRAMES,), F32),
            pltpu.VMEM((1, OWN), F32),
            pltpu.VMEM((9, OWN, CH), BF16),
            pltpu.VMEM((FRAMES, ROWS + 2, WIDE, CH), BF16),
            pltpu.VMEM((2, 3 * CH, CH), BF16),
            pltpu.VMEM((2, HALF, WIDE, LANES), F32),
            pltpu.VMEM((ROWS, WIDE, LANES), F32),
            pltpu.SemaphoreType.DMA((CHUNKS, 2)),
            pltpu.SemaphoreType.DMA((3,)),
        ],
        compiler_params=pltpu.CompilerParams(vmem_limit_bytes=60 << 20),
        cost_estimate=cost(8),
        name="drive",
    )(intervals, rates, kernel_t, frames)


def window(begin, size, place, own, near, swapped, far, frames, later):
    chunks = size // WINDOW_STEP
    return pl.pallas_call(
        functools.partial(window_kernel, begin, size),
        out_shape=[
            jax.ShapeDtypeStruct((size, WINDOW, WIDE, CH), BF16),
            jax.ShapeDtypeStruct((8, LANES), F32),
        ],
        in_specs=[in_smem()] + [in_vmem()] * CHANS + [anywhere()] * 2,
        out_specs=[anywhere(), in_vmem()],
        scratch_shapes=[
            pltpu.VMEM((9, CHANS * OWN, CH), BF16),
            pltpu.VMEM((size, TALL, WIDE, CH), BF16),
            pltpu.VMEM((size, WINDOW, WIDE, CH), BF16),
            pltpu.SemaphoreType.DMA((chunks,)),
            pltpu.SemaphoreType.DMA((chunks,)),
        ],
        compiler_params=pltpu.CompilerParams(vmem_limit_bytes=52 << 20),
        cost_estimate=cost(1),
        name="window",
    )(place, own, near, swapped, far, frames, later)


def hold_kernel(value, *refs):
    result, sem = refs[-2:]
    copy = pltpu.make_async_copy(value, result, sem)
    copy.start()
    copy.wait()


def hold(value, others):
    return pl.pallas_call(
        hold_kernel,
        out_shape=jax.ShapeDtypeStruct(value.shape, value.dtype),
        in_specs=[anywhere()] * (1 + len(others)),
        out_specs=anywhere(),
        scratch_shapes=[pltpu.SemaphoreType.DMA],
        compiler_params=pltpu.CompilerParams(vmem_limit_bytes=16 << 20),
        cost_estimate=cost(1),
        name="hold",
    )(value, *others)


def relay(place, rates, received, token):
    return pl.pallas_call(
        relay_kernel,
        out_shape=[
            jax.ShapeDtypeStruct((XS * CHANS, WINDOW // 2 + 1, WIDE, LANES), BF16),
            jax.ShapeDtypeStruct((8, LANES), F32),
        ],
        in_specs=[in_smem(), in_vmem(), in_vmem(), anywhere()],
        out_specs=[in_vmem()] * 2,
        compiler_params=pltpu.CompilerParams(vmem_limit_bytes=16 << 20),
        cost_estimate=cost(1),
        name="relay",
    )(place, rates, received, token)


def read_out(place, intervals, skip_gain, received, early, late, kernels, frames):
    return pl.pallas_call(
        readout_kernel,
        out_shape=jax.ShapeDtypeStruct((FRAMES, CHANS, WIDE, CH), BF16),
        in_specs=[in_smem(), anywhere(), in_vmem(), in_vmem(), anywhere(), anywhere()]
        + [in_vmem()] * CHANS
        + [anywhere()],
        out_specs=anywhere(),
        scratch_shapes=[
            pltpu.SMEM((FRAMES,), F32),
            pltpu.VMEM((9, CHANS * OWN, CH), BF16),
            pltpu.VMEM((FRAMES, CHANS, WIDE, CH), BF16),
            pltpu.VMEM((FRAMES, WINDOW, WIDE, CH), BF16),
            pltpu.VMEM((FRAMES, WINDOW, WIDE, CH), BF16),
            pltpu.VMEM((FRAMES, CHANS, WIDE, CH), BF16),
            pltpu.VMEM((2, FRAMES, WIDE, CH), F32),
            pltpu.VMEM((WINDOW, WIDE, CH), F32),
            pltpu.SemaphoreType.DMA((OUT_CHUNKS,)),
            pltpu.SemaphoreType.DMA((OUT_CHUNKS,)),
            pltpu.SemaphoreType.DMA((OUT_CHUNKS,)),
            pltpu.SemaphoreType.DMA,
        ],
        compiler_params=pltpu.CompilerParams(vmem_limit_bytes=52 << 20),
        cost_estimate=cost(6),
        name="read_out",
    )(place, intervals, skip_gain, received, early, late, *kernels, frames)


def around(value):
    near = [
        (2 * c + core, 2 * ((c + step) % CHANS) + core)
        for c in range(CHANS)
        for core, step in ((0, 1), (1, CHANS - 1))
    ]
    far = [(c, (c + 2) % CHANS) for c in range(CHANS)]
    return lax.ppermute(value, ("chan", "clip"), near), lax.ppermute(value, "chan", far)


def after_kernel(*refs):
    del refs


def after(value, other, length=0):
    return pl.pallas_call(
        after_kernel,
        out_shape=jax.ShapeDtypeStruct(value.shape, value.dtype),
        in_specs=[anywhere()] * 2,
        out_specs=anywhere(),
        input_output_aliases={0: 0},
        compiler_params=pltpu.CompilerParams(vmem_limit_bytes=16 << 20),
        cost_estimate=cost(length),
        name="after",
    )(value, other)


def swap(value):
    return lax.ppermute(value, "clip", [(0, 1), (1, 0)])


def local(frames, intervals, decay_rates, in_kernel, out_kernel, skip_gain):
    axes = ("chan", "x", "z", "clip")
    place = jnp.stack([lax.axis_index(name) for name in axes]).astype(jnp.int32)
    rates = decay_rates.reshape(1, OWN)
    kernel_t = jnp.transpose(in_kernel.reshape(9, CH, OWN), (0, 2, 1))
    out_own = out_kernel.reshape(9, OWN, CH)
    in_near, in_far = around(kernel_t)
    in_far = after(in_far, in_near, 2)
    message = drive(intervals, rates, kernel_t, frames)
    backwards = [list(reversed(range(ZS)))]
    arrived = lax.all_to_all(message, "z", 0, 0, axis_index_groups=backwards)
    out_near, out_far = around(hold(out_own, (in_near, in_far)))
    pieces = (kernel_t, in_near, swap(in_near), in_far)
    early, done = window(0, EARLY, place, *pieces, frames, place)
    onward, done = relay(place, rates, arrived, done)
    late, _ = window(EARLY, FRAMES - EARLY, place, *pieces, frames, done)
    out_near = after(out_near, done)
    backwards = [list(reversed(range(XS * CHANS)))]
    received = lax.all_to_all(onward, ("x", "chan"), 0, 0, axis_index_groups=backwards)
    received = after(received, place, 2)
    out_far = after(out_far, done, 2)
    kernels = (out_own, out_near, swap(out_near), out_far)
    skip = skip_gain.reshape(1, CH)
    return read_out(place, intervals, skip, received, early, late, kernels, frames)


def solution(mesh):
    whole = jax.sharding.Mesh(
        mesh.devices.reshape(XS, ZS, CHANS, 2), ("x", "z", "chan", "clip")
    )
    time = ("clip", "x", "z")
    placed = (
        P(time, None, None, None),
        P(time),
        P("chan"),
        P(None, None, None, "chan"),
        P(None, None, "chan", None),
        P(),
    )
    return jax.shard_map(
        local,
        mesh=whole,
        in_specs=placed,
        out_specs=P(time, "chan", None, None),
        check_vma=False,
    )
```

```python
import functools

import jax
import jax.numpy as jnp
from jax import lax
from jax.experimental import pallas as pl
from jax.experimental.pallas import tpu as pltpu
from jax.sharding import PartitionSpec as P

F32 = jnp.float32
BF16 = jnp.bfloat16
FRAMES = 32
HALF = 16
ROWS = 16
WIDE = 16
CH = 256
OWN = 64
LANES = 128
CHANS = 4
ZS = 8
XS = 4
WINDOW = 6
LAST = XS * CHANS - 1
TURN = (6, 7, 0, 1, 5, 4, 3, 2)
STEP = 4
PIECES = ((0, 4), (4, 4), (8, 4), (12, 4))
CHUNKS = len(PIECES)


def split3(value):
    high = value.astype(BF16)
    rest = value - high.astype(F32)
    middle = rest.astype(BF16)
    low = (rest - middle.astype(F32)).astype(BF16)
    return high, middle, low


def join3(block, start):
    parts = block.astype(F32)
    return parts[start : start + 1] + parts[start + 1 : start + 2] + parts[start + 2 : start + 3]


def low_half(shape):
    return lax.broadcasted_iota(jnp.int32, shape, len(shape) - 1) < OWN


def swap_halves(value):
    return pltpu.roll(value, OWN, value.ndim - 1)


def doubled(rates):
    row = jnp.concatenate([rates, rates], axis=1)
    return row


def table(low_values, high_values):
    row = lax.broadcasted_iota(jnp.int32, (HALF, LANES), 0)
    low = low_half((HALF, LANES))
    result = jnp.zeros((HALF, LANES), F32)
    for t in range(HALF):
        result = jnp.where(row == t, jnp.where(low, low_values[t], high_values[t]), result)
    return result


def spread(target, index, lanes, rows):
    for t in range(HALF):
        target[index, t, :, lanes] = jnp.broadcast_to(rows[t : t + 1], (WIDE, LANES))


def one_minus_exp(value):
    series = value * (
        1.0 - value * (0.5 - value * (1.0 / 6 - value * (1.0 / 24 - value * (1.0 / 120))))
    )
    return jnp.where(value < 0.125, series, 1.0 - jnp.exp(-value))


def beside(left, centre, right):
    column = lax.broadcasted_iota(jnp.int32, centre.shape, 1)
    total = centre + jnp.where(column == 0, 0.0, pltpu.roll(left, 1, 1))
    return total + jnp.where(column == WIDE - 1, 0.0, pltpu.roll(right, WIDE - 1, 1))


def running(values):
    sums = [values[0]]
    for value in values[1:]:
        sums.append(sums[-1] + value)
    return sums


def drive_kernel(
    intervals_far, rates_far, kernel_far, frames,
    message,
    intervals, rates, kernel_t, padded, weights, factors, state, load_sem, small_sem,
):
    small = [
        pltpu.make_async_copy(source, target, small_sem.at[index])
        for index, (source, target) in enumerate(
            ((kernel_far, kernel_t), (intervals_far, intervals), (rates_far, rates))
        )
    ]
    for copy in small:
        copy.start()

    def load(chunk, half):
        first, size = PIECES[chunk]
        part = pl.ds(half * HALF + first, size)
        return pltpu.make_async_copy(
            frames.at[part],
            padded.at[part, pl.ds(1, ROWS)],
            load_sem.at[chunk, half],
        )

    load(0, 0).start()
    load(0, 1).start()

    empty = jnp.zeros((FRAMES, 1, WIDE, CH), BF16)
    padded[:, 0:1] = empty
    padded[:, ROWS + 1 : ROWS + 2] = empty
    nothing = jnp.zeros((CH, OWN), BF16)
    for copy in small:
        copy.wait()
    for chunk in range(1, CHUNKS):
        load(chunk, 0).start()
        load(chunk, 1).start()
    for i in range(3):
        tap = [kernel_t[3 * i + j].astype(F32).T.astype(BF16) for j in range(3)]
        weights[0, CH * i : CH * (i + 1), :] = jnp.concatenate([tap[0], tap[1], tap[2], nothing], 1)
        weights[1, CH * i : CH * (i + 1), :] = jnp.concatenate([tap[1], tap[0], nothing, tap[2]], 1)

    values = [intervals[t] for t in range(FRAMES)]
    rate = doubled(rates[...])
    scaled = table(values[:HALF], values[HALF:]) * rate
    spread(factors, 0, slice(None), jnp.exp(-scaled))
    spread(factors, 1, slice(None), jnp.sqrt(one_minus_exp(2.0 * scaled)))
    state[...] = jnp.zeros_like(state)

    def products(chunk):
        load(chunk, 0).wait()
        load(chunk, 1).wait()
        begin, size = PIECES[chunk]
        both = []
        for half in range(2):
            block = padded[pl.ds(half * HALF + begin, size)]
            taps = [block[:, i : i + ROWS].reshape(size * ROWS * WIDE, CH) for i in range(3)]
            both.append(
                jnp.dot(jnp.concatenate(taps, axis=1), weights[half], preferred_element_type=F32)
            )
        return both

    def advance(chunk, first, second):
        begin, size = PIECES[chunk]
        low = low_half((size * ROWS * WIDE, LANES))
        left = jnp.where(low, first[:, :LANES], second[:, :LANES])
        centre = swap_halves(jnp.where(low, second[:, :LANES], first[:, :LANES]))
        right = first[:, LANES:] + second[:, LANES:]
        shape = (size * ROWS, WIDE, LANES)
        drives = beside(left.reshape(shape), centre.reshape(shape), right.reshape(shape))
        drives = drives.reshape(size, ROWS, WIDE, LANES)
        carried = state[...]
        for step in range(size):
            now = begin + step
            carried = factors[0, now] * carried + factors[1, now] * drives[step]
        state[...] = carried

    waiting = products(0)
    for chunk in range(CHUNKS):
        ready = waiting
        if chunk + 1 < CHUNKS:
            waiting = products(chunk + 1)
        advance(chunk, *ready)

    late = functools.reduce(lambda a, b: a + b, values[HALF:])
    total = functools.reduce(lambda a, b: a + b, values[:HALF]) + late
    carried = state[...]
    end = carried + jnp.exp(-late * rate).reshape(1, 1, LANES) * swap_halves(carried)
    other = swap_halves(end)
    low = low_half((ROWS // 2, WIDE, LANES))
    packed = jnp.where(low, other[: ROWS // 2], end[ROWS // 2 :]).astype(BF16)
    row = lax.broadcasted_iota(jnp.int32, (WIDE, LANES), 0)
    pieces = split3(jnp.full((WIDE, LANES), total, F32))
    extra = jnp.zeros((WIDE, LANES), F32)
    for index, piece in enumerate(pieces):
        extra = jnp.where(row == index, piece.astype(F32), extra)
    extra = extra.astype(BF16)
    for z in range(ZS):
        message[z, : ROWS // 2] = packed
        message[z, ROWS // 2] = extra


WINDOW_STEP = 8
WINDOW_CHUNKS = FRAMES // WINDOW_STEP
TALL = 12


def assemble(target, own, near, swapped, far, first):
    def tap(index, carry):
        left = jnp.where(first, near[index], swapped[index])
        right = jnp.where(first, swapped[index], near[index])
        target[index] = jnp.concatenate([own[index], left, far[index], right], axis=0)
        return carry

    lax.fori_loop(0, 9, tap, 0)


def window_kernel(
    place, own, near, swapped, far, frames, later,
    drives, token,
    weights, rows, written, load_sem, store_sem,
):
    chan, first = place[0], place[3] == 0
    source = jnp.clip(CHANS * chan - 2, 0, 8)
    target = source - CHANS * chan + 4

    def load(chunk):
        part = pl.ds(chunk * WINDOW_STEP, WINDOW_STEP)
        return pltpu.make_async_copy(
            frames.at[part, pl.ds(source, 8)], rows.at[part, pl.ds(target, 8)], load_sem.at[chunk]
        )

    def store(chunk):
        part = pl.ds(chunk * WINDOW_STEP, WINDOW_STEP)
        return pltpu.make_async_copy(written.at[part], drives.at[part], store_sem.at[chunk])

    for chunk in range(WINDOW_CHUNKS):
        load(chunk).start()
    empty = jnp.zeros((FRAMES, 2, WIDE, CH), BF16)

    @pl.when(chan == 0)
    def _():
        rows[:, 2:4] = empty

    @pl.when(chan == CHANS - 1)
    def _():
        rows[:, 8:10] = empty

    token[...] = jnp.zeros_like(token)
    assemble(weights, own, near, swapped, far, first)

    def convolve(chunk, carry):
        load(chunk).wait()
        start = pl.multiple_of(chunk * WINDOW_STEP, WINDOW_STEP)
        block = rows[pl.ds(start, WINDOW_STEP)]
        size = WINDOW_STEP * WINDOW * WIDE
        taps = [block[:, 2 + i : 2 + i + WINDOW].reshape(size, CH) for i in range(3)]
        operand = jnp.concatenate(taps, axis=1)
        shape = (WINDOW_STEP * WINDOW, WIDE, CH)
        dims = (((1,), (1,)), ((), ()))
        parts = []
        for j in range(3):
            weight = jnp.concatenate([weights[3 * i + j] for i in range(3)], axis=1)
            parts.append(
                lax.dot_general(operand, weight, dims, preferred_element_type=F32).reshape(shape)
            )
        total = beside(*parts).reshape(WINDOW_STEP, WINDOW, WIDE, CH)
        for r in range(WINDOW):
            kept = total[:, r]
            if r == 0:
                kept = jnp.where(chan == 0, 0.0, kept)
            if r == WINDOW - 1:
                kept = jnp.where(chan == CHANS - 1, 0.0, kept)
            written[pl.ds(start, WINDOW_STEP), r] = kept.astype(BF16)
        store(chunk).start()
        return carry

    lax.fori_loop(0, WINDOW_CHUNKS, convolve, 0)
    for chunk in range(WINDOW_CHUNKS):
        store(chunk).wait()


def relay_kernel(place, rates, received, token, later, message):
    x, z = place[1], place[2]
    rate = doubled(rates[...])
    total = jnp.zeros((ROWS // 2, WIDE, LANES), F32)
    before = total
    elapsed = jnp.zeros((1, LANES), F32)
    elapsed_before = elapsed
    for other in range(ZS):
        mine = z == other
        before = jnp.where(mine, total, before)
        elapsed_before = jnp.where(mine, elapsed, elapsed_before)
        spent = join3(received[TURN.index(other), ROWS // 2], 0)
        decay = jnp.exp(-spent * rate).reshape(1, 1, LANES)
        total = decay * total + received[TURN.index(other), : ROWS // 2].astype(F32)
        elapsed = elapsed + spent

    low = low_half((WIDE, LANES))
    blank = jnp.zeros((WIDE, LANES), F32)

    def rows_of(value):
        swapped = swap_halves(value)
        top = [jnp.where(low, value[r], swapped[r]) for r in range(ROWS // 2)]
        bottom = [jnp.where(low, swapped[r], value[r]) for r in range(ROWS // 2)]
        return [blank] + top + bottom + [blank]

    totals, befores = rows_of(total), rows_of(before)
    row = lax.broadcasted_iota(jnp.int32, (WIDE, LANES), 0)
    extra = blank
    pieces = split3(elapsed) + split3(elapsed_before) + split3(rate)
    for index, piece in enumerate(pieces):
        extra = jnp.where(row == index, piece.astype(F32), extra)
    extra = extra.astype(BF16)
    for chan in range(CHANS):
        for q in range(WINDOW // 2):
            here = CHANS * chan + q
            there = here + WINDOW // 2
            later = jnp.where(low, totals[here], totals[there]).astype(BF16)
            level = jnp.where(low, befores[here], befores[there]).astype(BF16)
            for to in range(XS):
                message[LAST - to * CHANS - chan, q] = jnp.where(x == to, level, later)
        for to in range(XS):
            message[LAST - to * CHANS - chan, WINDOW // 2] = extra


OUT_STEP = 8
OUT_CHUNKS = FRAMES // OUT_STEP


def readout_kernel(
    place, intervals_far, skip_gain, received, drives_far,
    own, near, swapped, far, frames,
    result,
    intervals, weights, direct, drives, states, written, factors, state,
    load_sem, drive_sem, store_sem, small_sem,
):
    small = [pltpu.make_async_copy(intervals_far, intervals, small_sem)]
    for copy in small:
        copy.start()
    chan, x, first = place[0], place[1], place[3] == 0

    def load(chunk):
        part = pl.ds(chunk * OUT_STEP, OUT_STEP)
        return pltpu.make_async_copy(
            frames.at[part, pl.ds(CHANS * chan, CHANS)], direct.at[part], load_sem.at[chunk]
        )

    def arrive(chunk):
        part = pl.ds(chunk * OUT_STEP, OUT_STEP)
        return pltpu.make_async_copy(drives_far.at[part], drives.at[part], drive_sem.at[chunk])

    def store(chunk):
        part = pl.ds(chunk * OUT_STEP, OUT_STEP)
        return pltpu.make_async_copy(written.at[part], result.at[part], store_sem.at[chunk])

    for chunk in range(OUT_CHUNKS):
        arrive(chunk).start()
        load(chunk).start()

    assemble(weights, own, near, swapped, far, first)
    low = low_half((WIDE, LANES))
    rates, entering = [], []
    for step in range(CHANS):
        source = lax.rem(chan + CHANS - step, CHANS)
        level = received[LAST - x * CHANS - source]
        rate = join3(level[WINDOW // 2], 6)
        spent = join3(level[WINDOW // 2], 3)
        total = jnp.zeros((WINDOW // 2, WIDE, LANES), F32)
        for other in range(XS - 1):
            earlier = received[LAST - other * CHANS - source]
            decay = jnp.exp(-join3(earlier[WINDOW // 2], 0) * rate).reshape(1, 1, LANES)
            added = decay * total + earlier[: WINDOW // 2].astype(F32)
            total = jnp.where(other < x, added, total)
        decay = jnp.exp(-spent * rate).reshape(1, 1, LANES)
        total = level[: WINDOW // 2].astype(F32) + decay * total
        swapped = swap_halves(total)
        rates.append(rate)
        entering.append(
            [jnp.where(low, total[r], swapped[r]) for r in range(WINDOW // 2)]
            + [jnp.where(low, swapped[r], total[r]) for r in range(WINDOW // 2)]
        )

    for copy in small:
        copy.wait()
    values = [intervals[t] for t in range(FRAMES)]
    low_row = low_half((1, LANES))
    for pair in range(2):
        rate = jnp.where(low_row, rates[2 * pair], rates[2 * pair + 1])
        part = slice(LANES * pair, LANES * (pair + 1))
        for half in range(2):
            some = values[HALF * half : HALF * (half + 1)]
            scaled = table(some, some) * rate
            rest = pl.ds(HALF * half, HALF)
            spread(factors.at[:, rest], 0, part, jnp.exp(-scaled))
            spread(factors.at[:, rest], 1, part, jnp.sqrt(one_minus_exp(2.0 * scaled)))
        for r in range(WINDOW):
            state[r, :, part] = jnp.where(low, entering[2 * pair][r], entering[2 * pair + 1][r])

    def convolve(chunk, carry):
        start = pl.multiple_of(chunk * OUT_STEP, OUT_STEP)
        arrive(chunk).wait()
        carried = state[...]
        for step in range(OUT_STEP):
            decay, gain = factors[0, start + step], factors[1, start + step]
            carried = decay * carried + gain * drives[start + step].astype(F32)
            states[start + step] = carried.astype(BF16)
        state[...] = carried
        size = OUT_STEP * CHANS * WIDE
        block = states[pl.ds(start, OUT_STEP)]
        taps = [block[:, i : i + CHANS].reshape(size, CH) for i in range(3)]
        operand = jnp.concatenate(taps, axis=1)
        shape = (OUT_STEP * CHANS, WIDE, CH)
        parts = []
        for j in range(3):
            weight = jnp.concatenate([weights[3 * i + j] for i in range(3)], axis=0)
            parts.append(jnp.dot(operand, weight, preferred_element_type=F32).reshape(shape))
        load(chunk).wait()
        passed = direct[pl.ds(start, OUT_STEP)].astype(F32).reshape(shape)
        total = beside(*parts) + skip_gain[...].reshape(1, 1, CH) * passed
        written[pl.ds(start, OUT_STEP)] = total.astype(BF16).reshape(OUT_STEP, CHANS, WIDE, CH)
        store(chunk).start()
        return carry

    lax.fori_loop(0, OUT_CHUNKS, convolve, 0)
    for chunk in range(OUT_CHUNKS):
        store(chunk).wait()


def in_vmem():
    return pl.BlockSpec(memory_space=pltpu.VMEM)


def in_smem():
    return pl.BlockSpec(memory_space=pltpu.SMEM)


def anywhere():
    return pl.BlockSpec(memory_space=pl.ANY)


def cost(microseconds):
    return pl.CostEstimate(
        flops=int(microseconds * 1.1e9), bytes_accessed=1 << 20, transcendentals=0
    )


def drive(intervals, rates, kernel_t, frames):
    return pl.pallas_call(
        drive_kernel,
        out_shape=jax.ShapeDtypeStruct((ZS, ROWS // 2 + 1, WIDE, LANES), BF16),
        in_specs=[anywhere()] * 4,
        out_specs=in_vmem(),
        scratch_shapes=[
            pltpu.SMEM((FRAMES,), F32),
            pltpu.VMEM((1, OWN), F32),
            pltpu.VMEM((9, OWN, CH), BF16),
            pltpu.VMEM((FRAMES, ROWS + 2, WIDE, CH), BF16),
            pltpu.VMEM((2, 3 * CH, CH), BF16),
            pltpu.VMEM((2, HALF, WIDE, LANES), F32),
            pltpu.VMEM((ROWS, WIDE, LANES), F32),
            pltpu.SemaphoreType.DMA((CHUNKS, 2)),
            pltpu.SemaphoreType.DMA((3,)),
        ],
        compiler_params=pltpu.CompilerParams(vmem_limit_bytes=60 << 20),
        cost_estimate=cost(8),
        name="drive",
    )(intervals, rates, kernel_t, frames)


def window(place, own, near, swapped, far, frames, later):
    return pl.pallas_call(
        window_kernel,
        out_shape=[
            jax.ShapeDtypeStruct((FRAMES, WINDOW, WIDE, CH), BF16),
            jax.ShapeDtypeStruct((8, LANES), F32),
        ],
        in_specs=[in_smem()] + [in_vmem()] * CHANS + [anywhere()] * 2,
        out_specs=[anywhere(), in_vmem()],
        scratch_shapes=[
            pltpu.VMEM((9, CHANS * OWN, CH), BF16),
            pltpu.VMEM((FRAMES, TALL, WIDE, CH), BF16),
            pltpu.VMEM((FRAMES, WINDOW, WIDE, CH), BF16),
            pltpu.SemaphoreType.DMA((WINDOW_CHUNKS,)),
            pltpu.SemaphoreType.DMA((WINDOW_CHUNKS,)),
        ],
        compiler_params=pltpu.CompilerParams(vmem_limit_bytes=52 << 20),
        cost_estimate=cost(1),
        name="window",
    )(place, own, near, swapped, far, frames, later)


def relay(place, rates, received, token, later):
    return pl.pallas_call(
        relay_kernel,
        out_shape=jax.ShapeDtypeStruct((XS * CHANS, WINDOW // 2 + 1, WIDE, LANES), BF16),
        in_specs=[in_smem(), in_vmem(), in_vmem(), anywhere(), anywhere()],
        out_specs=in_vmem(),
        compiler_params=pltpu.CompilerParams(vmem_limit_bytes=16 << 20),
        cost_estimate=cost(1),
        name="relay",
    )(place, rates, received, token, later)


def read_out(place, intervals, skip_gain, received, drives, kernels, frames):
    return pl.pallas_call(
        readout_kernel,
        out_shape=jax.ShapeDtypeStruct((FRAMES, CHANS, WIDE, CH), BF16),
        in_specs=[in_smem(), anywhere(), in_vmem(), in_vmem(), anywhere()]
        + [in_vmem()] * CHANS
        + [anywhere()],
        out_specs=anywhere(),
        scratch_shapes=[
            pltpu.SMEM((FRAMES,), F32),
            pltpu.VMEM((9, CHANS * OWN, CH), BF16),
            pltpu.VMEM((FRAMES, CHANS, WIDE, CH), BF16),
            pltpu.VMEM((FRAMES, WINDOW, WIDE, CH), BF16),
            pltpu.VMEM((FRAMES, WINDOW, WIDE, CH), BF16),
            pltpu.VMEM((FRAMES, CHANS, WIDE, CH), BF16),
            pltpu.VMEM((2, FRAMES, WIDE, CH), F32),
            pltpu.VMEM((WINDOW, WIDE, CH), F32),
            pltpu.SemaphoreType.DMA((OUT_CHUNKS,)),
            pltpu.SemaphoreType.DMA((OUT_CHUNKS,)),
            pltpu.SemaphoreType.DMA((OUT_CHUNKS,)),
            pltpu.SemaphoreType.DMA,
        ],
        compiler_params=pltpu.CompilerParams(vmem_limit_bytes=52 << 20),
        cost_estimate=cost(6),
        name="read_out",
    )(place, intervals, skip_gain, received, drives, *kernels, frames)


def neighbour(value):
    route = [
        (2 * c + core, 2 * ((c + step) % CHANS) + core)
        for c in range(CHANS)
        for core, step in ((0, 1), (1, CHANS - 1))
    ]
    return lax.ppermute(value, ("chan", "clip"), route)


def opposite(value):
    return lax.ppermute(value, "chan", [(c, (c + 2) % CHANS) for c in range(CHANS)])


def after_kernel(*refs):
    del refs


def after(value, other, length=0):
    return pl.pallas_call(
        after_kernel,
        out_shape=jax.ShapeDtypeStruct(value.shape, value.dtype),
        in_specs=[anywhere()] * 2,
        out_specs=anywhere(),
        input_output_aliases={0: 0},
        compiler_params=pltpu.CompilerParams(vmem_limit_bytes=16 << 20),
        cost_estimate=cost(length),
        name="after",
    )(value, other)


def swap(value):
    return lax.ppermute(value, "clip", [(0, 1), (1, 0)])


def local(frames, intervals, decay_rates, in_kernel, out_kernel, skip_gain):
    axes = ("chan", "x", "z", "clip")
    place = jnp.stack([lax.axis_index(name) for name in axes]).astype(jnp.int32)
    rates = decay_rates.reshape(1, OWN)
    kernel_t = jnp.transpose(in_kernel.reshape(9, CH, OWN), (0, 2, 1))
    out_own = out_kernel.reshape(9, OWN, CH)
    near, out_near = neighbour(kernel_t), neighbour(out_own)
    far = opposite(kernel_t)
    message = drive(intervals, rates, kernel_t, frames)
    backwards = [list(TURN)]
    arrived = lax.all_to_all(message, "z", 0, 0, axis_index_groups=backwards)
    pieces = (kernel_t, near, swap(near), after(far, near, 2))
    out_pieces = (out_own, out_near, swap(out_near), neighbour(out_near))
    drives, done = window(place, *pieces, frames, out_pieces[2])
    onward = relay(place, rates, arrived, done, out_pieces[3])
    backwards = [list(reversed(range(XS * CHANS)))]
    received = lax.all_to_all(onward, ("x", "chan"), 0, 0, axis_index_groups=backwards)
    skip = skip_gain.reshape(1, CH)
    return read_out(place, intervals, skip, received, drives, out_pieces, frames)


def solution(mesh):
    whole = jax.sharding.Mesh(
        mesh.devices.reshape(XS, ZS, CHANS, 2), ("x", "z", "chan", "clip")
    )
    time = ("clip", "x", "z")
    placed = (
        P(time, None, None, None),
        P(time),
        P("chan"),
        P(None, None, None, "chan"),
        P(None, None, "chan", None),
        P(),
    )
    return jax.shard_map(
        local,
        mesh=whole,
        in_specs=placed,
        out_specs=P(time, "chan", None, None),
        check_vma=False,
    )
```
